32 devices in a mesh: dp: 8 (over y, x, core), fsdp: 4 (over z).
Axes of the slice: x: 2, y: 2, z: 4, core: 2. Of those that a mesh axis runs over, the one named last changes fastest.
Arguments:
- tokens: bfloat16 [32768, 768], P(('dp', 'fsdp'))
- cotangent: bfloat16 [32768, 768], P(('dp', 'fsdp')), may hold values from -6 to 6
- doc_lengths: int32 [32, 8], P(('dp', 'fsdp')), may hold values from 1 to 512, 1024 in all within a row
- block_slot: int32 [48], replicated, may hold values from 0 to 47, as said below
- matrices: float32 [48, 384, 384], P('dp', 'fsdp')
- vectors: float32 [9216], replicated
- vector_second: float32 [9216], replicated
- left_stat: float32 [48, 384, 384], P('dp', 'fsdp')
- right_stat: float32 [48, 384, 384], P('dp', 'fsdp')
- left_root: float32 [48, 384, 384], P('dp', 'fsdp')
- right_root: float32 [48, 384, 384], P('dp', 'fsdp')
Outputs:
- output: bfloat16 [32768, 768], P(('dp', 'fsdp'))
- x_grad: float32 [32768, 768], P(('dp', 'fsdp'))
- matrix_grad: float32 [48, 384, 384], P('dp', 'fsdp')
- left_new: float32 [48, 384, 384], P('dp', 'fsdp')
- right_new: float32 [48, 384, 384], P('dp', 'fsdp')
- matrix_new: float32 [48, 384, 384], P('dp', 'fsdp')
- vector_grad: float32 [9216], replicated
- second_new: float32 [9216], replicated
- vector_new: float32 [9216], replicated
- residual_scale: float32 [4], replicated
The draws below stay inside these ranges and needn't reach their ends.
Inputs may be any that keep to these rules, and one draw needn't show every extreme that they name: block_slot is a permutation: block u of the layer's matrices, in the order of the steps, is stored in slot block_slot[u]. `doc_lengths`: each row's 8 document lengths sum to 1024.
All inputs are finite; a program needn't handle non-finite values.
Results may differ from the reference program's by a relative error of at most 0.0089.
Values may be sent and summed in bfloat16 or wider, within the bound.
No kernel may reach another device: no remote copies, remote signals or barrier semaphores. Data moves between devices by JAX's collectives and lax.ppermute only.
A program may use at most 320 MiB of HBM per device.

```python
import math
import jax
import jax.numpy as jnp
import numpy as np
from jax import lax

D = 768
HEADS = 12
HEAD_DIM = 64
FF = 3072
BLK = 384
SEQ = 1024
DOCS = 8
TOK_DEV = 1024
ROWS = 32
TOKENS = 32768
NBLK = 48
NVEC = 9216
DP_WAYS = 8
FSDP_WAYS = 4


MATRIX_GRADS = (1.0, 0.35, 0.3, 0.65)


VECTOR_GRADS = (1.9, 1.9, 1.0, 1.0, 1.1, 0.6, 0.6, 1.0, 0.3)


def slot_order(key):
    return jax.random.permutation(key, NBLK).astype(jnp.int32)


def slot_kind(key):
    use_index = jnp.argsort(slot_order(key)).astype(jnp.int32)
    qkv_count = D // BLK * (3 * D // BLK)
    out_count = D // BLK * (D // BLK)
    fc_count = D // BLK * (FF // BLK)
    kind = (use_index >= qkv_count).astype(jnp.int32)
    kind = kind + (use_index >= qkv_count + out_count).astype(jnp.int32)
    return kind + (use_index >= qkv_count + out_count + fc_count).astype(jnp.int32)


def lookup(kind, table):
    return jnp.array(table, jnp.float32)[kind]


def grad_level(kind):
    level = lookup(kind, MATRIX_GRADS) * TOKENS ** 0.5
    return BLK * level * level


def symmetric(factor, noise, diag_level, off_level):
    mixed = (noise + jnp.swapaxes(noise, 1, 2)) * 0.7071
    identity = jnp.eye(BLK, dtype=jnp.float32)
    diagonal = (factor * diag_level[:, None])[:, :, None] * identity[None]
    return diagonal + mixed * (1.0 - identity)[None] * off_level[:, None, None]


def vector_piece():
    return jnp.minimum(jnp.arange(NVEC, dtype=jnp.int32) // D, 8)


def draw_block_slot(key, part):
    return slot_order(key)


def draw_tokens(key, part):
    key = jax.random.fold_in(key, 1)
    device = jnp.arange(TOKENS, dtype=jnp.int32) // TOK_DEV
    along_dp = (device // FSDP_WAYS).astype(jnp.float32) / max(DP_WAYS - 1, 1)
    along_fsdp = (device % FSDP_WAYS).astype(jnp.float32) / max(FSDP_WAYS - 1, 1)
    base = 3.0
    noise = jnp.clip(jax.random.normal(key, (TOKENS, D), jnp.float32), -4.0, 4.0)
    scale = jnp.exp(math.log(base) * 0.5 * (along_dp + along_fsdp))
    return (noise * scale[:, None]).astype(jnp.bfloat16)


def draw_matrices(key, part):
    kind = slot_kind(key)
    key = jax.random.fold_in(key, 2)
    spread = lookup(kind, (D ** (-0.5), 0.125, D ** (-0.5), FF ** (-0.5)))
    noise = jnp.clip(jax.random.normal(key, (NBLK, BLK, BLK), jnp.float32), -4.0, 4.0)
    return noise * spread[:, None, None]


def draw_left_stat(key, part):
    kind = slot_kind(key)
    key = jax.random.fold_in(key, 3)
    first, second = jax.random.split(key)
    factor = jnp.exp(jax.random.uniform(first, (NBLK, BLK), jnp.float32, 0.0, math.log(4.0)))
    noise = jax.random.normal(second, (NBLK, BLK, BLK), jnp.float32)
    level = grad_level(kind)
    return symmetric(factor, noise, level, 0.1 * level * BLK ** (-0.5))


def draw_right_stat(key, part):
    kind = slot_kind(key)
    key = jax.random.fold_in(key, 4)
    first, second = jax.random.split(key)
    factor = jnp.exp(jax.random.uniform(first, (NBLK, BLK), jnp.float32, 0.0, math.log(4.0)))
    noise = jax.random.normal(second, (NBLK, BLK, BLK), jnp.float32)
    level = grad_level(kind)
    return symmetric(factor, noise, level, 0.1 * level * BLK ** (-0.5))


def draw_left_root(key, part):
    kind = slot_kind(key)
    key = jax.random.fold_in(key, 5)
    first, second = jax.random.split(key)
    factor = jnp.exp(jax.random.uniform(first, (NBLK, BLK), jnp.float32, math.log(0.5), math.log(2.0)))
    noise = jax.random.normal(second, (NBLK, BLK, BLK), jnp.float32)
    level = grad_level(kind) ** (-0.25)
    return symmetric(factor, noise, level, 0.3 * level * BLK ** (-0.5))


def draw_right_root(key, part):
    kind = slot_kind(key)
    key = jax.random.fold_in(key, 6)
    first, second = jax.random.split(key)
    factor = jnp.exp(jax.random.uniform(first, (NBLK, BLK), jnp.float32, math.log(0.5), math.log(2.0)))
    noise = jax.random.normal(second, (NBLK, BLK, BLK), jnp.float32)
    level = grad_level(kind) ** (-0.25)
    return symmetric(factor, noise, level, 0.3 * level * BLK ** (-0.5))


def draw_vectors(key, part):
    key = jax.random.fold_in(key, 7)
    piece = vector_piece()
    noise = jnp.clip(jax.random.normal(key, (NVEC,), jnp.float32), -4.0, 4.0)
    gains = (piece == 0) | (piece == 5)
    return jnp.where(gains, 1.0 + 0.1 * noise, 0.2 * noise)


def draw_vector_second(key, part):
    key = jax.random.fold_in(key, 8)
    factor = jnp.exp(jax.random.uniform(key, (NVEC,), jnp.float32, 0.0, math.log(4.0)))
    level = lookup(vector_piece(), VECTOR_GRADS) * TOKENS ** 0.5
    return factor * level * level


def levels(rng, extent, cuts, low, high):
    factor_of = 1.0
    for position, blocks in cuts:
        steps = jax.random.uniform(jax.random.fold_in(jax.random.fold_in(rng, 6), position), (blocks,), jnp.float32, low / len(cuts), high / len(cuts))
        factor_of = factor_of * jnp.repeat(jnp.exp(steps), extent[position] // blocks).reshape((-1,) + (1,) * (len(extent) - 1 - position))
    return factor_of


def split_up(number_of, total, bound, slope):
    loads = [(1 << 20) // math.isqrt(standing ** slope) + 1 for standing in range(2, number_of + 1)]
    rest, given = total - bound - (number_of - 1), [1] * (number_of - 1)
    while rest > 0:
        free = [i for i in range(number_of - 1) if given[i] < bound]
        pool, remaining = sum([loads[i] for i in free]), rest
        for i in free:
            more = min(bound - given[i], max(1, remaining * loads[i] // pool), rest)
            given[i] = given[i] + more
            rest = rest - more
    return np.array([bound] + given)


def uneven_parts(stream_key, number_of, total, limit, skew):
    if number_of == 2:
        one = jax.random.randint(stream_key, (), max(1, total - limit), min(limit, total - 1) + 1)
        return jnp.stack([one, total - one])
    sizes = jnp.asarray(split_up(number_of, total, limit, skew), jnp.int32)
    pairs = (number_of - 1) // 2
    giver, taker = sizes[1:1 + 2 * pairs:2], sizes[2:2 + 2 * pairs:2]
    slack = jnp.minimum(giver - 1, limit - taker)
    shifted = jax.random.randint(jax.random.fold_in(stream_key, 1), (pairs,), 0, 1 << 20) % (slack + 1)
    sizes = sizes.at[1:1 + 2 * pairs:2].set(giver - shifted).at[2:2 + 2 * pairs:2].set(taker + shifted)
    return sizes[jax.random.permutation(jax.random.fold_in(stream_key, 2), number_of)]


def scatter_about(key, shape, scale, limit, cuts=(), held_as=jnp.bfloat16):
    values = scale * jax.random.normal(key, shape, jnp.float32)
    if cuts:
        values = values * levels(key, shape, cuts, -0.22, 0.18)
    return jnp.clip(values, -limit, limit).astype(held_as)


def setup_inputs(seed: int = 0) -> dict:
    keys = jax.random.split(jax.random.key(seed), 12)
    tokens = draw_tokens(jax.random.fold_in(keys[11], 71), 0)
    cotangent = scatter_about(keys[1], (TOKENS, D), 1.0, 6.0, ((0, 32),))
    doc_lengths = jax.vmap(lambda own: uneven_parts(own, DOCS, SEQ, SEQ // 2, 2))(jax.random.split(keys[2], ROWS)).reshape((ROWS, DOCS)).astype(jnp.int32)
    block_slot = draw_block_slot(jax.random.fold_in(keys[11], 71), 0)
    matrices = draw_matrices(jax.random.fold_in(keys[11], 71), 0)
    vectors = draw_vectors(jax.random.fold_in(keys[11], 71), 0)
    vector_second = draw_vector_second(jax.random.fold_in(keys[11], 71), 0)
    left_stat = draw_left_stat(jax.random.fold_in(keys[11], 71), 0)
    right_stat = draw_right_stat(jax.random.fold_in(keys[11], 71), 0)
    left_root = draw_left_root(jax.random.fold_in(keys[11], 71), 0)
    right_root = draw_right_root(jax.random.fold_in(keys[11], 71), 0)
    return dict(tokens=tokens, cotangent=cotangent, doc_lengths=doc_lengths, block_slot=block_slot, matrices=matrices, vectors=vectors, vector_second=vector_second, left_stat=left_stat, right_stat=right_stat, left_root=left_root, right_root=right_root)


NORM_EPSILON = 1e-05
ROOT_EPSILON = 1e-08
DECAY = 0.5
MATRIX_RATE = 1.5
VECTOR_RATE = 0.1
MASKED = -1e+30
HIGHEST = lax.Precision.HIGHEST

@jax.custom_vjp
def low(v):
    return lax.optimization_barrier(v.astype(jnp.bfloat16)).astype(jnp.float32)

@jax.custom_vjp
def low_back(v):
    return v

def low_keep(v):
    return (low(v), None)

def low_pass(kept, grad):
    return (grad,)

def back_keep(v):
    return (v, None)

def back_low(kept, grad):
    return (low(grad),)
low.defvjp(low_keep, low_pass)
low_back.defvjp(back_keep, back_low)

def layer_norm(values, gain, shift):
    center = values - lax.optimization_barrier(jnp.mean(values, axis=-1, keepdims=True))
    spread = lax.optimization_barrier(jnp.mean(center * center, axis=-1, keepdims=True))
    return center * lax.rsqrt(spread + NORM_EPSILON) * gain + shift

def split_vectors(packed):
    return [packed[index * D:(index + 1) * D] for index in range(8)] + [packed[8 * D:]]

def matmul(left, right):
    return jnp.dot(left, right, precision=HIGHEST, preferred_element_type=jnp.float32)

def assemble(blocks, grid_rows, grid_cols):
    shaped = blocks.reshape(grid_rows, grid_cols, BLK, BLK)
    return shaped.transpose(0, 2, 1, 3).reshape(grid_rows * BLK, grid_cols * BLK)

def allowed_pairs(lengths):
    ends = jnp.cumsum(lengths).astype(jnp.int32)
    places = jnp.arange(SEQ, dtype=jnp.int32)
    doc_index = lax.optimization_barrier(jnp.sum((places[:, None] >= ends[None, :]).astype(jnp.int32), axis=1))
    same_doc = doc_index[:, None] == doc_index[None, :]
    return same_doc & (places[None, :] <= places[:, None])

def attend_row(operands):
    queries, key_rows, value_rows, lengths = operands
    allowed = allowed_pairs(lengths)
    query_heads = queries.reshape(SEQ, HEADS, HEAD_DIM)
    key_heads = key_rows.reshape(SEQ, HEADS, HEAD_DIM)
    value_heads = value_rows.reshape(SEQ, HEADS, HEAD_DIM)
    raw = jnp.einsum('qhd,khd->hqk', query_heads, key_heads, precision=HIGHEST)
    scores = low_back(raw * HEAD_DIM ** (-0.5))
    probs = jax.nn.softmax(jnp.where(allowed[None], scores, MASKED), axis=-1)
    mixed = jnp.einsum('hqk,khd->qhd', low(probs), value_heads, precision=HIGHEST)
    return mixed.reshape(SEQ, D)

def group_forward(rows_in, lengths, weights, packed):
    w_qkv, w_out, w_fc, w_proj = weights
    ln1_gain, ln1_shift, q_bias, v_bias, out_bias, ln2_gain, ln2_shift, proj_bias, fc_bias = split_vectors(packed)
    normed1 = low(layer_norm(rows_in, ln1_gain, ln1_shift))
    bias_qkv = jnp.concatenate([q_bias, jnp.zeros_like(q_bias), v_bias])
    projected = low(low_back(matmul(normed1, w_qkv) + bias_qkv))
    count = lengths.shape[0]
    parts = projected.reshape(count, SEQ, 3 * D)
    attended = lax.map(jax.checkpoint(attend_row), (parts[:, :, :D], parts[:, :, D:2 * D], parts[:, :, 2 * D:], lengths))
    attended = low(low_back(attended.reshape(count * SEQ, D)))
    attn_out = low_back(matmul(attended, w_out) + out_bias)
    middle = rows_in + attn_out
    normed2 = low(layer_norm(middle, ln2_gain, ln2_shift))
    pre_act = low_back(matmul(normed2, w_fc) + fc_bias)
    hidden = low(jax.nn.gelu(pre_act, approximate=True))
    mlp_out = low_back(matmul(hidden, w_proj) + proj_bias)
    result = middle + mlp_out
    sums = jnp.stack([jnp.sum(middle * middle), jnp.sum(attn_out * attn_out), jnp.sum(mlp_out * mlp_out)])
    return (result, sums)

def reference(tokens, cotangent, doc_lengths, block_slot, matrices, vectors, vector_second, left_stat, right_stat, left_root, right_root):
    row_grid = D // BLK
    ff_grid = FF // BLK
    bounds = [0, 3 * row_grid * row_grid, 4 * row_grid * row_grid, 4 * row_grid * row_grid + row_grid * ff_grid, NBLK]
    shapes = [(row_grid, 3 * row_grid), (row_grid, row_grid), (row_grid, ff_grid), (ff_grid, row_grid)]
    group = math.gcd(ROWS, max(1, 4096 // SEQ))

    def forward(inputs, mats, packed):
        used = low(mats)[block_slot]
        weights = tuple((assemble(used[bounds[index]:bounds[index + 1]], shapes[index][0], shapes[index][1]) for index in range(4)))
        x_groups = inputs.reshape(ROWS // group, group * SEQ, D)
        length_groups = doc_lengths.reshape(ROWS // group, group, DOCS)

        def advance(total, operands):
            result, squares = jax.checkpoint(group_forward)(operands[0], operands[1], weights, packed)
            return (total + squares, result)
        squares, results = lax.scan(advance, jnp.zeros((3,), jnp.float32), (x_groups, length_groups))
        return (results.reshape(TOKENS, D), squares)
    inputs = tokens.astype(jnp.float32)
    (result, squares), pullback = jax.vjp(forward, inputs, matrices, vectors)
    x_grad, matrix_grad, vector_grad = pullback((cotangent.astype(jnp.float32), jnp.zeros((3,), jnp.float32)))
    all_squares = jnp.stack([squares[0], jnp.sum(result * result), squares[1], squares[2]])
    residual_scale = jnp.sqrt(all_squares / (TOKENS * D))
    left_new = DECAY * left_stat + (1.0 - DECAY) * jnp.einsum('bik,bjk->bij', matrix_grad, matrix_grad, precision=HIGHEST)
    right_new = DECAY * right_stat + (1.0 - DECAY) * jnp.einsum('bki,bkj->bij', matrix_grad, matrix_grad, precision=HIGHEST)
    half = jnp.einsum('bik,bkj->bij', left_root, matrix_grad, precision=HIGHEST)
    update = jnp.einsum('bik,bkj->bij', half, right_root, precision=HIGHEST)
    matrix_new = matrices - MATRIX_RATE * update
    second_new = DECAY * vector_second + (1.0 - DECAY) * vector_grad * vector_grad
    vector_new = vectors - VECTOR_RATE * vector_grad / (jnp.sqrt(second_new) + ROOT_EPSILON)
    return (result.astype(jnp.bfloat16), x_grad, matrix_grad, left_new, right_new, matrix_new, vector_grad, second_new, vector_new, residual_scale)
```

```python
import functools

import jax
import jax.numpy as jnp
from jax import lax
from jax.experimental import pallas as pl
from jax.experimental.pallas import tpu as pltpu
from jax.sharding import PartitionSpec as P

D = 768
HEADS = 12
HEAD_DIM = 64
FF = 3072
LONGEST = 512

NORM_EPSILON = 1e-05
ROOT_EPSILON = 1e-08
DECAY = 0.5
MATRIX_RATE = 1.5
VECTOR_RATE = 0.1
MASKED = -1e30

BF = jnp.bfloat16
F32 = jnp.float32
PAIR = 2 * HEAD_DIM
TILE = 256
VMEM = 60 * 1024 * 1024

LN1_GAIN, LN1_SHIFT, Q_BIAS, V_BIAS, OUT_BIAS, LN2_GAIN, LN2_SHIFT, PROJ_BIAS, FC_BIAS = range(9)


def nn(left, right):
    return jnp.dot(left, right, preferred_element_type=F32)


def nt(left, right):
    return lax.dot_general(left, right, (((1,), (1,)), ((), ())), preferred_element_type=F32)


def tn(left, right):
    return lax.dot_general(left, right, (((0,), (0,)), ((), ())), preferred_element_type=F32)


def col_sum(values):
    return jnp.sum(values, axis=0, keepdims=True)


def norm_parts(values):
    center = values - jnp.mean(values, axis=-1, keepdims=True)
    spread = jnp.mean(center * center, axis=-1, keepdims=True)
    root = lax.rsqrt(spread + NORM_EPSILON)
    return center * root, root


def norm_back(unit, root, gain, grad):
    scaled = grad * gain
    return root * (
        scaled
        - jnp.mean(scaled, axis=-1, keepdims=True)
        - unit * jnp.mean(scaled * unit, axis=-1, keepdims=True)
    )


def place(weight, blocks, rows, cols):
    width = blocks.shape[-1]
    for row in range(rows):
        for col in range(cols):
            weight[row * width : (row + 1) * width, col * width : (col + 1) * width] = blocks[
                row * cols + col
            ]


def call(kernel, grid, ins, outs, scratch=(), scalars=(), flops=0, name=None):
    spec = pltpu.PrefetchScalarGridSpec(
        num_scalar_prefetch=len(scalars),
        grid=grid,
        in_specs=[pl.BlockSpec(block, index) for _, block, index in ins],
        out_specs=[pl.BlockSpec(block, index) for _, _, block, index in outs],
        scratch_shapes=list(scratch),
    )
    shapes = [jax.ShapeDtypeStruct(shape, dtype) for shape, dtype, _, _ in outs]
    moved = sum(array.size * array.dtype.itemsize for array, _, _ in ins)
    moved += sum(shape.size * shape.dtype.itemsize for shape in shapes)
    return pl.pallas_call(
        kernel,
        grid_spec=spec,
        out_shape=shapes,
        compiler_params=pltpu.CompilerParams(
            dimension_semantics=("arbitrary",) * len(grid), vmem_limit_bytes=VMEM
        ),
        cost_estimate=pl.CostEstimate(flops=flops, bytes_accessed=moved, transcendentals=0),
        name=name,
    )(*scalars, *[array for array, _, _ in ins])


def qkv_kernel(x_ref, vec_ref, blocks_ref, normed_ref, projected_ref, weight):
    @pl.when(pl.program_id(0) == 0)
    def _():
        place(weight, blocks_ref, 2, 6)

    unit, _ = norm_parts(x_ref[...].astype(F32))
    normed = (unit * vec_ref[LN1_GAIN : LN1_GAIN + 1] + vec_ref[LN1_SHIFT : LN1_SHIFT + 1]).astype(
        BF
    )
    normed_ref[...] = normed
    for part in range(3):
        cols = slice(part * D, (part + 1) * D)
        value = nn(normed, weight[:, cols])
        if part != 1:
            row = Q_BIAS if part == 0 else V_BIAS
            value = value + vec_ref[row : row + 1]
        projected_ref[:, cols] = value.astype(BF)


def spans(seq_len):
    out = []
    start = 0
    for first in range(0, seq_len, TILE):
        low = max(0, first - LONGEST)
        out.append((first, low, first + TILE, start))
        start += first + TILE - low
    return out, start


def fill_bias(bias, lengths_ref, row, seq_len, docs):
    for first, low, high, start in spans(seq_len)[0]:
        place_q = lax.broadcasted_iota(jnp.int32, (1, TILE), 1) + first
        begin = jnp.zeros((1, TILE), jnp.int32)
        end = jnp.int32(0)
        for doc in range(docs):
            end = end + lengths_ref[row, doc]
            begin = jnp.where(place_q >= end, end, begin)
        place_k = lax.broadcasted_iota(jnp.int32, (high - low, TILE), 0) + low
        allowed = (place_k >= begin) & (place_k <= place_q)
        bias[start : start + high - low, :] = jnp.where(allowed, 0.0, MASKED)


def head_rows(values, head):
    rows = lax.broadcasted_iota(jnp.int32, values.shape, 0) // HEAD_DIM
    return jnp.where(rows == head, values, jnp.zeros_like(values))


def head_cols(values, head):
    cols = lax.broadcasted_iota(jnp.int32, values.shape, 1) // HEAD_DIM
    return jnp.where(cols == head, values, jnp.zeros_like(values))


def attend_kernel(lengths_ref, q_ref, k_ref, v_ref, out_ref, lse_ref, bias, mixed, *, row, docs):
    seq_len = q_ref.shape[0]

    @pl.when(pl.program_id(0) == 0)
    def _():
        fill_bias(bias, lengths_ref, row, seq_len, docs)

    query_t = (q_ref[...] * BF(HEAD_DIM**-0.5)).T
    value_t = v_ref[...].T
    for head in range(2):
        rows = slice(head * HEAD_DIM, (head + 1) * HEAD_DIM)
        query_h = head_rows(query_t, head)
        for first, low, high, start in spans(seq_len)[0]:
            cols = slice(first, first + TILE)
            scores = nn(k_ref[low:high, :], query_h[:, cols]) + bias[start : start + high - low, :]
            peak = jnp.max(scores, axis=0, keepdims=True)
            weights = jnp.exp(scores - peak)
            total = jnp.sum(weights, axis=0, keepdims=True)
            part = nn(value_t[rows, low:high], weights.astype(BF))
            mixed[rows, cols] = part / total
            lse_ref[0, head : head + 1, cols] = peak + jnp.log(total)
    out_ref[...] = mixed[...].astype(BF).T


def attend_back_kernel(
    lengths_ref,
    q_ref,
    k_ref,
    v_ref,
    out_ref,
    grad_ref,
    lse_ref,
    dq_ref,
    dk_ref,
    dv_ref,
    bias,
    key_sum,
    value_sum,
    query_sum,
    *,
    row,
    docs,
):
    seq_len = q_ref.shape[0]

    @pl.when(pl.program_id(0) == 0)
    def _():
        fill_bias(bias, lengths_ref, row, seq_len, docs)

    query = q_ref[...] * BF(HEAD_DIM**-0.5)
    query_t = query.T
    key_t = k_ref[...].T
    grad = grad_ref[...]
    grad_t = grad.T
    weighted = grad_t.astype(F32) * out_ref[...].T.astype(F32)
    key_sum[...] = jnp.zeros_like(key_sum)
    value_sum[...] = jnp.zeros_like(value_sum)
    for head in range(2):
        rows = slice(head * HEAD_DIM, (head + 1) * HEAD_DIM)
        query_th = head_rows(query_t, head)
        grad_th = head_rows(grad_t, head)
        query_h = head_cols(query, head)
        grad_h = head_cols(grad, head)
        inner = jnp.sum(weighted[rows, :], axis=0, keepdims=True)
        for first, low, high, start in spans(seq_len)[0]:
            cols = slice(first, first + TILE)
            scores = nn(k_ref[low:high, :], query_th[:, cols]) + bias[start : start + high - low, :]
            probs = jnp.exp(scores - lse_ref[0, head : head + 1, cols])
            grad_probs = nn(v_ref[low:high, :], grad_th[:, cols])
            grad_scores = (probs * (grad_probs - inner[:, cols])).astype(BF)
            value_sum[low:high, :] += nn(probs.astype(BF), grad_h[cols, :])
            key_sum[low:high, :] += nn(grad_scores, query_h[cols, :])
            query_sum[rows, cols] = nn(key_t[rows, low:high], grad_scores)
    dq_ref[...] = (query_sum[...] * (HEAD_DIM**-0.5)).astype(BF).T
    dk_ref[...] = key_sum[...].astype(BF)
    dv_ref[...] = value_sum[...].astype(BF)


def out_kernel(att_ref, x_ref, vec_ref, blocks_ref, middle_ref, normed_ref, sums_ref, weight):
    @pl.when(pl.program_id(0) == 0)
    def _():
        place(weight, blocks_ref, 2, 2)
        sums_ref[...] = jnp.zeros_like(sums_ref)

    branch = nn(att_ref[...], weight[...]) + vec_ref[OUT_BIAS : OUT_BIAS + 1]
    middle = x_ref[...].astype(F32) + branch
    middle_ref[...] = middle
    unit, _ = norm_parts(middle)
    normed_ref[...] = (
        unit * vec_ref[LN2_GAIN : LN2_GAIN + 1] + vec_ref[LN2_SHIFT : LN2_SHIFT + 1]
    ).astype(BF)
    sums_ref[0:1] += col_sum(middle * middle)
    sums_ref[1:2] += col_sum(branch * branch)


def mlp_kernel(
    normed_ref,
    cot_ref,
    vec_ref,
    fc_ref,
    proj_ref,
    mlp_ref,
    back_ref,
    dfc_ref,
    dproj_ref,
    bias_ref,
    w_fc,
    w_fc_t,
    w_proj,
    w_proj_t,
    hidden,
    grad_pre,
):
    tile = pl.program_id(0)
    place(w_fc, fc_ref.at[0], 1, 2)
    place(w_fc.at[pl.ds(D // 2, D // 2)], fc_ref.at[1], 1, 2)
    place(w_proj.at[pl.ds(0, D // 2)], proj_ref.at[0], 1, 2)
    place(w_proj.at[pl.ds(D // 2, D // 2)], proj_ref.at[1], 1, 2)
    w_fc_t[...] = w_fc[...].T
    w_proj_t[...] = w_proj[...].T
    bias_row = vec_ref[pl.ds(FC_BIAS + tile, 1)]

    @pl.when(tile == 0)
    def _():
        mlp_ref[...] = jnp.zeros_like(mlp_ref)
        back_ref[...] = jnp.zeros_like(back_ref)

    def chunk(index, total):
        rows = pl.ds(pl.multiple_of(index * TILE, TILE), TILE)
        pre = nn(normed_ref[rows], w_fc[...]) + bias_row
        grad = nn(cot_ref[rows], w_proj_t[...])
        root = 0.7978845608028654
        square = pre * pre
        tanh = jnp.tanh(pre * (root + root * 0.044715 * square))
        half = 0.5 + 0.5 * tanh
        low = (pre * half).astype(BF)
        slope = half + (0.5 * pre) * (1.0 - tanh * tanh) * (root + root * 3.0 * 0.044715 * square)
        back = (grad * slope).astype(BF)
        hidden[rows] = low
        grad_pre[rows] = back
        mlp_ref[rows] += nn(low, w_proj[...])
        back_ref[rows] += nn(back, w_fc_t[...])
        return total + col_sum(back.astype(F32))

    count = normed_ref.shape[0]
    bias_ref[0] = lax.fori_loop(0, count // TILE, chunk, jnp.zeros((1, D), F32))
    half = D // 2
    dproj = tn(hidden[...], cot_ref[...]).astype(BF)
    dfc = tn(normed_ref[...], grad_pre[...]).astype(BF)
    for row in range(2):
        for col in range(2):
            part = (slice(row * half, (row + 1) * half), slice(col * half, (col + 1) * half))
            dproj_ref[row, col] = dproj[part]
            dfc_ref[row, col] = dfc[part]


def middle_kernel(
    middle_ref,
    mlp_ref,
    back_ref,
    cot_ref,
    att_ref,
    vec_ref,
    blocks_ref,
    output_ref,
    grad_ref,
    grad_att_ref,
    dout_ref,
    sums_ref,
    weight,
    branch,
):
    step = pl.program_id(0)

    @pl.when(step == 0)
    def _():
        place(weight, blocks_ref, 2, 2)
        sums_ref[...] = jnp.zeros_like(sums_ref)

    middle = middle_ref[...]
    mlp = mlp_ref[...] + vec_ref[PROJ_BIAS : PROJ_BIAS + 1]
    result = middle + mlp
    output_ref[...] = result.astype(BF)
    cot = cot_ref[...].astype(F32)
    unit, root = norm_parts(middle)
    back = back_ref[...]
    grad = cot + norm_back(unit, root, vec_ref[LN2_GAIN : LN2_GAIN + 1], back)
    grad_ref[...] = grad
    low = grad.astype(BF)
    grad_att_ref[...] = nt(low, weight[...]).astype(BF)
    branch[pl.ds(pl.multiple_of(step * TILE, TILE), TILE)] = low
    sums_ref[0:1] += col_sum(result * result)
    sums_ref[1:2] += col_sum(mlp * mlp)
    sums_ref[2:3] += col_sum(back * unit)
    sums_ref[3:4] += col_sum(back)
    sums_ref[4:5] += col_sum(low.astype(F32))
    sums_ref[5:6] += col_sum(cot)

    @pl.when(step == pl.num_programs(0) - 1)
    def _():
        half = D // 2
        dout = tn(att_ref[...], branch[...]).astype(BF)
        for row in range(2):
            for col in range(2):
                dout_ref[2 * row + col] = dout[
                    row * half : (row + 1) * half, col * half : (col + 1) * half
                ]


def dqkv_kernel(normed_ref, dq_ref, dk_ref, dv_ref, grad_ref, sums_ref):
    half = D // 2
    sums_ref[0:1] = col_sum(dq_ref[...].astype(F32))
    sums_ref[1:2] = col_sum(dv_ref[...].astype(F32))
    for part, ref in enumerate((dq_ref, dk_ref, dv_ref)):
        grad = tn(normed_ref[...], ref[...]).astype(BF)
        for row in range(2):
            for col in range(2):
                grad_ref[row * 6 + part * 2 + col] = grad[
                    row * half : (row + 1) * half, col * half : (col + 1) * half
                ]


def input_kernel(
    x_ref, dq_ref, dk_ref, dv_ref, grad_ref, vec_ref, blocks_ref, out_ref, sums_ref, weight
):
    @pl.when(pl.program_id(0) == 0)
    def _():
        place(weight, blocks_ref, 2, 6)
        sums_ref[...] = jnp.zeros_like(sums_ref)

    back = nt(dq_ref[...], weight[:, :D])
    back += nt(dk_ref[...], weight[:, D : 2 * D])
    back += nt(dv_ref[...], weight[:, 2 * D :])
    unit, root = norm_parts(x_ref[...].astype(F32))
    out_ref[...] = grad_ref[...] + norm_back(unit, root, vec_ref[LN1_GAIN : LN1_GAIN + 1], back)
    sums_ref[0:1] += col_sum(back * unit)
    sums_ref[1:2] += col_sum(back)


def factor_kernel(
    shard_ref,
    grad_ref,
    right_ref,
    matrix_ref,
    left_stat_ref,
    right_stat_ref,
    left_root_ref,
    rows_ref,
    left_ref,
    right_new_ref,
    matrix_new_ref,
    grad_t,
):
    rows = matrix_ref.shape[1]
    grad = grad_ref[0]
    grad_t[...] = grad.T
    own = pl.ds(pl.multiple_of(shard_ref[0] * rows, rows), rows)
    grad_rows = grad_ref[0, own, :]
    rows_ref[0] = grad_rows.astype(F32)
    left_ref[0] = DECAY * left_stat_ref[0] + (1.0 - DECAY) * nn(grad_rows, grad_t[...])
    right_new_ref[0] = DECAY * right_stat_ref[0] + (1.0 - DECAY) * nn(grad_t[own, :], grad)
    half = nn(left_root_ref[0].astype(BF), grad)
    update = nn(half.astype(BF), right_ref[0])
    matrix_new_ref[0] = matrix_ref[0] - MATRIX_RATE * update


def whole(array):
    return (array, array.shape, lambda *_: (0,) * array.ndim)


def tokens_in(array, cols=None):
    return (array, (TILE, cols or array.shape[1]), lambda i, *_: (i, 0))


def out_whole(shape, dtype):
    return (shape, dtype, shape, lambda *_: (0,) * len(shape))


def per_device(
    tokens,
    cotangent,
    doc_lengths,
    block_slot,
    matrices,
    vectors,
    vector_second,
    left_stat,
    right_stat,
    left_root,
    right_root,
):
    dp_count = lax.axis_size("dp")
    fsdp_count = lax.axis_size("fsdp")
    own_blocks, own_rows, width = matrices.shape
    blocks = own_blocks * dp_count
    slot_place = block_slot % own_blocks * dp_count + block_slot // own_blocks
    low_shards = matrices.astype(BF)
    gathered = lax.all_gather(low_shards, ("dp", "fsdp"), axis=1, tiled=True)
    used = jnp.take(gathered.reshape(blocks, width, width), slot_place, axis=0)
    right_whole = lax.all_gather(right_root.astype(BF), "fsdp", axis=1, tiled=True)

    vec = vectors.reshape(-1, D)
    count = tokens.shape[0]
    rows_here, docs = doc_lengths.shape
    seq_len = count // rows_here
    steps = count // TILE
    weight_scratch = [pltpu.VMEM((D, 3 * D), BF)]
    small_scratch = [pltpu.VMEM((D, D), BF)]
    qkv_in = (used, (12, width, width), lambda *_: (0, 0, 0))
    out_in = (used, (4, width, width), lambda *_: (3, 0, 0))

    normed1, projected = call(
        qkv_kernel,
        (steps,),
        [tokens_in(tokens), whole(vec), qkv_in],
        [
            ((count, D), BF, (TILE, D), lambda i: (i, 0)),
            ((count, 3 * D), BF, (TILE, 3 * D), lambda i: (i, 0)),
        ],
        weight_scratch,
        flops=2 * count * D * 3 * D,
        name="qkv",
    )

    pairs = HEADS // 2
    bias_rows = spans(seq_len)[1]

    def pair_in(array, row, offset):
        return (array, (seq_len, PAIR), lambda p, *_: (row, offset + p))

    attended, lses = [], []
    for row in range(rows_here):
        one, lse = call(
            functools.partial(attend_kernel, row=row, docs=docs),
            (pairs,),
            [pair_in(projected, row, part * pairs) for part in range(3)],
            [
                ((seq_len, D), BF, (seq_len, PAIR), lambda p, *_: (0, p)),
                ((pairs, 2, seq_len), F32, (1, 2, seq_len), lambda p, *_: (p, 0, 0)),
            ],
            [pltpu.VMEM((bias_rows, TILE), F32), pltpu.VMEM((PAIR, seq_len), F32)],
            scalars=[doc_lengths],
            flops=8 * seq_len * seq_len * D,
            name="attend",
        )
        attended.append(one)
        lses.append(lse)
    attended = attended[0] if rows_here == 1 else jnp.concatenate(attended, axis=0)

    middle, normed2, sums_mid = call(
        out_kernel,
        (steps,),
        [tokens_in(attended), tokens_in(tokens), whole(vec), out_in],
        [
            ((count, D), F32, (TILE, D), lambda i: (i, 0)),
            ((count, D), BF, (TILE, D), lambda i: (i, 0)),
            out_whole((8, D), F32),
        ],
        small_scratch,
        flops=2 * count * D * D,
        name="attn_out",
    )

    ff_tiles = FF // D
    fc_view = used.reshape(6, 8, width, width)
    proj_view = used.reshape(24, 2, width, width)
    mlp, back2, dfc, dproj, fc_bias_grad = call(
        mlp_kernel,
        (ff_tiles,),
        [
            whole(normed2),
            whole(cotangent),
            whole(vec),
            (fc_view, (2, 2, width, width), lambda t: (1, t, 0, 0)),
            (proj_view, (2, 2, width, width), lambda t: (8 + t, 0, 0, 0)),
        ],
        [
            out_whole((count, D), F32),
            out_whole((count, D), F32),
            ((2, 8, width, width), BF, (2, 2, width, width), lambda t: (0, t, 0, 0)),
            ((8, 2, width, width), BF, (2, 2, width, width), lambda t: (t, 0, 0, 0)),
            ((ff_tiles, 1, D), F32, (1, 1, D), lambda t: (t, 0, 0)),
        ],
        [pltpu.VMEM((D, D), BF)] * 4 + [pltpu.VMEM((count, D), BF)] * 2,
        flops=12 * count * D * FF,
        name="mlp",
    )

    output, grad_middle, grad_attended, dout, sums_back = call(
        middle_kernel,
        (steps,),
        [
            tokens_in(middle),
            tokens_in(mlp),
            tokens_in(back2),
            tokens_in(cotangent),
            whole(attended),
            whole(vec),
            out_in,
        ],
        [
            ((count, D), BF, (TILE, D), lambda i: (i, 0)),
            ((count, D), F32, (TILE, D), lambda i: (i, 0)),
            ((count, D), BF, (TILE, D), lambda i: (i, 0)),
            out_whole((4, width, width), BF),
            out_whole((8, D), F32),
        ],
        small_scratch + [pltpu.VMEM((count, D), BF)],
        flops=4 * count * D * D,
        name="middle_back",
    )

    query_grads, key_grads, value_grads = [], [], []
    for row in range(rows_here):
        grads = call(
            functools.partial(attend_back_kernel, row=row, docs=docs),
            (pairs,),
            [pair_in(projected, row, part * pairs) for part in range(3)]
            + [
                pair_in(attended, row, 0),
                pair_in(grad_attended, row, 0),
                (lses[row], (1, 2, seq_len), lambda p, *_: (p, 0, 0)),
            ],
            [((seq_len, D), BF, (seq_len, PAIR), lambda p, *_: (0, p))] * 3,
            [
                pltpu.VMEM((bias_rows, TILE), F32),
                pltpu.VMEM((seq_len, PAIR), F32),
                pltpu.VMEM((seq_len, PAIR), F32),
                pltpu.VMEM((PAIR, seq_len), F32),
            ],
            scalars=[doc_lengths],
            flops=20 * seq_len * seq_len * D,
            name="attend_back",
        )
        for held, one in zip((query_grads, key_grads, value_grads), grads):
            held.append(one)
    dq, dk, dv = [
        held[0] if rows_here == 1 else jnp.concatenate(held, axis=0)
        for held in (query_grads, key_grads, value_grads)
    ]

    dqkv, sums_qkv = call(
        dqkv_kernel,
        (1,),
        [whole(normed1), whole(dq), whole(dk), whole(dv)],
        [out_whole((12, width, width), BF), out_whole((8, D), F32)],
        flops=2 * count * D * 3 * D,
        name="qkv_weight_back",
    )
    x_grad, sums_in = call(
        input_kernel,
        (steps,),
        [
            tokens_in(tokens),
            tokens_in(dq),
            tokens_in(dk),
            tokens_in(dv),
            tokens_in(grad_middle),
            whole(vec),
            qkv_in,
        ],
        [((count, D), F32, (TILE, D), lambda i: (i, 0)), out_whole((8, D), F32)],
        weight_scratch,
        flops=2 * count * D * 3 * D,
        name="input_back",
    )

    vector_local = jnp.concatenate(
        [
            sums_in[0],
            sums_in[1],
            sums_qkv[0],
            sums_qkv[1],
            sums_back[4],
            sums_back[2],
            sums_back[3],
            sums_back[5],
            fc_bias_grad.reshape(-1),
        ]
    )
    square_terms = jnp.stack(
        [jnp.sum(sums_mid[0]), jnp.sum(sums_back[0]), jnp.sum(sums_mid[1]), jnp.sum(sums_back[1])]
    )
    vector_grad, square_sums = lax.psum((vector_local, square_terms), ("dp", "fsdp"))

    grads_used = jnp.concatenate(
        [dqkv, dout, dfc.reshape(16, width, width), dproj.reshape(16, width, width)], axis=0
    )
    grads_laid = jnp.take(grads_used, jnp.argsort(slot_place), axis=0).reshape(
        own_blocks, dp_count * width, width
    )
    grad_rows = lax.psum_scatter(grads_laid, ("dp", "fsdp"), scatter_dimension=1, tiled=True)
    grad_whole = lax.all_gather(grad_rows, "fsdp", axis=1, tiled=True)

    shard = lax.axis_index("fsdp").astype(jnp.int32).reshape(1)

    def block_in(array):
        return (array, (1,) + array.shape[1:], lambda b, *_: (b, 0, 0))

    matrix_grad, left_new, right_new, matrix_new = call(
        factor_kernel,
        (own_blocks,),
        [
            block_in(a)
            for a in (grad_whole, right_whole, matrices, left_stat, right_stat, left_root)
        ],
        [(matrices.shape, F32, (1, own_rows, width), lambda b, *_: (b, 0, 0))] * 4,
        [pltpu.VMEM((width, width), BF)],
        scalars=[shard],
        flops=8 * own_blocks * own_rows * width * width,
        name="factor",
    )

    residual_scale = jnp.sqrt(square_sums / (count * dp_count * fsdp_count * D))
    second_new = DECAY * vector_second + (1.0 - DECAY) * vector_grad * vector_grad
    vector_new = vectors - VECTOR_RATE * vector_grad / (jnp.sqrt(second_new) + ROOT_EPSILON)
    return (
        output,
        x_grad,
        matrix_grad,
        left_new,
        right_new,
        matrix_new,
        vector_grad,
        second_new,
        vector_new,
        residual_scale,
    )


def solution(mesh):
    tokens = P(("dp", "fsdp"), None)
    stored = P("dp", "fsdp", None)
    return jax.shard_map(
        per_device,
        mesh=mesh,
        in_specs=(tokens, tokens, tokens, P(), stored, P(), P()) + (stored,) * 4,
        out_specs=(tokens, tokens) + (stored,) * 4 + (P(),) * 4,
        check_vma=False,
    )
```

```python
import functools

import jax
import jax.numpy as jnp
from jax import lax
from jax.experimental import pallas as pl
from jax.experimental.pallas import tpu as pltpu
from jax.sharding import PartitionSpec as P

D = 768
HEADS = 12
HEAD_DIM = 64
FF = 3072
LONGEST = 512

NORM_EPSILON = 1e-05
ROOT_EPSILON = 1e-08
DECAY = 0.5
MATRIX_RATE = 1.5
VECTOR_RATE = 0.1
MASKED = -1e30

BF = jnp.bfloat16
F32 = jnp.float32
PAIR = 2 * HEAD_DIM
TILE = 256
VMEM = 60 * 1024 * 1024
FIRST_TILES = 2

LN1_GAIN, LN1_SHIFT, Q_BIAS, V_BIAS, OUT_BIAS, LN2_GAIN, LN2_SHIFT, PROJ_BIAS, FC_BIAS = range(9)


def nn(left, right):
    return jnp.dot(left, right, preferred_element_type=F32)


def nt(left, right):
    return lax.dot_general(left, right, (((1,), (1,)), ((), ())), preferred_element_type=F32)


def tn(left, right):
    return lax.dot_general(left, right, (((0,), (0,)), ((), ())), preferred_element_type=F32)


def col_sum(values):
    return jnp.sum(values, axis=0, keepdims=True)


def norm_parts(values):
    center = values - jnp.mean(values, axis=-1, keepdims=True)
    spread = jnp.mean(center * center, axis=-1, keepdims=True)
    root = lax.rsqrt(spread + NORM_EPSILON)
    return center * root, root


def norm_back(unit, root, gain, grad):
    scaled = grad * gain
    return root * (
        scaled
        - jnp.mean(scaled, axis=-1, keepdims=True)
        - unit * jnp.mean(scaled * unit, axis=-1, keepdims=True)
    )


def place(weight, blocks, rows, cols):
    width = blocks[0].shape[-1]
    for row in range(rows):
        for col in range(cols):
            weight[row * width : (row + 1) * width, col * width : (col + 1) * width] = blocks[
                row * cols + col
            ][0]


def call(kernel, grid, ins, outs, scratch=(), scalars=(), ties=(), name=None):
    first = len(scalars) + len(ins)

    def body(*refs):
        kernel(*refs[:first], *refs[first + len(ties) :])

    spec = pltpu.PrefetchScalarGridSpec(
        num_scalar_prefetch=len(scalars),
        grid=grid,
        in_specs=[pl.BlockSpec(block, index) for _, block, index in ins]
        + [pl.BlockSpec(memory_space=pl.ANY)] * len(ties),
        out_specs=[pl.BlockSpec(block, index) for _, _, block, index in outs],
        scratch_shapes=list(scratch),
    )
    return pl.pallas_call(
        body,
        grid_spec=spec,
        out_shape=[jax.ShapeDtypeStruct(shape, dtype) for shape, dtype, _, _ in outs],
        compiler_params=pltpu.CompilerParams(
            dimension_semantics=("arbitrary",) * len(grid), vmem_limit_bytes=VMEM
        ),
        cost_estimate=pl.CostEstimate(flops=1024, bytes_accessed=1024, transcendentals=0),
        name=name,
    )(*scalars, *[array for array, _, _ in ins], *ties)


def whole(array):
    return (array, array.shape, lambda *_: (0,) * array.ndim)


def tokens_in(array, cols=None):
    return (array, (TILE, cols or array.shape[1]), lambda i, *_: (i, 0))


def out_whole(shape, dtype):
    return (shape, dtype, shape, lambda *_: (0,) * len(shape))


def plane_sum_kernel(half_ref, *refs):
    half = len(refs) // 2
    for parts, out in zip(refs[:half], refs[half:]):
        total = parts[0].astype(F32)
        for part in range(1, parts.shape[0]):
            total = total + parts[part].astype(F32)
        out[...] = total.astype(BF)


def plane_sum(parts, half, ties, name):
    count, blocks, height, width = parts.shape
    size = blocks // 2

    def group(offset):
        return (parts, (count, size, height, width), lambda i, at: (0, at[0] ^ offset, 0, 0))

    return call(
        plane_sum_kernel,
        (1,),
        [group(0), group(1)],
        [out_whole((size, height, width), BF)] * 2,
        scalars=[half],
        ties=ties,
        name=name,
    )


def add_kernel(left_ref, right_ref, out_ref):
    out_ref[...] = (left_ref[...].astype(F32) + right_ref[...].astype(F32)).astype(BF)


def add_up(left, right, ties, name):
    return call(
        add_kernel,
        (1,),
        [whole(left), whole(right)],
        [out_whole(left.shape, BF)],
        ties=ties,
        name=name,
    )[0]


def line_half(halves, ties, name):
    return add_up(halves[0], across_fsdp(halves[1], 1), ties, name)


def line_rest(total, ties, name):
    offset = 3
    while offset <= lax.axis_size("fsdp"):
        total = add_up(total, across_fsdp(total, offset), ties, name)
        offset = 2 * offset - 1
    return total


def line_spread(total):
    return [total, across_fsdp(total, 1)]


def pack_kernel(in_ref, qkv_ref, back_ref, mid_ref, *refs):
    fc_refs, out_ref = refs[:-1], refs[-1]
    out_ref[0:2] = in_ref[0:2]
    out_ref[2:4] = qkv_ref[0:2]
    out_ref[4:5] = back_ref[4:5]
    out_ref[5:7] = back_ref[2:4]
    out_ref[7:8] = back_ref[5:6]
    row = 8
    for ref in fc_refs:
        for tile in range(ref.shape[0]):
            out_ref[row : row + 1] = ref[tile]
            row += 1
    lanes = lax.broadcasted_iota(jnp.int32, (1, D), 1)
    line = jnp.zeros((1, D), F32)
    for lane, value in enumerate((mid_ref[0:1], back_ref[0:1], mid_ref[1:2], back_ref[1:2])):
        line = jnp.where(lanes == lane, jnp.sum(value), line)
    out_ref[row : row + 1] = line
    out_ref[row + 1 :] = jnp.zeros_like(out_ref[row + 1 :])


def qkv_kernel(place_ref, x_ref, vec_ref, *refs):
    blocks, (normed_ref, projected_ref, weight) = refs[:12], refs[12:]

    @pl.when(pl.program_id(0) == 0)
    def _():
        place(weight, blocks, 2, 6)

    unit, _ = norm_parts(x_ref[...].astype(F32))
    normed = (unit * vec_ref[LN1_GAIN : LN1_GAIN + 1] + vec_ref[LN1_SHIFT : LN1_SHIFT + 1]).astype(
        BF
    )
    normed_ref[...] = normed
    for part in range(3):
        cols = slice(part * D, (part + 1) * D)
        value = nn(normed, weight[:, cols])
        if part != 1:
            row = Q_BIAS if part == 0 else V_BIAS
            value = value + vec_ref[row : row + 1]
        projected_ref[:, cols] = value.astype(BF)


def spans(seq_len):
    out = []
    start = 0
    for first in range(0, seq_len, TILE):
        low = max(0, first - LONGEST)
        out.append((first, low, first + TILE, start))
        start += first + TILE - low
    return out, start


def fill_bias(bias, lengths_ref, row, seq_len, docs):
    for first, low, high, start in spans(seq_len)[0]:
        place_q = lax.broadcasted_iota(jnp.int32, (1, TILE), 1) + first
        begin = jnp.zeros((1, TILE), jnp.int32)
        end = jnp.int32(0)
        for doc in range(docs):
            end = end + lengths_ref[row, doc]
            begin = jnp.where(place_q >= end, end, begin)
        place_k = lax.broadcasted_iota(jnp.int32, (high - low, TILE), 0) + low
        allowed = (place_k >= begin) & (place_k <= place_q)
        bias[start : start + high - low, :] = jnp.where(allowed, 0.0, MASKED)


def head_rows(values, head):
    rows = lax.broadcasted_iota(jnp.int32, values.shape, 0) // HEAD_DIM
    return jnp.where(rows == head, values, jnp.zeros_like(values))


def head_cols(values, head):
    cols = lax.broadcasted_iota(jnp.int32, values.shape, 1) // HEAD_DIM
    return jnp.where(cols == head, values, jnp.zeros_like(values))


def attend_kernel(lengths_ref, q_ref, k_ref, v_ref, out_ref, lse_ref, bias, mixed, *, row, docs):
    seq_len = q_ref.shape[0]

    @pl.when(pl.program_id(0) == 0)
    def _():
        fill_bias(bias, lengths_ref, row, seq_len, docs)

    query_t = (q_ref[...] * BF(HEAD_DIM**-0.5)).T
    value_t = v_ref[...].T
    for head in range(2):
        rows = slice(head * HEAD_DIM, (head + 1) * HEAD_DIM)
        query_h = head_rows(query_t, head)
        for first, low, high, start in spans(seq_len)[0]:
            cols = slice(first, first + TILE)
            scores = nn(k_ref[low:high, :], query_h[:, cols]) + bias[start : start + high - low, :]
            peak = jnp.max(scores, axis=0, keepdims=True)
            weights = jnp.exp(scores - peak)
            total = jnp.sum(weights, axis=0, keepdims=True)
            part = nn(value_t[rows, low:high], weights.astype(BF))
            mixed[rows, cols] = part / total
            lse_ref[0, head : head + 1, cols] = peak + jnp.log(total)
    out_ref[...] = mixed[...].astype(BF).T


def attend_back_kernel(
    lengths_ref,
    q_ref,
    k_ref,
    v_ref,
    out_ref,
    grad_ref,
    lse_ref,
    dq_ref,
    dk_ref,
    dv_ref,
    bias,
    key_sum,
    value_sum,
    query_sum,
    *,
    row,
    docs,
):
    seq_len = q_ref.shape[0]

    @pl.when(pl.program_id(0) == 0)
    def _():
        fill_bias(bias, lengths_ref, row, seq_len, docs)

    query = q_ref[...] * BF(HEAD_DIM**-0.5)
    query_t = query.T
    key_t = k_ref[...].T
    grad = grad_ref[...]
    grad_t = grad.T
    weighted = grad_t.astype(F32) * out_ref[...].T.astype(F32)
    key_sum[...] = jnp.zeros_like(key_sum)
    value_sum[...] = jnp.zeros_like(value_sum)
    for head in range(2):
        rows = slice(head * HEAD_DIM, (head + 1) * HEAD_DIM)
        query_th = head_rows(query_t, head)
        grad_th = head_rows(grad_t, head)
        query_h = head_cols(query, head)
        grad_h = head_cols(grad, head)
        inner = jnp.sum(weighted[rows, :], axis=0, keepdims=True)
        for first, low, high, start in spans(seq_len)[0]:
            cols = slice(first, first + TILE)
            scores = nn(k_ref[low:high, :], query_th[:, cols]) + bias[start : start + high - low, :]
            probs = jnp.exp(scores - lse_ref[0, head : head + 1, cols])
            grad_probs = nn(v_ref[low:high, :], grad_th[:, cols])
            grad_scores = (probs * (grad_probs - inner[:, cols])).astype(BF)
            value_sum[low:high, :] += nn(probs.astype(BF), grad_h[cols, :])
            key_sum[low:high, :] += nn(grad_scores, query_h[cols, :])
            query_sum[rows, cols] = nn(key_t[rows, low:high], grad_scores)
    dq_ref[...] = (query_sum[...] * (HEAD_DIM**-0.5)).astype(BF).T
    dk_ref[...] = key_sum[...].astype(BF)
    dv_ref[...] = value_sum[...].astype(BF)


def out_kernel(place_ref, att_ref, x_ref, vec_ref, *refs):
    blocks, (middle_ref, normed_ref, sums_ref, weight) = refs[:4], refs[4:]

    @pl.when(pl.program_id(0) == 0)
    def _():
        place(weight, blocks, 2, 2)
        sums_ref[...] = jnp.zeros_like(sums_ref)

    branch = nn(att_ref[...], weight[...]) + vec_ref[OUT_BIAS : OUT_BIAS + 1]
    middle = x_ref[...].astype(F32) + branch
    middle_ref[...] = middle
    unit, _ = norm_parts(middle)
    normed_ref[...] = (
        unit * vec_ref[LN2_GAIN : LN2_GAIN + 1] + vec_ref[LN2_SHIFT : LN2_SHIFT + 1]
    ).astype(BF)
    sums_ref[0:1] += col_sum(middle * middle)
    sums_ref[1:2] += col_sum(branch * branch)


def put_pieces(keep_ref, send_ref, grad, core, base):
    height, width = keep_ref.shape[-2:]
    for held, ref in enumerate((keep_ref, send_ref)):
        for pair in range(ref.shape[0]):
            piece = 2 * pair + (core ^ held)
            for row in range(2):
                top = pl.multiple_of(row * width + piece * height, 8)
                for col in range(2):
                    ref[pair, base + 2 * row + col] = grad[
                        pl.ds(top, height), col * width : (col + 1) * width
                    ].astype(BF)


def mlp_kernel(place_ref, me_ref, normed_ref, cot_ref, vec_ref, *refs, first, paired):
    fc_blocks, proj_blocks, refs = refs[:4], refs[4:8], refs[8:]
    if first == 0:
        before = None
    else:
        before, refs = refs[:2], refs[2:]
    if paired:
        mlp_ref, back_ref, keep_ref, send_ref, bias_ref = refs[:5]
        refs = refs[5:]
    else:
        mlp_ref, back_ref, grad_ref, bias_ref = refs[:4]
        refs = refs[4:]
    w_fc, w_fc_t, w_proj, w_proj_t, hidden, grad_pre, whole_grad = refs
    step = pl.program_id(0)
    place(w_fc, fc_blocks, 2, 2)
    place(w_proj, proj_blocks, 2, 2)
    w_fc_t[...] = w_fc[...].T
    w_proj_t[...] = w_proj[...].T
    bias_row = vec_ref[pl.ds(FC_BIAS + first + step, 1)]

    @pl.when(step == 0)
    def _():
        if first == 0:
            mlp_ref[...] = jnp.zeros_like(mlp_ref)
            back_ref[...] = jnp.zeros_like(back_ref)
        else:
            mlp_ref[...] = before[0][...]
            back_ref[...] = before[1][...]

    def chunk(index, total):
        rows = pl.ds(pl.multiple_of(index * TILE, TILE), TILE)
        pre = nn(normed_ref[rows], w_fc[...]) + bias_row
        grad = nn(cot_ref[rows], w_proj_t[...])
        root = 0.7978845608028654
        square = pre * pre
        tanh = jnp.tanh(pre * (root + root * 0.044715 * square))
        half = 0.5 + 0.5 * tanh
        low = (pre * half).astype(BF)
        slope = half + (0.5 * pre) * (1.0 - tanh * tanh) * (root + root * 3.0 * 0.044715 * square)
        back = (grad * slope).astype(BF)
        hidden[rows] = low
        grad_pre[rows] = back
        mlp_ref[rows] += nn(low, w_proj[...])
        back_ref[rows] += nn(back, w_fc_t[...])
        return total + col_sum(back.astype(F32))

    count = normed_ref.shape[0]
    bias_ref[0] = lax.fori_loop(0, count // TILE, chunk, jnp.zeros((1, D), F32))
    for base, left, right in ((0, normed_ref, grad_pre), (4, hidden, cot_ref)):
        if paired:
            whole_grad[...] = tn(left[...], right[...])
            put_pieces(keep_ref, send_ref, whole_grad, me_ref[0] % 2, base)
        else:
            pieces, _, _, height, width = grad_ref.shape
            grad = tn(left[...], right[...]).astype(BF)
            for row in range(2):
                for col in range(2):
                    for piece in range(pieces):
                        top = row * width + piece * height
                        grad_ref[piece, 0, base + 2 * row + col] = grad[
                            top : top + height, col * width : (col + 1) * width
                        ]


def middle_kernel(
    place_ref,
    me_ref,
    middle_ref,
    mlp_ref,
    back_ref,
    cot_ref,
    att_ref,
    vec_ref,
    *refs,
):
    blocks, refs = refs[:4], refs[4:]
    output_ref, grad_ref, grad_att_ref, keep_ref, send_ref, sums_ref, weight, branch, out_grad = refs
    step = pl.program_id(0)

    @pl.when(step == 0)
    def _():
        place(weight, blocks, 2, 2)
        sums_ref[...] = jnp.zeros_like(sums_ref)

    middle = middle_ref[...]
    mlp = mlp_ref[...] + vec_ref[PROJ_BIAS : PROJ_BIAS + 1]
    result = middle + mlp
    output_ref[...] = result.astype(BF)
    cot = cot_ref[...].astype(F32)
    unit, root = norm_parts(middle)
    back = back_ref[...]
    grad = cot + norm_back(unit, root, vec_ref[LN2_GAIN : LN2_GAIN + 1], back)
    grad_ref[...] = grad
    low = grad.astype(BF)
    branch[pl.ds(pl.multiple_of(step * TILE, TILE), TILE)] = low
    grad_att_ref[...] = nt(low, weight[...]).astype(BF)
    sums_ref[0:1] += col_sum(result * result)
    sums_ref[1:2] += col_sum(mlp * mlp)
    sums_ref[2:3] += col_sum(back * unit)
    sums_ref[3:4] += col_sum(back)
    sums_ref[4:5] += col_sum(low.astype(F32))
    sums_ref[5:6] += col_sum(cot)

    @pl.when(step == pl.num_programs(0) - 1)
    def _():
        out_grad[...] = tn(att_ref[...], branch[...])
        put_pieces(keep_ref, send_ref, out_grad, me_ref[0] % 2, 0)


def weight_back_kernel(
    me_ref, normed_ref, dq_ref, dk_ref, dv_ref, keep_ref, send_ref, sums_ref, grad
):
    step = pl.program_id(0)

    @pl.when(step == 0)
    def _():
        sums_ref[0:1] = col_sum(dq_ref[...].astype(F32))
        sums_ref[1:2] = col_sum(dv_ref[...].astype(F32))

    for part, ref in enumerate((dq_ref, dk_ref, dv_ref)):

        @pl.when(step == part)
        def _():
            grad[...] = tn(normed_ref[...], ref[...])

    put_pieces(keep_ref, send_ref, grad, me_ref[0] % 2, 0)


def input_kernel(place_ref, x_ref, dq_ref, dk_ref, dv_ref, grad_ref, vec_ref, *refs):
    blocks, (out_ref, sums_ref, weight) = refs[:12], refs[12:]

    @pl.when(pl.program_id(0) == 0)
    def _():
        place(weight, blocks, 2, 6)
        sums_ref[...] = jnp.zeros_like(sums_ref)

    back = nt(dq_ref[...], weight[:, :D])
    back += nt(dk_ref[...], weight[:, D : 2 * D])
    back += nt(dv_ref[...], weight[:, 2 * D :])
    unit, root = norm_parts(x_ref[...].astype(F32))
    out_ref[...] = grad_ref[...] + norm_back(unit, root, vec_ref[LN1_GAIN : LN1_GAIN + 1], back)
    sums_ref[0:1] += col_sum(back * unit)
    sums_ref[1:2] += col_sum(back)


def lay_kernel(source_ref, *refs):
    out_ref, pieces = refs[-2:]
    begin = 0
    for ref in refs[:-2]:
        pieces[begin : begin + ref.shape[0]] = ref[...]
        begin += ref.shape[0]
    shards, own = out_ref.shape[:2]
    for shard in range(shards):
        for slot in range(own):
            out_ref[shard, slot] = pieces[source_ref[shard * own + slot]]


def factor_kernel(
    shard_ref,
    grad_ref,
    right_ref,
    matrix_ref,
    left_stat_ref,
    right_stat_ref,
    left_root_ref,
    rows_ref,
    left_ref,
    right_new_ref,
    matrix_new_ref,
    whole_grad,
    grad_t,
):
    rows = matrix_ref.shape[1]
    pieces, _, height, _ = grad_ref.shape
    for piece in range(pieces):
        whole_grad[piece * height : (piece + 1) * height, :] = grad_ref[piece, 0]
    grad = whole_grad[...]
    grad_t[...] = grad.T
    own = pl.ds(pl.multiple_of(shard_ref[0] * rows, rows), rows)
    grad_rows = whole_grad[own, :]
    rows_ref[0] = grad_rows.astype(F32)
    left_ref[0] = DECAY * left_stat_ref[0] + (1.0 - DECAY) * nn(grad_rows, grad_t[...])
    right_new_ref[0] = DECAY * right_stat_ref[0] + (1.0 - DECAY) * nn(grad_t[own, :], grad)
    half = nn(left_root_ref[0].astype(BF), grad)
    update = nn(half.astype(BF), right_ref[0])
    matrix_new_ref[0] = matrix_ref[0] - MATRIX_RATE * update


def core_sum_kernel(*refs):
    out_ref = refs[-1]
    begin = 0
    for keep, sent in zip(refs[:-1:2], refs[1:-1:2]):
        blocks = keep.shape[1]
        out_ref[0, begin : begin + blocks] = (keep[0].astype(F32) + sent[0].astype(F32)).astype(BF)
        begin += blocks


def across_dp(values, bit):
    count = lax.axis_size("dp")
    return lax.ppermute(values, "dp", [(i, i ^ (1 << bit)) for i in range(count)])


def across_fsdp(values, offset):
    count = lax.axis_size("fsdp")
    return lax.ppermute(values, "fsdp", [(i, i ^ offset) for i in range(count)])


def core_sum(grads, name, ties=()):
    ins = []
    for keep, send in grads:
        ins += [keep, across_dp(send, 0)]
    pairs = ins[0].shape[0]
    rest = ins[0].shape[2:]
    blocks = sum(keep.shape[1] for keep, _ in grads)

    def one(array):
        return (array, (1,) + array.shape[1:], lambda i: (i, 0, 0, 0))

    return call(
        core_sum_kernel,
        (pairs,),
        [one(array) for array in ins],
        [((pairs, blocks) + rest, BF, (1, blocks) + rest, lambda i: (i, 0, 0, 0))],
        ties=ties,
        name=name,
    )[0]


def plane_parts(values):
    pairs = lax.axis_size("dp") // 2
    groups = [[2 * pair + core for pair in range(pairs)] for core in range(2)]
    return lax.all_to_all(values, "dp", 0, 0, axis_index_groups=groups, tiled=True)


def everywhere_sum(values, bits):
    for bit in range(bits):
        values = values + across_dp(values, bit)
    offset = 1
    while offset < lax.axis_size("fsdp"):
        values = values + across_fsdp(values, offset)
        offset *= 2
    return values


def per_device(
    tokens,
    cotangent,
    doc_lengths,
    block_slot,
    matrices,
    vectors,
    vector_second,
    left_stat,
    right_stat,
    left_root,
    right_root,
):
    dp_count = lax.axis_size("dp")
    fsdp_count = lax.axis_size("fsdp")
    bits = dp_count.bit_length() - 1
    own_blocks, own_rows, width = matrices.shape
    blocks = own_blocks * dp_count
    height = width // dp_count
    me = lax.axis_index("dp").astype(jnp.int32).reshape(1)
    shard = lax.axis_index("fsdp").astype(jnp.int32).reshape(1)
    half = lax.axis_index("fsdp")
    half = sum((half >> bit) & 1 for bit in range(fsdp_count.bit_length())) % 2
    half = half.astype(jnp.int32).reshape(1)
    slot_place = block_slot % own_blocks * dp_count + block_slot // own_blocks
    gathered = lax.all_gather(matrices.astype(BF), ("dp", "fsdp"), axis=1, tiled=True)
    gathered = gathered.reshape(blocks, width, width)
    right_whole = lax.all_gather(right_root.astype(BF), "fsdp", axis=1, tiled=True)

    vec = vectors.reshape(-1, D)
    count = tokens.shape[0]
    rows_here, docs = doc_lengths.shape
    seq_len = count // rows_here
    steps = count // TILE

    def block_of(number):
        return (gathered, (1, width, width), lambda t, at, *_: (at[number(t)], 0, 0))

    qkv_in = [block_of(lambda t, u=u: u) for u in range(12)]
    out_in = [block_of(lambda t, u=u: 12 + u) for u in range(4)]

    normed1, projected = call(
        qkv_kernel,
        (steps,),
        [tokens_in(tokens), whole(vec)] + qkv_in,
        [
            ((count, D), BF, (TILE, D), lambda i, *_: (i, 0)),
            ((count, 3 * D), BF, (TILE, 3 * D), lambda i, *_: (i, 0)),
        ],
        [pltpu.VMEM((D, 3 * D), BF)],
        scalars=[slot_place],
        name="qkv",
    )

    pairs = HEADS // 2
    bias_rows = spans(seq_len)[1]

    def pair_in(array, row, offset):
        return (array, (seq_len, PAIR), lambda p, *_: (row, offset + p))

    attended, lses = [], []
    for row in range(rows_here):
        one, lse = call(
            functools.partial(attend_kernel, row=row, docs=docs),
            (pairs,),
            [pair_in(projected, row, part * pairs) for part in range(3)],
            [
                ((seq_len, D), BF, (seq_len, PAIR), lambda p, *_: (0, p)),
                ((pairs, 2, seq_len), F32, (1, 2, seq_len), lambda p, *_: (p, 0, 0)),
            ],
            [pltpu.VMEM((bias_rows, TILE), F32), pltpu.VMEM((PAIR, seq_len), F32)],
            scalars=[doc_lengths],
            name="attend",
        )
        attended.append(one)
        lses.append(lse)
    attended = attended[0] if rows_here == 1 else jnp.concatenate(attended, axis=0)

    middle, normed2, sums_mid = call(
        out_kernel,
        (steps,),
        [tokens_in(attended), tokens_in(tokens), whole(vec)] + out_in,
        [
            ((count, D), F32, (TILE, D), lambda i, *_: (i, 0)),
            ((count, D), BF, (TILE, D), lambda i, *_: (i, 0)),
            out_whole((8, D), F32),
        ],
        [pltpu.VMEM((D, D), BF)],
        scalars=[slot_place],
        name="attn_out",
    )

    ff_cols = FF // width
    pair_count = dp_count // 2
    tile_parts = ((0, FIRST_TILES), (FIRST_TILES, FF // D))
    held, fc_sums, mlp_grads = [], [], []
    for start, stop in tile_parts:
        tiles = stop - start
        fc_in = [
            block_of(lambda t, r=r, c=c, s=start: 16 + r * ff_cols + 2 * (t + s) + c)
            for r in range(2)
            for c in range(2)
        ]
        proj_in = [
            block_of(lambda t, r=r, c=c, s=start: 16 + 2 * ff_cols + 2 * (2 * (t + s) + r) + c)
            for r in range(2)
            for c in range(2)
        ]
        if start == 0:
            pieces = [
                (
                    (dp_count, tiles, 8, height, width),
                    BF,
                    (dp_count, 1, 8, height, width),
                    lambda t, *_: (0, t, 0, 0, 0),
                )
            ]
        else:
            pieces = [
                (
                    (pair_count, tiles * 8, height, width),
                    BF,
                    (pair_count, 8, height, width),
                    lambda t, *_: (0, t, 0, 0),
                )
            ] * 2
        mlp, back2, *grads, fc_sum = call(
            functools.partial(mlp_kernel, first=start, paired=start > 0),
            (tiles,),
            [whole(normed2), whole(cotangent), whole(vec)]
            + fc_in
            + proj_in
            + [whole(array) for array in held],
            [out_whole((count, D), F32), out_whole((count, D), F32)]
            + pieces
            + [((tiles, 1, D), F32, (1, 1, D), lambda t, *_: (t, 0, 0))],
            [pltpu.VMEM((D, D), BF)] * 4
            + [pltpu.VMEM((count, D), BF)] * 2
            + [pltpu.VMEM((D, D), F32)],
            scalars=[slot_place, me],
            ties=[right_whole] if start else [],
            name="mlp",
        )
        held = [mlp, back2]
        fc_sums.append(fc_sum)
        mlp_grads.append(grads)
    first_grads = lax.psum_scatter(
        mlp_grads[0][0].reshape(-1, width), "dp", scatter_dimension=0, tiled=True
    )

    output, grad_middle, grad_attended, *out_grads, sums_back = call(
        middle_kernel,
        (steps,),
        [
            tokens_in(middle),
            tokens_in(mlp),
            tokens_in(back2),
            tokens_in(cotangent),
            whole(attended),
            whole(vec),
        ]
        + out_in,
        [
            ((count, D), BF, (TILE, D), lambda i, *_: (i, 0)),
            ((count, D), F32, (TILE, D), lambda i, *_: (i, 0)),
            ((count, D), BF, (TILE, D), lambda i, *_: (i, 0)),
            out_whole((pair_count, 4, height, width), BF),
            out_whole((pair_count, 4, height, width), BF),
            out_whole((8, D), F32),
        ],
        [pltpu.VMEM((D, D), BF), pltpu.VMEM((count, D), BF), pltpu.VMEM((D, D), F32)],
        scalars=[slot_place, me],
        name="middle_back",
    )

    second_core = core_sum([mlp_grads[1], out_grads], "second_core")
    first_halves = plane_sum(first_grads.reshape(1, -1, height, width), half, [], "first_split")
    first_half = line_half(first_halves, [grad_attended], "first_half")
    second_parts = plane_parts(second_core)
    query_grads, key_grads, value_grads = [], [], []
    for row in range(rows_here):
        grads = call(
            functools.partial(attend_back_kernel, row=row, docs=docs),
            (pairs,),
            [pair_in(projected, row, part * pairs) for part in range(3)]
            + [
                pair_in(attended, row, 0),
                pair_in(grad_attended, row, 0),
                (lses[row], (1, 2, seq_len), lambda p, *_: (p, 0, 0)),
            ],
            [((seq_len, D), BF, (seq_len, PAIR), lambda p, *_: (0, p))] * 3,
            [
                pltpu.VMEM((bias_rows, TILE), F32),
                pltpu.VMEM((seq_len, PAIR), F32),
                pltpu.VMEM((seq_len, PAIR), F32),
                pltpu.VMEM((PAIR, seq_len), F32),
            ],
            scalars=[doc_lengths],
            ties=[second_core, first_halves[0]],
            name="attend_back",
        )
        for kept, one in zip((query_grads, key_grads, value_grads), grads):
            kept.append(one)
    dq, dk, dv = [
        kept[0] if rows_here == 1 else jnp.concatenate(kept, axis=0)
        for kept in (query_grads, key_grads, value_grads)
    ]

    half_shape = (pair_count, 12, height, width)
    keep, send, sums_qkv = call(
        weight_back_kernel,
        (3,),
        [whole(array) for array in (normed1, dq, dk, dv)],
        [(half_shape, BF, (pair_count, 4, height, width), lambda p, *_: (0, p, 0, 0))] * 2
        + [out_whole((8, D), F32)],
        [pltpu.VMEM((D, D), F32)],
        scalars=[me],
        ties=[first_half],
        name="qkv_weight_back",
    )
    first_total = line_rest(first_half, [keep], "first_rest")
    third_core = core_sum([(keep, send)], "third_core")
    second_halves = plane_sum(second_parts, half, [], "second_plane")
    third_parts = plane_parts(third_core)

    x_grad, sums_in = call(
        input_kernel,
        (steps,),
        [
            tokens_in(tokens),
            tokens_in(dq),
            tokens_in(dk),
            tokens_in(dv),
            tokens_in(grad_middle),
            whole(vec),
        ]
        + qkv_in,
        [((count, D), F32, (TILE, D), lambda i, *_: (i, 0)), out_whole((8, D), F32)],
        [pltpu.VMEM((D, 3 * D), BF)],
        scalars=[slot_place],
        ties=[second_halves[0], third_core, first_total],
        name="input_back",
    )

    second_half = line_half(second_halves, [x_grad], "second_half")
    second_total = line_rest(second_half, [], "second_rest")
    vector_local = call(
        pack_kernel,
        (1,),
        [whole(array) for array in (sums_in, sums_qkv, sums_back, sums_mid, *fc_sums)],
        [out_whole((16, D), F32)],
        name="pack",
    )[0]
    vector_sums = everywhere_sum(vector_local, bits)
    third_halves = plane_sum(third_parts, half, [second_half], "third_plane")
    third_total = line_rest(line_half(third_halves, [], "third_half"), [], "third_rest")
    vector_grad = vector_sums[:12].reshape(-1)
    square_sums = vector_sums[12, :4]

    order = []
    for tile in range(FF // D):
        order += [16 + r * ff_cols + 2 * tile + c for r in range(2) for c in range(2)]
        order += [16 + 2 * ff_cols + 2 * (2 * tile + r) + c for r in range(2) for c in range(2)]
    order += list(range(12, 16))
    order += [r * 6 + 2 * part + c for part in range(3) for r in range(2) for c in range(2)]
    numbers = jnp.arange(blocks, dtype=jnp.int32)
    standing = jnp.array([order.index(u) for u in range(blocks)], jnp.int32)
    source = jnp.sum(
        jnp.where(block_slot[None, :] == numbers[:, None], standing[None, :], 0), axis=1
    )
    begin = 0
    spread = []
    for total in (first_total, second_total, third_total):
        size = total.shape[0]
        inside = source - begin
        moved = begin + (inside // size ^ half[0]) * size + inside % size
        source = jnp.where((inside >= 0) & (inside < size * 2), moved, source)
        begin += size * 2
        spread += line_spread(total)
    laid = call(
        lay_kernel,
        (1,),
        [whole(array) for array in spread],
        [out_whole((dp_count, own_blocks, height, width), BF)],
        [pltpu.VMEM((blocks, height, width), BF)],
        scalars=[source],
        ties=[vector_sums],
        name="lay",
    )[0]
    grad_whole = lax.all_to_all(laid, "dp", 0, 0, tiled=True)

    def block_in(array):
        return (array, (1,) + array.shape[1:], lambda b, *_: (b, 0, 0))

    matrix_grad, left_new, right_new, matrix_new = call(
        factor_kernel,
        (own_blocks,),
        [(grad_whole, (dp_count, 1, height, width), lambda b, *_: (0, b, 0, 0))]
        + [block_in(a) for a in (right_whole, matrices, left_stat, right_stat, left_root)],
        [(matrices.shape, F32, (1, own_rows, width), lambda b, *_: (b, 0, 0))] * 4,
        [pltpu.VMEM((width, width), BF)] * 2,
        scalars=[shard],
        name="factor",
    )

    residual_scale = jnp.sqrt(square_sums / (count * dp_count * fsdp_count * D))
    second_new = DECAY * vector_second + (1.0 - DECAY) * vector_grad * vector_grad
    vector_new = vectors - VECTOR_RATE * vector_grad / (jnp.sqrt(second_new) + ROOT_EPSILON)
    return (
        output,
        x_grad,
        matrix_grad,
        left_new,
        right_new,
        matrix_new,
        vector_grad,
        second_new,
        vector_new,
        residual_scale,
    )


def solution(mesh):
    tokens = P(("dp", "fsdp"), None)
    stored = P("dp", "fsdp", None)
    return jax.shard_map(
        per_device,
        mesh=mesh,
        in_specs=(tokens, tokens, tokens, P(), stored, P(), P()) + (stored,) * 4,
        out_specs=(tokens, tokens) + (stored,) * 4 + (P(),) * 4,
        check_vma=False,
    )
```

```python
import functools

import jax
import jax.numpy as jnp
from jax import lax
from jax.experimental import pallas as pl
from jax.experimental.pallas import tpu as pltpu
from jax.sharding import PartitionSpec as P

D = 768
HEADS = 12
HEAD_DIM = 64
FF = 3072
LONGEST = 512

NORM_EPSILON = 1e-05
ROOT_EPSILON = 1e-08
DECAY = 0.5
MATRIX_RATE = 1.5
VECTOR_RATE = 0.1
MASKED = -1e30

BF = jnp.bfloat16
F32 = jnp.float32
PAIR = 2 * HEAD_DIM
TILE = 256
VMEM = 60 * 1024 * 1024
FIRST_TILES = 2

LN1_GAIN, LN1_SHIFT, Q_BIAS, V_BIAS, OUT_BIAS, LN2_GAIN, LN2_SHIFT, PROJ_BIAS, FC_BIAS = range(9)


def nn(left, right):
    return jnp.dot(left, right, preferred_element_type=F32)


def nt(left, right):
    return lax.dot_general(left, right, (((1,), (1,)), ((), ())), preferred_element_type=F32)


def tn(left, right):
    return lax.dot_general(left, right, (((0,), (0,)), ((), ())), preferred_element_type=F32)


def col_sum(values):
    return jnp.sum(values, axis=0, keepdims=True)


def norm_parts(values):
    center = values - jnp.mean(values, axis=-1, keepdims=True)
    spread = jnp.mean(center * center, axis=-1, keepdims=True)
    root = lax.rsqrt(spread + NORM_EPSILON)
    return center * root, root


def norm_back(unit, root, gain, grad):
    scaled = grad * gain
    return root * (
        scaled
        - jnp.mean(scaled, axis=-1, keepdims=True)
        - unit * jnp.mean(scaled * unit, axis=-1, keepdims=True)
    )


def place(weight, blocks, rows, cols):
    width = blocks[0].shape[-1]
    for row in range(rows):
        for col in range(cols):
            weight[row * width : (row + 1) * width, col * width : (col + 1) * width] = blocks[
                row * cols + col
            ][0]


def call(kernel, grid, ins, outs, scratch=(), scalars=(), ties=(), onto=(), name=None):
    first = len(scalars) + len(ins)
    ties = list(onto) + list(ties)

    def body(*refs):
        kernel(*refs[:first], *refs[first + len(ties) :])

    spec = pltpu.PrefetchScalarGridSpec(
        num_scalar_prefetch=len(scalars),
        grid=grid,
        in_specs=[pl.BlockSpec(block, index) for _, block, index in ins]
        + [pl.BlockSpec(memory_space=pl.ANY)] * len(ties),
        out_specs=[pl.BlockSpec(block, index) for _, _, block, index in outs],
        scratch_shapes=list(scratch),
    )
    return pl.pallas_call(
        body,
        grid_spec=spec,
        out_shape=[jax.ShapeDtypeStruct(shape, dtype) for shape, dtype, _, _ in outs],
        compiler_params=pltpu.CompilerParams(
            dimension_semantics=("arbitrary",) * len(grid), vmem_limit_bytes=VMEM
        ),
        cost_estimate=pl.CostEstimate(flops=1024, bytes_accessed=1024, transcendentals=0),
        input_output_aliases={first + place: place for place in range(len(onto))},
        name=name,
    )(*scalars, *[array for array, _, _ in ins], *ties)


def whole(array):
    return (array, array.shape, lambda *_: (0,) * array.ndim)


def tokens_in(array, cols=None):
    return (array, (TILE, cols or array.shape[1]), lambda i, *_: (i, 0))


def out_whole(shape, dtype):
    return (shape, dtype, shape, lambda *_: (0,) * len(shape))


def plane_sum_kernel(half_ref, *refs):
    half = len(refs) // 2
    for parts, out in zip(refs[:half], refs[half:]):
        total = parts[0].astype(F32)
        for part in range(1, parts.shape[0]):
            total = total + parts[part].astype(F32)
        out[...] = total.astype(BF)


def plane_sum(parts, half, ties, name):
    count, blocks, height, width = parts.shape
    size = blocks // 2

    def group(offset):
        return (parts, (count, size, height, width), lambda i, at: (0, at[0] ^ offset, 0, 0))

    return call(
        plane_sum_kernel,
        (1,),
        [group(0), group(1)],
        [out_whole((size, height, width), BF)] * 2,
        scalars=[half],
        ties=ties,
        name=name,
    )


def add_kernel(left_ref, right_ref, out_ref):
    out_ref[...] = (left_ref[...].astype(F32) + right_ref[...].astype(F32)).astype(BF)


def add_up(left, right, ties, name):
    return call(
        add_kernel,
        (1,),
        [whole(left), whole(right)],
        [out_whole(left.shape, BF)],
        ties=ties,
        name=name,
    )[0]


def line_half(halves, ties, name):
    return add_up(halves[0], across_fsdp(halves[1], 1), ties, name)


def line_rest(total, ties, name):
    offset = 3
    while offset <= lax.axis_size("fsdp"):
        total = add_up(total, across_fsdp(total, offset), ties, name)
        offset = 2 * offset - 1
    return total


def line_spread(total):
    return [total, across_fsdp(total, 1)]


def pack_kernel(in_ref, qkv_ref, back_ref, mid_ref, *refs):
    fc_refs, out_ref = refs[:-1], refs[-1]
    out_ref[0:2] = in_ref[0:2]
    out_ref[2:4] = qkv_ref[0:2]
    out_ref[4:5] = back_ref[4:5]
    out_ref[5:7] = back_ref[2:4]
    out_ref[7:8] = back_ref[5:6]
    row = 8
    for ref in fc_refs:
        for tile in range(ref.shape[0]):
            out_ref[row : row + 1] = ref[tile]
            row += 1
    lanes = lax.broadcasted_iota(jnp.int32, (1, D), 1)
    line = jnp.zeros((1, D), F32)
    for lane, value in enumerate((mid_ref[0:1], back_ref[0:1], mid_ref[1:2], back_ref[1:2])):
        line = jnp.where(lanes == lane, jnp.sum(value), line)
    out_ref[row : row + 1] = line
    out_ref[row + 1 :] = jnp.zeros_like(out_ref[row + 1 :])


def qkv_kernel(place_ref, x_ref, vec_ref, *refs):
    blocks, (normed_ref, projected_ref, weight) = refs[:12], refs[12:]

    @pl.when(pl.program_id(0) == 0)
    def _():
        place(weight, blocks, 2, 6)

    unit, _ = norm_parts(x_ref[...].astype(F32))
    normed = (unit * vec_ref[LN1_GAIN : LN1_GAIN + 1] + vec_ref[LN1_SHIFT : LN1_SHIFT + 1]).astype(
        BF
    )
    normed_ref[...] = normed
    for part in range(3):
        cols = slice(part * D, (part + 1) * D)
        value = nn(normed, weight[:, cols])
        if part != 1:
            row = Q_BIAS if part == 0 else V_BIAS
            value = value + vec_ref[row : row + 1]
        projected_ref[:, cols] = value.astype(BF)


def spans(seq_len):
    out = []
    start = 0
    for first in range(0, seq_len, TILE):
        low = max(0, first - LONGEST)
        out.append((first, low, first + TILE, start))
        start += first + TILE - low
    return out, start


def fill_bias(bias, lengths_ref, row, seq_len, docs):
    for first, low, high, start in spans(seq_len)[0]:
        place_q = lax.broadcasted_iota(jnp.int32, (1, TILE), 1) + first
        begin = jnp.zeros((1, TILE), jnp.int32)
        end = jnp.int32(0)
        for doc in range(docs):
            end = end + lengths_ref[row, doc]
            begin = jnp.where(place_q >= end, end, begin)
        place_k = lax.broadcasted_iota(jnp.int32, (high - low, TILE), 0) + low
        allowed = (place_k >= begin) & (place_k <= place_q)
        bias[start : start + high - low, :] = jnp.where(allowed, 0.0, MASKED)


def head_rows(values, head):
    rows = lax.broadcasted_iota(jnp.int32, values.shape, 0) // HEAD_DIM
    return jnp.where(rows == head, values, jnp.zeros_like(values))


def head_cols(values, head):
    cols = lax.broadcasted_iota(jnp.int32, values.shape, 1) // HEAD_DIM
    return jnp.where(cols == head, values, jnp.zeros_like(values))


def staged(bodies, stages, lags):
    held = [None] * len(bodies)
    for step in range(len(bodies) + sum(lags)):
        at = step
        for index, stage in enumerate(stages):
            if 0 <= at < len(bodies):
                held[at] = stage(*bodies[at]) if index == 0 else stage(held[at], *bodies[at])
            if index < len(lags):
                at -= lags[index]


def attend_kernel(lengths_ref, q_ref, k_ref, v_ref, out_ref, lse_ref, bias, mixed, *, row, docs):
    seq_len = q_ref.shape[0]

    @pl.when(pl.program_id(0) == 0)
    def _():
        fill_bias(bias, lengths_ref, row, seq_len, docs)

    query_t = (q_ref[...] * BF(HEAD_DIM**-0.5)).T
    value_t = v_ref[...].T
    query_h = [head_rows(query_t, head) for head in range(2)]

    def scores_of(head, first, low, high, start):
        cols = slice(first, first + TILE)
        scores = nn(k_ref[low:high, :], query_h[head][:, cols]) + bias[start : start + high - low, :]
        return scores, jnp.max(scores, axis=0, keepdims=True)

    def weights_of(held, head, first, low, high, start):
        scores, peak = held
        weights = jnp.exp(scores - peak)
        total = jnp.sum(weights, axis=0, keepdims=True)
        lse_ref[0, head : head + 1, first : first + TILE] = peak + jnp.log(total)
        return weights.astype(BF), 1.0 / total

    def mix(held, head, first, low, high, start):
        weights, scale = held
        rows = slice(head * HEAD_DIM, (head + 1) * HEAD_DIM)
        mixed[rows, first : first + TILE] = nn(value_t[rows, low:high], weights) * scale

    bodies = [(head,) + span for head in range(2) for span in spans(seq_len)[0]]
    staged(bodies, (scores_of, weights_of, mix), (2, 1))
    out_ref[...] = mixed[...].astype(BF).T


def attend_back_kernel(
    lengths_ref,
    q_ref,
    k_ref,
    v_ref,
    out_ref,
    grad_ref,
    lse_ref,
    dq_ref,
    dk_ref,
    dv_ref,
    bias,
    key_sum,
    value_sum,
    query_sum,
    *,
    row,
    docs,
):
    seq_len = q_ref.shape[0]

    @pl.when(pl.program_id(0) == 0)
    def _():
        fill_bias(bias, lengths_ref, row, seq_len, docs)

    query = q_ref[...] * BF(HEAD_DIM**-0.5)
    query_t = query.T
    key_t = k_ref[...].T
    grad = grad_ref[...]
    grad_t = grad.T
    weighted = grad_t.astype(F32) * out_ref[...].T.astype(F32)
    key_sum[...] = jnp.zeros_like(key_sum)
    value_sum[...] = jnp.zeros_like(value_sum)
    query_th = [head_rows(query_t, head) for head in range(2)]
    grad_th = [head_rows(grad_t, head) for head in range(2)]
    query_h = [head_cols(query, head) for head in range(2)]
    grad_h = [head_cols(grad, head) for head in range(2)]
    inner = [
        col_sum(weighted[head * HEAD_DIM : (head + 1) * HEAD_DIM, :]) for head in range(2)
    ]
    bodies = []
    for first, low, high, start in spans(seq_len)[0]:
        for head in range(2):
            for key in range(low, high, TILE):
                bodies.append((head, first, key, start + key - low, key == low))

    def products(head, first, key, start, opening):
        cols, rows = slice(first, first + TILE), slice(key, key + TILE)
        scores = nn(k_ref[rows, :], query_th[head][:, cols]) + bias[start : start + TILE, :]
        return scores, nn(v_ref[rows, :], grad_th[head][:, cols])

    def score_grads(held, head, first, key, start, opening):
        scores, grad_probs = held
        cols = slice(first, first + TILE)
        probs = jnp.exp(scores - lse_ref[0, head : head + 1, cols])
        return probs.astype(BF), (probs * (grad_probs - inner[head][:, cols])).astype(BF)

    def add_grads(held, head, first, key, start, opening):
        probs, grad_scores = held
        cols, rows = slice(first, first + TILE), slice(key, key + TILE)
        value_sum[rows, :] += nn(probs, grad_h[head][cols, :])
        key_sum[rows, :] += nn(grad_scores, query_h[head][cols, :])
        lanes = slice(head * HEAD_DIM, (head + 1) * HEAD_DIM)
        part = nn(key_t[lanes, rows], grad_scores)
        if opening:
            query_sum[lanes, cols] = part
        else:
            query_sum[lanes, cols] += part

    staged(bodies, (products, score_grads, add_grads), (2, 1))
    dq_ref[...] = (query_sum[...] * (HEAD_DIM**-0.5)).astype(BF).T
    dk_ref[...] = key_sum[...].astype(BF)
    dv_ref[...] = value_sum[...].astype(BF)


def out_kernel(place_ref, att_ref, x_ref, vec_ref, *refs):
    blocks, (middle_ref, normed_ref, sums_ref, weight) = refs[:4], refs[4:]

    @pl.when(pl.program_id(0) == 0)
    def _():
        place(weight, blocks, 2, 2)
        sums_ref[...] = jnp.zeros_like(sums_ref)

    branch = nn(att_ref[...], weight[...]) + vec_ref[OUT_BIAS : OUT_BIAS + 1]
    middle = x_ref[...].astype(F32) + branch
    middle_ref[...] = middle
    unit, _ = norm_parts(middle)
    normed_ref[...] = (
        unit * vec_ref[LN2_GAIN : LN2_GAIN + 1] + vec_ref[LN2_SHIFT : LN2_SHIFT + 1]
    ).astype(BF)
    sums_ref[0:1] += col_sum(middle * middle)
    sums_ref[1:2] += col_sum(branch * branch)


def put_pieces(keep_ref, send_ref, grad, core, base):
    height, width = keep_ref.shape[-2:]
    for held, ref in enumerate((keep_ref, send_ref)):
        for pair in range(ref.shape[0]):
            piece = 2 * pair + (core ^ held)
            for row in range(2):
                top = pl.multiple_of(row * width + piece * height, 8)
                for col in range(2):
                    ref[pair, base + 2 * row + col] = grad[
                        pl.ds(top, height), col * width : (col + 1) * width
                    ].astype(BF)


def mlp_kernel(place_ref, me_ref, normed_ref, cot_ref, vec_ref, *refs, first, paired):
    fc_blocks, proj_blocks, refs = refs[:4], refs[4:8], refs[8:]
    if first == 0:
        before = None
    else:
        before, refs = refs[:2], refs[2:]
    if paired:
        mlp_ref, back_ref, keep_ref, send_ref, bias_ref = refs[:5]
        refs = refs[5:]
    else:
        mlp_ref, back_ref, grad_ref, bias_ref = refs[:4]
        refs = refs[4:]
    w_fc, w_proj, hidden, grad_pre, whole_grad = refs
    step = pl.program_id(0)
    place(w_fc, fc_blocks, 2, 2)
    place(w_proj, proj_blocks, 2, 2)
    bias_row = vec_ref[pl.ds(FC_BIAS + first + step, 1)]

    @pl.when(step == 0)
    def _():
        if first == 0:
            mlp_ref[...] = jnp.zeros_like(mlp_ref)
            back_ref[...] = jnp.zeros_like(back_ref)
        else:
            mlp_ref[...] = before[0][...]
            back_ref[...] = before[1][...]

    def entering(rows):
        return nn(normed_ref[rows], w_fc[...]) + bias_row, nt(cot_ref[rows], w_proj[...])

    def activated(held, rows):
        pre, grad = held
        root = 0.7978845608028654
        square = pre * pre
        tanh = jnp.tanh(pre * (root + root * 0.044715 * square))
        half = 0.5 + 0.5 * tanh
        low = (pre * half).astype(BF)
        slope = half + (0.5 * pre) * (1.0 - tanh * tanh) * (root + root * 3.0 * 0.044715 * square)
        back = (grad * slope).astype(BF)
        hidden[rows] = low
        grad_pre[rows] = back
        mlp_ref[rows] += nn(low, w_proj[...])
        back_ref[rows] += nt(back, w_fc[...])
        sums.append(col_sum(back.astype(F32)))

    sums = []
    count = normed_ref.shape[0]
    staged(
        [(slice(row, row + TILE),) for row in range(0, count, TILE)], (entering, activated), (1,)
    )
    bias_ref[0] = sum(sums)
    for base, left, right in ((0, normed_ref, grad_pre), (4, hidden, cot_ref)):
        if paired:
            whole_grad[...] = tn(left[...], right[...])
            put_pieces(keep_ref, send_ref, whole_grad, me_ref[0] % 2, base)
        else:
            pieces, _, _, height, width = grad_ref.shape
            grad = tn(left[...], right[...]).astype(BF)
            for row in range(2):
                for col in range(2):
                    for piece in range(pieces):
                        top = row * width + piece * height
                        grad_ref[piece, 0, base + 2 * row + col] = grad[
                            top : top + height, col * width : (col + 1) * width
                        ]


def middle_kernel(
    place_ref,
    me_ref,
    middle_ref,
    mlp_ref,
    back_ref,
    cot_ref,
    att_ref,
    vec_ref,
    *refs,
):
    blocks, refs = refs[:4], refs[4:]
    output_ref, grad_ref, grad_att_ref, keep_ref, send_ref, sums_ref, weight, branch, out_grad = refs
    step = pl.program_id(0)

    @pl.when(step == 0)
    def _():
        place(weight, blocks, 2, 2)
        sums_ref[...] = jnp.zeros_like(sums_ref)

    middle = middle_ref[...]
    mlp = mlp_ref[...] + vec_ref[PROJ_BIAS : PROJ_BIAS + 1]
    result = middle + mlp
    output_ref[...] = result.astype(BF)
    cot = cot_ref[...].astype(F32)
    unit, root = norm_parts(middle)
    back = back_ref[...]
    grad = cot + norm_back(unit, root, vec_ref[LN2_GAIN : LN2_GAIN + 1], back)
    grad_ref[...] = grad
    low = grad.astype(BF)
    branch[pl.ds(pl.multiple_of(step * TILE, TILE), TILE)] = low
    grad_att_ref[...] = nt(low, weight[...]).astype(BF)
    sums_ref[0:1] += col_sum(result * result)
    sums_ref[1:2] += col_sum(mlp * mlp)
    sums_ref[2:3] += col_sum(back * unit)
    sums_ref[3:4] += col_sum(back)
    sums_ref[4:5] += col_sum(low.astype(F32))
    sums_ref[5:6] += col_sum(cot)

    @pl.when(step == pl.num_programs(0) - 1)
    def _():
        out_grad[...] = tn(att_ref[...], branch[...])
        put_pieces(keep_ref, send_ref, out_grad, me_ref[0] % 2, 0)


def weight_back_kernel(
    me_ref, normed_ref, dq_ref, dk_ref, dv_ref, keep_ref, send_ref, sums_ref, grad
):
    step = pl.program_id(0)

    @pl.when(step == 0)
    def _():
        sums_ref[0:1] = col_sum(dq_ref[...].astype(F32))
        sums_ref[1:2] = col_sum(dv_ref[...].astype(F32))

    for part, ref in enumerate((dq_ref, dk_ref, dv_ref)):

        @pl.when(step == part)
        def _():
            grad[...] = tn(normed_ref[...], ref[...])

    put_pieces(keep_ref, send_ref, grad, me_ref[0] % 2, 0)


def input_kernel(place_ref, x_ref, dq_ref, dk_ref, dv_ref, grad_ref, vec_ref, *refs):
    blocks, (out_ref, sums_ref, weight) = refs[:12], refs[12:]

    @pl.when(pl.program_id(0) == 0)
    def _():
        place(weight, blocks, 2, 6)
        sums_ref[...] = jnp.zeros_like(sums_ref)

    back = nt(dq_ref[...], weight[:, :D])
    back += nt(dk_ref[...], weight[:, D : 2 * D])
    back += nt(dv_ref[...], weight[:, 2 * D :])
    unit, root = norm_parts(x_ref[...].astype(F32))
    out_ref[...] = grad_ref[...] + norm_back(unit, root, vec_ref[LN1_GAIN : LN1_GAIN + 1], back)
    sums_ref[0:1] += col_sum(back * unit)
    sums_ref[1:2] += col_sum(back)


def lay_kernel(source_ref, *refs):
    out_ref, pieces = refs[-2:]
    begin = 0
    for ref in refs[:-2]:
        pieces[begin : begin + ref.shape[0]] = ref[...]
        begin += ref.shape[0]
    shards, own = out_ref.shape[:2]
    for shard in range(shards):
        for slot in range(own):
            out_ref[shard, slot] = pieces[source_ref[shard * own + slot]]


def factor_kernel(
    shard_ref,
    grad_ref,
    right_ref,
    matrix_ref,
    left_stat_ref,
    right_stat_ref,
    left_root_ref,
    rows_ref,
    left_ref,
    right_new_ref,
    matrix_new_ref,
    whole_grad,
    grad_t,
):
    rows = matrix_ref.shape[1]
    pieces, _, height, _ = grad_ref.shape
    for piece in range(pieces):
        whole_grad[piece * height : (piece + 1) * height, :] = grad_ref[piece, 0]
    grad = whole_grad[...]
    grad_t[...] = grad.T
    own = pl.ds(pl.multiple_of(shard_ref[0] * rows, rows), rows)
    grad_rows = whole_grad[own, :]
    rows_ref[0] = grad_rows.astype(F32)
    left_ref[0] = DECAY * left_stat_ref[0] + (1.0 - DECAY) * nn(grad_rows, grad_t[...])
    right_new_ref[0] = DECAY * right_stat_ref[0] + (1.0 - DECAY) * nn(grad_t[own, :], grad)
    half = nn(left_root_ref[0].astype(BF), grad)
    update = nn(half.astype(BF), right_ref[0])
    matrix_new_ref[0] = matrix_ref[0] - MATRIX_RATE * update


def core_sum_kernel(*refs):
    out_ref = refs[-1]
    begin = 0
    for keep, sent in zip(refs[:-1:2], refs[1:-1:2]):
        blocks = keep.shape[1]
        out_ref[0, begin : begin + blocks] = (keep[0].astype(F32) + sent[0].astype(F32)).astype(BF)
        begin += blocks


def across_dp(values, bit):
    count = lax.axis_size("dp")
    return lax.ppermute(values, "dp", [(i, i ^ (1 << bit)) for i in range(count)])


def across_fsdp(values, offset):
    count = lax.axis_size("fsdp")
    return lax.ppermute(values, "fsdp", [(i, i ^ offset) for i in range(count)])


def core_sum(grads, name, ties=()):
    ins = []
    for keep, send in grads:
        ins += [keep, across_dp(send, 0)]
    pairs = ins[0].shape[0]
    rest = ins[0].shape[2:]
    blocks = sum(keep.shape[1] for keep, _ in grads)

    def one(array):
        return (array, (1,) + array.shape[1:], lambda i: (i, 0, 0, 0))

    return call(
        core_sum_kernel,
        (pairs,),
        [one(array) for array in ins],
        [((pairs, blocks) + rest, BF, (1, blocks) + rest, lambda i: (i, 0, 0, 0))],
        ties=ties,
        name=name,
    )[0]


def plane_parts(values):
    pairs = lax.axis_size("dp") // 2
    groups = [[2 * pair + core for pair in range(pairs)] for core in range(2)]
    return lax.all_to_all(values, "dp", 0, 0, axis_index_groups=groups, tiled=True)


def dp_sum(values):
    for bit in range(lax.axis_size("dp").bit_length() - 1):
        values = values + across_dp(values, bit)
    return values


def fsdp_sum(values):
    offset = 1
    while offset < lax.axis_size("fsdp"):
        values = values + across_fsdp(values, offset)
        offset *= 2
    return values


def per_device(
    tokens,
    cotangent,
    doc_lengths,
    block_slot,
    matrices,
    vectors,
    vector_second,
    left_stat,
    right_stat,
    left_root,
    right_root,
):
    dp_count = lax.axis_size("dp")
    fsdp_count = lax.axis_size("fsdp")
    own_blocks, own_rows, width = matrices.shape
    blocks = own_blocks * dp_count
    height = width // dp_count
    me = lax.axis_index("dp").astype(jnp.int32).reshape(1)
    shard = lax.axis_index("fsdp").astype(jnp.int32).reshape(1)
    half = lax.axis_index("fsdp")
    half = sum((half >> bit) & 1 for bit in range(fsdp_count.bit_length())) % 2
    half = half.astype(jnp.int32).reshape(1)
    slot_place = block_slot % own_blocks * dp_count + block_slot // own_blocks
    gathered = lax.all_gather(matrices.astype(BF), ("dp", "fsdp"), axis=1, tiled=True)
    gathered = gathered.reshape(blocks, width, width)
    right_whole = lax.all_gather(right_root.astype(BF), "fsdp", axis=1, tiled=True)

    vec = vectors.reshape(-1, D)
    count = tokens.shape[0]
    rows_here, docs = doc_lengths.shape
    seq_len = count // rows_here
    steps = count // TILE

    def block_of(number):
        return (gathered, (1, width, width), lambda t, at, *_: (at[number(t)], 0, 0))

    qkv_in = [block_of(lambda t, u=u: u) for u in range(12)]
    out_in = [block_of(lambda t, u=u: 12 + u) for u in range(4)]

    normed1, projected = call(
        qkv_kernel,
        (steps,),
        [tokens_in(tokens), whole(vec)] + qkv_in,
        [
            ((count, D), BF, (TILE, D), lambda i, *_: (i, 0)),
            ((count, 3 * D), BF, (TILE, 3 * D), lambda i, *_: (i, 0)),
        ],
        [pltpu.VMEM((D, 3 * D), BF)],
        scalars=[slot_place],
        name="qkv",
    )

    pairs = HEADS // 2
    bias_rows = spans(seq_len)[1]

    def pair_in(array, row, offset):
        return (array, (seq_len, PAIR), lambda p, *_: (row, offset + p))

    attended, lses = [], []
    for row in range(rows_here):
        one, lse = call(
            functools.partial(attend_kernel, row=row, docs=docs),
            (pairs,),
            [pair_in(projected, row, part * pairs) for part in range(3)],
            [
                ((seq_len, D), BF, (seq_len, PAIR), lambda p, *_: (0, p)),
                ((pairs, 2, seq_len), F32, (1, 2, seq_len), lambda p, *_: (p, 0, 0)),
            ],
            [pltpu.VMEM((bias_rows, TILE), F32), pltpu.VMEM((PAIR, seq_len), F32)],
            scalars=[doc_lengths],
            name="attend",
        )
        attended.append(one)
        lses.append(lse)
    attended = attended[0] if rows_here == 1 else jnp.concatenate(attended, axis=0)

    middle, normed2, sums_mid = call(
        out_kernel,
        (steps,),
        [tokens_in(attended), tokens_in(tokens), whole(vec)] + out_in,
        [
            ((count, D), F32, (TILE, D), lambda i, *_: (i, 0)),
            ((count, D), BF, (TILE, D), lambda i, *_: (i, 0)),
            out_whole((8, D), F32),
        ],
        [pltpu.VMEM((D, D), BF)],
        scalars=[slot_place],
        name="attn_out",
    )

    ff_cols = FF // width
    pair_count = dp_count // 2
    tile_parts = ((0, FIRST_TILES), (FIRST_TILES, FF // D))
    held, fc_sums, mlp_grads = [], [], []
    for start, stop in tile_parts:
        tiles = stop - start
        fc_in = [
            block_of(lambda t, r=r, c=c, s=start: 16 + r * ff_cols + 2 * (t + s) + c)
            for r in range(2)
            for c in range(2)
        ]
        proj_in = [
            block_of(lambda t, r=r, c=c, s=start: 16 + 2 * ff_cols + 2 * (2 * (t + s) + r) + c)
            for r in range(2)
            for c in range(2)
        ]
        if start == 0:
            pieces = [
                (
                    (dp_count, tiles, 8, height, width),
                    BF,
                    (dp_count, 1, 8, height, width),
                    lambda t, *_: (0, t, 0, 0, 0),
                )
            ]
        else:
            pieces = [
                (
                    (pair_count, tiles * 8, height, width),
                    BF,
                    (pair_count, 8, height, width),
                    lambda t, *_: (0, t, 0, 0),
                )
            ] * 2
        mlp, back2, *grads, fc_sum = call(
            functools.partial(mlp_kernel, first=start, paired=start > 0),
            (tiles,),
            [whole(normed2), whole(cotangent), whole(vec)]
            + fc_in
            + proj_in
            + [whole(array) for array in held],
            [out_whole((count, D), F32), out_whole((count, D), F32)]
            + pieces
            + [((tiles, 1, D), F32, (1, 1, D), lambda t, *_: (t, 0, 0))],
            [pltpu.VMEM((D, D), BF)] * 2
            + [pltpu.VMEM((count, D), BF)] * 2
            + [pltpu.VMEM((D, D), F32)],
            scalars=[slot_place, me],
            ties=[right_whole] if start else [],
            name="mlp",
        )
        held = [mlp, back2]
        fc_sums.append(fc_sum)
        mlp_grads.append(grads)
    first_grads = lax.psum_scatter(
        mlp_grads[0][0].reshape(-1, width), "dp", scatter_dimension=0, tiled=True
    )

    output, grad_middle, grad_attended, *out_grads, sums_back = call(
        middle_kernel,
        (steps,),
        [
            tokens_in(middle),
            tokens_in(mlp),
            tokens_in(back2),
            tokens_in(cotangent),
            whole(attended),
            whole(vec),
        ]
        + out_in,
        [
            ((count, D), BF, (TILE, D), lambda i, *_: (i, 0)),
            ((count, D), F32, (TILE, D), lambda i, *_: (i, 0)),
            ((count, D), BF, (TILE, D), lambda i, *_: (i, 0)),
            out_whole((pair_count, 4, height, width), BF),
            out_whole((pair_count, 4, height, width), BF),
            out_whole((8, D), F32),
        ],
        [pltpu.VMEM((D, D), BF), pltpu.VMEM((count, D), BF), pltpu.VMEM((D, D), F32)],
        scalars=[slot_place, me],
        name="middle_back",
    )

    second_core = core_sum([mlp_grads[1], out_grads], "second_core")
    first_halves = plane_sum(first_grads.reshape(1, -1, height, width), half, [], "first_split")
    first_half = line_half(first_halves, [], "first_half")
    second_parts = plane_parts(second_core)
    def attend_back(row, begin, stop, onto, ties):
        return call(
            functools.partial(attend_back_kernel, row=row, docs=docs),
            (stop - begin,),
            [pair_in(projected, row, part * pairs + begin) for part in range(3)]
            + [
                pair_in(attended, row, begin),
                pair_in(grad_attended, row, begin),
                (lses[row], (1, 2, seq_len), lambda p, *_: (p + begin, 0, 0)),
            ],
            [((count, D), BF, (seq_len, PAIR), lambda p, *_: (row, p + begin))] * 3,
            [
                pltpu.VMEM((bias_rows, TILE), F32),
                pltpu.VMEM((seq_len, PAIR), F32),
                pltpu.VMEM((seq_len, PAIR), F32),
                pltpu.VMEM((PAIR, seq_len), F32),
            ],
            scalars=[doc_lengths],
            ties=ties,
            onto=onto,
            name="attend_back",
        )

    grads = ()
    for row in range(rows_here):
        grads = attend_back(row, 0, pairs // 2, grads, [second_core])
        grads = attend_back(row, pairs // 2, pairs, grads, [first_halves[0]])
    dq, dk, dv = grads

    half_shape = (pair_count, 12, height, width)
    keep, send, sums_qkv = call(
        weight_back_kernel,
        (3,),
        [whole(array) for array in (normed1, dq, dk, dv)],
        [(half_shape, BF, (pair_count, 4, height, width), lambda p, *_: (0, p, 0, 0))] * 2
        + [out_whole((8, D), F32)],
        [pltpu.VMEM((D, D), F32)],
        scalars=[me],
        ties=[first_half],
        name="qkv_weight_back",
    )
    third_core = core_sum([(keep, send)], "third_core")
    second_halves = plane_sum(second_parts, half, [], "second_plane")
    third_parts = plane_parts(third_core)

    x_grad, sums_in = call(
        input_kernel,
        (steps,),
        [
            tokens_in(tokens),
            tokens_in(dq),
            tokens_in(dk),
            tokens_in(dv),
            tokens_in(grad_middle),
            whole(vec),
        ]
        + qkv_in,
        [((count, D), F32, (TILE, D), lambda i, *_: (i, 0)), out_whole((8, D), F32)],
        [pltpu.VMEM((D, 3 * D), BF)],
        scalars=[slot_place],
        ties=[second_halves[0], third_core],
        name="input_back",
    )

    first_total = line_rest(first_half, [x_grad], "first_rest")
    second_half = line_half(second_halves, [x_grad, first_total], "second_half")
    second_total = line_rest(second_half, [], "second_rest")
    vector_local = call(
        pack_kernel,
        (1,),
        [whole(array) for array in (sums_in, sums_qkv, sums_back, sums_mid, *fc_sums)],
        [out_whole((16, D), F32)],
        name="pack",
    )[0]
    vector_plane = dp_sum(vector_local)
    vector_sums = fsdp_sum(vector_plane)
    third_halves = plane_sum(third_parts, half, [second_half], "third_plane")
    third_total = line_rest(line_half(third_halves, [], "third_half"), [], "third_rest")
    vector_grad = vector_sums[:12].reshape(-1)
    square_sums = vector_sums[12, :4]

    order = []
    for tile in range(FF // D):
        order += [16 + r * ff_cols + 2 * tile + c for r in range(2) for c in range(2)]
        order += [16 + 2 * ff_cols + 2 * (2 * tile + r) + c for r in range(2) for c in range(2)]
    order += list(range(12, 16))
    order += [r * 6 + 2 * part + c for part in range(3) for r in range(2) for c in range(2)]
    numbers = jnp.arange(blocks, dtype=jnp.int32)
    standing = jnp.array([order.index(u) for u in range(blocks)], jnp.int32)
    source = jnp.sum(
        jnp.where(block_slot[None, :] == numbers[:, None], standing[None, :], 0), axis=1
    )
    begin = 0
    spread = []
    for total in (first_total, second_total, third_total):
        size = total.shape[0]
        inside = source - begin
        moved = begin + (inside // size ^ half[0]) * size + inside % size
        source = jnp.where((inside >= 0) & (inside < size * 2), moved, source)
        begin += size * 2
        spread += line_spread(total)
    laid = call(
        lay_kernel,
        (1,),
        [whole(array) for array in spread],
        [out_whole((dp_count, own_blocks, height, width), BF)],
        [pltpu.VMEM((blocks, height, width), BF)],
        scalars=[source],
        ties=[vector_plane],
        name="lay",
    )[0]
    grad_whole = lax.all_to_all(laid, "dp", 0, 0, tiled=True)

    def block_in(array):
        return (array, (1,) + array.shape[1:], lambda b, *_: (b, 0, 0))

    matrix_grad, left_new, right_new, matrix_new = call(
        factor_kernel,
        (own_blocks,),
        [(grad_whole, (dp_count, 1, height, width), lambda b, *_: (0, b, 0, 0))]
        + [block_in(a) for a in (right_whole, matrices, left_stat, right_stat, left_root)],
        [(matrices.shape, F32, (1, own_rows, width), lambda b, *_: (b, 0, 0))] * 4,
        [pltpu.VMEM((width, width), BF)] * 2,
        scalars=[shard],
        name="factor",
    )

    residual_scale = jnp.sqrt(square_sums / (count * dp_count * fsdp_count * D))
    second_new = DECAY * vector_second + (1.0 - DECAY) * vector_grad * vector_grad
    vector_new = vectors - VECTOR_RATE * vector_grad / (jnp.sqrt(second_new) + ROOT_EPSILON)
    return (
        output,
        x_grad,
        matrix_grad,
        left_new,
        right_new,
        matrix_new,
        vector_grad,
        second_new,
        vector_new,
        residual_scale,
    )


def solution(mesh):
    tokens = P(("dp", "fsdp"), None)
    stored = P("dp", "fsdp", None)
    return jax.shard_map(
        per_device,
        mesh=mesh,
        in_specs=(tokens, tokens, tokens, P(), stored, P(), P()) + (stored,) * 4,
        out_specs=(tokens, tokens) + (stored,) * 4 + (P(),) * 4,
        check_vma=False,
    )
```

```python
import functools

import jax
import jax.numpy as jnp
from jax import lax
from jax.experimental import pallas as pl
from jax.experimental.pallas import tpu as pltpu
from jax.sharding import PartitionSpec as P

D = 768
HEADS = 12
HEAD_DIM = 64
FF = 3072
LONGEST = 512

NORM_EPSILON = 1e-05
ROOT_EPSILON = 1e-08
DECAY = 0.5
MATRIX_RATE = 1.5
VECTOR_RATE = 0.1
MASKED = -1e30

BF = jnp.bfloat16
F32 = jnp.float32
PAIR = 2 * HEAD_DIM
TILE = 256
VMEM = 60 * 1024 * 1024
FIRST_TILES = 2

LN1_GAIN, LN1_SHIFT, Q_BIAS, V_BIAS, OUT_BIAS, LN2_GAIN, LN2_SHIFT, PROJ_BIAS, FC_BIAS = range(9)


def nn(left, right):
    return jnp.dot(left, right, preferred_element_type=F32)


def nt(left, right):
    return lax.dot_general(left, right, (((1,), (1,)), ((), ())), preferred_element_type=F32)


def tn(left, right):
    return lax.dot_general(left, right, (((0,), (0,)), ((), ())), preferred_element_type=F32)


def col_sum(values):
    return jnp.sum(values, axis=0, keepdims=True)


def norm_parts(values):
    center = values - jnp.mean(values, axis=-1, keepdims=True)
    spread = jnp.mean(center * center, axis=-1, keepdims=True)
    root = lax.rsqrt(spread + NORM_EPSILON)
    return center * root, root


def norm_back(unit, root, gain, grad):
    scaled = grad * gain
    return root * (
        scaled
        - jnp.mean(scaled, axis=-1, keepdims=True)
        - unit * jnp.mean(scaled * unit, axis=-1, keepdims=True)
    )


def start_fill(weight, table_ref, sources, sem, blocks):
    _, height, width = sources[0].shape
    units = width // height
    half = table_ref.shape[0] // 2
    for number, row, col in blocks:
        for unit in range(units):
            at = number * units + unit
            source, index = table_ref[at], table_ref[half + at]
            top = row * width + unit * height
            target = weight.at[pl.ds(top, height), pl.ds(col * width, width)]
            for which, ref in enumerate(sources):

                @pl.when(source == which)
                def _():
                    pltpu.make_async_copy(ref.at[index], target, sem).start()


def wait_fill(weight, sem):
    pltpu.make_async_copy(weight, weight, sem).wait()


def fill(weight, table_ref, sources, sem, blocks):
    start_fill(weight, table_ref, sources, sem, blocks)
    wait_fill(weight, sem)


QKV_BLOCKS = [(row * 6 + col, row, col) for row in range(2) for col in range(6)]
OUT_BLOCKS = [(12 + row * 2 + col, row, col) for row in range(2) for col in range(2)]
SOURCES = 5


def call(kernel, grid, ins, outs, scratch=(), scalars=(), ties=(), onto=(), name=None):
    first = len(scalars) + len(ins)
    ties = list(onto) + list(ties)

    def body(*refs):
        kernel(*refs[:first], *refs[first + len(ties) :])

    spec = pltpu.PrefetchScalarGridSpec(
        num_scalar_prefetch=len(scalars),
        grid=grid,
        in_specs=[
            pl.BlockSpec(memory_space=pltpu.HBM) if block is None else pl.BlockSpec(block, index)
            for _, block, index in ins
        ]
        + [pl.BlockSpec(memory_space=pl.ANY)] * len(ties),
        out_specs=[pl.BlockSpec(block, index) for _, _, block, index in outs],
        scratch_shapes=list(scratch),
    )
    return pl.pallas_call(
        body,
        grid_spec=spec,
        out_shape=[jax.ShapeDtypeStruct(shape, dtype) for shape, dtype, _, _ in outs],
        compiler_params=pltpu.CompilerParams(
            dimension_semantics=("arbitrary",) * len(grid), vmem_limit_bytes=VMEM
        ),
        cost_estimate=pl.CostEstimate(flops=1024, bytes_accessed=1024, transcendentals=0),
        input_output_aliases={first + place: place for place in range(len(onto))},
        name=name,
    )(*scalars, *[array for array, _, _ in ins], *ties)


def whole(array):
    return (array, array.shape, lambda *_: (0,) * array.ndim)


def tokens_in(array, cols=None):
    return (array, (TILE, cols or array.shape[1]), lambda i, *_: (i, 0))


def out_whole(shape, dtype):
    return (shape, dtype, shape, lambda *_: (0,) * len(shape))


def plane_sum_kernel(half_ref, *refs):
    half = len(refs) // 2
    for parts, out in zip(refs[:half], refs[half:]):
        total = parts[0].astype(F32)
        for part in range(1, parts.shape[0]):
            total = total + parts[part].astype(F32)
        out[...] = total.astype(BF)


def plane_sum(parts, half, ties, name):
    count, blocks, height, width = parts.shape
    size = blocks // 2

    def group(offset):
        return (parts, (count, size, height, width), lambda i, at: (0, at[0] ^ offset, 0, 0))

    return call(
        plane_sum_kernel,
        (1,),
        [group(0), group(1)],
        [out_whole((size, height, width), BF)] * 2,
        scalars=[half],
        ties=ties,
        name=name,
    )


def add_kernel(left_ref, right_ref, out_ref):
    out_ref[...] = (left_ref[...].astype(F32) + right_ref[...].astype(F32)).astype(BF)


def add_up(left, right, ties, name):
    return call(
        add_kernel,
        (1,),
        [whole(left), whole(right)],
        [out_whole(left.shape, BF)],
        ties=ties,
        name=name,
    )[0]


def line_half(halves, ties, name):
    return add_up(halves[0], across_fsdp(halves[1], 1), ties, name)


def line_rest(total, ties, name):
    offset = 3
    while offset <= lax.axis_size("fsdp"):
        total = add_up(total, across_fsdp(total, offset), ties, name)
        offset = 2 * offset - 1
    return total


def line_spread(total):
    return [total, across_fsdp(total, 1)]


def pack_kernel(in_ref, qkv_ref, back_ref, mid_ref, *refs):
    fc_refs, out_ref = refs[:-1], refs[-1]
    out_ref[0:2] = in_ref[0:2]
    out_ref[2:4] = qkv_ref[0:2]
    out_ref[4:5] = back_ref[4:5]
    out_ref[5:7] = back_ref[2:4]
    out_ref[7:8] = back_ref[5:6]
    row = 8
    for ref in fc_refs:
        for tile in range(ref.shape[0]):
            out_ref[row : row + 1] = ref[tile]
            row += 1
    lanes = lax.broadcasted_iota(jnp.int32, (1, D), 1)
    line = jnp.zeros((1, D), F32)
    for lane, value in enumerate((mid_ref[0:1], back_ref[0:1], mid_ref[1:2], back_ref[1:2])):
        line = jnp.where(lanes == lane, jnp.sum(value), line)
    out_ref[row : row + 1] = line
    out_ref[row + 1 :] = jnp.zeros_like(out_ref[row + 1 :])


def qkv_kernel(table_ref, x_ref, vec_ref, *refs):
    sources, (normed_ref, projected_ref, weight, sem) = refs[:SOURCES], refs[SOURCES:]

    @pl.when(pl.program_id(0) == 0)
    def _():
        fill(weight, table_ref, sources, sem, QKV_BLOCKS)

    unit, _ = norm_parts(x_ref[...].astype(F32))
    normed = (unit * vec_ref[LN1_GAIN : LN1_GAIN + 1] + vec_ref[LN1_SHIFT : LN1_SHIFT + 1]).astype(
        BF
    )
    normed_ref[...] = normed
    for part in range(3):
        cols = slice(part * D, (part + 1) * D)
        value = nn(normed, weight[:, cols])
        if part != 1:
            row = Q_BIAS if part == 0 else V_BIAS
            value = value + vec_ref[row : row + 1]
        projected_ref[:, cols] = value.astype(BF)


def spans(seq_len):
    out = []
    start = 0
    for first in range(0, seq_len, TILE):
        low = max(0, first - LONGEST)
        out.append((first, low, first + TILE, start))
        start += first + TILE - low
    return out, start


def fill_bias(bias, lengths_ref, row, seq_len, docs):
    for first, low, high, start in spans(seq_len)[0]:
        place_q = lax.broadcasted_iota(jnp.int32, (1, TILE), 1) + first
        begin = jnp.zeros((1, TILE), jnp.int32)
        end = jnp.int32(0)
        for doc in range(docs):
            end = end + lengths_ref[row, doc]
            begin = jnp.where(place_q >= end, end, begin)
        place_k = lax.broadcasted_iota(jnp.int32, (high - low, TILE), 0) + low
        allowed = (place_k >= begin) & (place_k <= place_q)
        bias[start : start + high - low, :] = jnp.where(allowed, 0.0, MASKED)


def head_rows(values, head):
    rows = lax.broadcasted_iota(jnp.int32, values.shape, 0) // HEAD_DIM
    return jnp.where(rows == head, values, jnp.zeros_like(values))


def head_cols(values, head):
    cols = lax.broadcasted_iota(jnp.int32, values.shape, 1) // HEAD_DIM
    return jnp.where(cols == head, values, jnp.zeros_like(values))


def staged(bodies, stages, lags):
    held = [None] * len(bodies)
    for step in range(len(bodies) + sum(lags)):
        at = step
        for index, stage in enumerate(stages):
            if 0 <= at < len(bodies):
                held[at] = stage(*bodies[at]) if index == 0 else stage(held[at], *bodies[at])
            if index < len(lags):
                at -= lags[index]


def attend_kernel(lengths_ref, q_ref, k_ref, v_ref, out_ref, lse_ref, bias, mixed, *, row, docs):
    seq_len = q_ref.shape[0]

    @pl.when(pl.program_id(0) == 0)
    def _():
        fill_bias(bias, lengths_ref, row, seq_len, docs)

    query_t = (q_ref[...] * BF(HEAD_DIM**-0.5)).T
    value_t = v_ref[...].T
    query_h = [head_rows(query_t, head) for head in range(2)]

    def scores_of(head, first, low, high, start):
        cols = slice(first, first + TILE)
        scores = nn(k_ref[low:high, :], query_h[head][:, cols]) + bias[start : start + high - low, :]
        return scores, jnp.max(scores, axis=0, keepdims=True)

    def weights_of(held, head, first, low, high, start):
        scores, peak = held
        weights = jnp.exp(scores - peak)
        total = jnp.sum(weights, axis=0, keepdims=True)
        lse_ref[0, head : head + 1, first : first + TILE] = peak + jnp.log(total)
        return weights.astype(BF), 1.0 / total

    def mix(held, head, first, low, high, start):
        weights, scale = held
        rows = slice(head * HEAD_DIM, (head + 1) * HEAD_DIM)
        mixed[rows, first : first + TILE] = nn(value_t[rows, low:high], weights) * scale

    bodies = [(head,) + span for head in range(2) for span in spans(seq_len)[0]]
    staged(bodies, (scores_of, weights_of, mix), (2, 1))
    out_ref[...] = mixed[...].astype(BF).T


def attend_back_kernel(
    lengths_ref,
    q_ref,
    k_ref,
    v_ref,
    out_ref,
    grad_ref,
    lse_ref,
    dq_ref,
    dk_ref,
    dv_ref,
    bias,
    key_sum,
    value_sum,
    query_sum,
    *,
    row,
    docs,
):
    seq_len = q_ref.shape[0]

    @pl.when(pl.program_id(0) == 0)
    def _():
        fill_bias(bias, lengths_ref, row, seq_len, docs)

    query = q_ref[...] * BF(HEAD_DIM**-0.5)
    query_t = query.T
    key_t = k_ref[...].T
    grad = grad_ref[...]
    grad_t = grad.T
    weighted = grad_t.astype(F32) * out_ref[...].T.astype(F32)
    key_sum[...] = jnp.zeros_like(key_sum)
    value_sum[...] = jnp.zeros_like(value_sum)
    query_th = [head_rows(query_t, head) for head in range(2)]
    grad_th = [head_rows(grad_t, head) for head in range(2)]
    query_h = [head_cols(query, head) for head in range(2)]
    grad_h = [head_cols(grad, head) for head in range(2)]
    inner = [
        col_sum(weighted[head * HEAD_DIM : (head + 1) * HEAD_DIM, :]) for head in range(2)
    ]
    bodies = []
    for first, low, high, start in spans(seq_len)[0]:
        for head in range(2):
            for key in range(low, high, TILE):
                bodies.append((head, first, key, start + key - low, key == low))

    def products(head, first, key, start, opening):
        cols, rows = slice(first, first + TILE), slice(key, key + TILE)
        scores = nn(k_ref[rows, :], query_th[head][:, cols]) + bias[start : start + TILE, :]
        return scores, nn(v_ref[rows, :], grad_th[head][:, cols])

    def score_grads(held, head, first, key, start, opening):
        scores, grad_probs = held
        cols = slice(first, first + TILE)
        probs = jnp.exp(scores - lse_ref[0, head : head + 1, cols])
        return probs.astype(BF), (probs * (grad_probs - inner[head][:, cols])).astype(BF)

    def add_grads(held, head, first, key, start, opening):
        probs, grad_scores = held
        cols, rows = slice(first, first + TILE), slice(key, key + TILE)
        value_sum[rows, :] += nn(probs, grad_h[head][cols, :])
        key_sum[rows, :] += nn(grad_scores, query_h[head][cols, :])
        lanes = slice(head * HEAD_DIM, (head + 1) * HEAD_DIM)
        part = nn(key_t[lanes, rows], grad_scores)
        if opening:
            query_sum[lanes, cols] = part
        else:
            query_sum[lanes, cols] += part

    staged(bodies, (products, score_grads, add_grads), (2, 1))
    dq_ref[...] = (query_sum[...] * (HEAD_DIM**-0.5)).astype(BF).T
    dk_ref[...] = key_sum[...].astype(BF)
    dv_ref[...] = value_sum[...].astype(BF)


def out_kernel(table_ref, att_ref, x_ref, vec_ref, *refs):
    sources, (middle_ref, normed_ref, sums_ref, weight, sem) = refs[:SOURCES], refs[SOURCES:]

    @pl.when(pl.program_id(0) == 0)
    def _():
        fill(weight, table_ref, sources, sem, OUT_BLOCKS)
        sums_ref[...] = jnp.zeros_like(sums_ref)

    branch = nn(att_ref[...], weight[...]) + vec_ref[OUT_BIAS : OUT_BIAS + 1]
    middle = x_ref[...].astype(F32) + branch
    middle_ref[...] = middle
    unit, _ = norm_parts(middle)
    normed_ref[...] = (
        unit * vec_ref[LN2_GAIN : LN2_GAIN + 1] + vec_ref[LN2_SHIFT : LN2_SHIFT + 1]
    ).astype(BF)
    sums_ref[0:1] += col_sum(middle * middle)
    sums_ref[1:2] += col_sum(branch * branch)


def put_pieces(keep_ref, send_ref, grad, core, base):
    height, width = keep_ref.shape[-2:]
    for held, ref in enumerate((keep_ref, send_ref)):
        for pair in range(ref.shape[0]):
            piece = 2 * pair + (core ^ held)
            for row in range(2):
                top = pl.multiple_of(row * width + piece * height, 8)
                for col in range(2):
                    ref[pair, base + 2 * row + col] = grad[
                        pl.ds(top, height), col * width : (col + 1) * width
                    ].astype(BF)


def mlp_kernel(table_ref, me_ref, normed_ref, cot_ref, vec_ref, *refs):
    sources, refs = refs[:SOURCES], refs[SOURCES:]
    mlp_ref, back_ref, grad_ref, keep_ref, send_ref, bias_ref = refs[:6]
    fc_tiles, proj_tiles, hidden, grad_pre, whole_grad, sems = refs[6:]
    step = pl.program_id(0)
    width = sources[0].shape[-1]
    ff_cols = FF // width
    tiles = fc_tiles.shape[0]

    @pl.when(step == 0)
    def _():
        for tile in range(tiles):
            at = 2 * tile
            fc_blocks = [(16 + r * ff_cols + at + c, r, c) for r in range(2) for c in range(2)]
            proj_first = 16 + 2 * ff_cols + 2 * at
            proj_blocks = [(proj_first + 2 * r + c, r, c) for r in range(2) for c in range(2)]
            start_fill(fc_tiles.at[tile], table_ref, sources, sems.at[tile], fc_blocks)
            start_fill(proj_tiles.at[tile], table_ref, sources, sems.at[tiles + tile], proj_blocks)

    w_fc, w_proj = fc_tiles.at[step], proj_tiles.at[step]
    wait_fill(w_fc, sems.at[step])
    wait_fill(w_proj, sems.at[tiles + step])
    bias_row = vec_ref[pl.ds(FC_BIAS + step, 1)]

    @pl.when(step == 0)
    def _():
        mlp_ref[...] = jnp.zeros_like(mlp_ref)
        back_ref[...] = jnp.zeros_like(back_ref)

    def entering(rows):
        return nn(normed_ref[rows], w_fc[...]) + bias_row, nt(cot_ref[rows], w_proj[...])

    def activated(held, rows):
        pre, grad = held
        root = 0.7978845608028654
        square = pre * pre
        tanh = jnp.tanh(pre * (root + root * 0.044715 * square))
        half = 0.5 + 0.5 * tanh
        low = (pre * half).astype(BF)
        slope = half + (0.5 * pre) * (1.0 - tanh * tanh) * (root + root * 3.0 * 0.044715 * square)
        back = (grad * slope).astype(BF)
        hidden[rows] = low
        grad_pre[rows] = back
        mlp_ref[rows] += nn(low, w_proj[...])
        back_ref[rows] += nt(back, w_fc[...])
        sums.append(col_sum(back.astype(F32)))

    sums = []
    count = normed_ref.shape[0]
    staged(
        [(slice(row, row + TILE),) for row in range(0, count, TILE)], (entering, activated), (1,)
    )
    bias_ref[0] = sum(sums)
    for base, left, right in ((0, normed_ref, grad_pre), (4, hidden, cot_ref)):
        grad = tn(left[...], right[...])

        @pl.when(step < FIRST_TILES)
        def _():
            pieces, _, _, height, _ = grad_ref.shape
            low = grad.astype(BF)
            for row in range(2):
                for col in range(2):
                    for piece in range(pieces):
                        top = row * width + piece * height
                        grad_ref[piece, 0, base + 2 * row + col] = low[
                            top : top + height, col * width : (col + 1) * width
                        ]

        @pl.when(step >= FIRST_TILES)
        def _():
            whole_grad[...] = grad
            put_pieces(keep_ref, send_ref, whole_grad, me_ref[0] % 2, base)


def middle_kernel(
    table_ref,
    me_ref,
    middle_ref,
    mlp_ref,
    back_ref,
    cot_ref,
    att_ref,
    vec_ref,
    *refs,
):
    sources, refs = refs[:SOURCES], refs[SOURCES:]
    output_ref, grad_ref, grad_att_ref, keep_ref, send_ref, sums_ref = refs[:6]
    weight, branch, out_grad, sem = refs[6:]
    step = pl.program_id(0)

    @pl.when(step == 0)
    def _():
        fill(weight, table_ref, sources, sem, OUT_BLOCKS)
        sums_ref[...] = jnp.zeros_like(sums_ref)

    middle = middle_ref[...]
    mlp = mlp_ref[...] + vec_ref[PROJ_BIAS : PROJ_BIAS + 1]
    result = middle + mlp
    output_ref[...] = result.astype(BF)
    cot = cot_ref[...].astype(F32)
    unit, root = norm_parts(middle)
    back = back_ref[...]
    grad = cot + norm_back(unit, root, vec_ref[LN2_GAIN : LN2_GAIN + 1], back)
    grad_ref[...] = grad
    low = grad.astype(BF)
    branch[pl.ds(pl.multiple_of(step * TILE, TILE), TILE)] = low
    grad_att_ref[...] = nt(low, weight[...]).astype(BF)
    sums_ref[0:1] += col_sum(result * result)
    sums_ref[1:2] += col_sum(mlp * mlp)
    sums_ref[2:3] += col_sum(back * unit)
    sums_ref[3:4] += col_sum(back)
    sums_ref[4:5] += col_sum(low.astype(F32))
    sums_ref[5:6] += col_sum(cot)

    @pl.when(step == pl.num_programs(0) - 1)
    def _():
        out_grad[...] = tn(att_ref[...], branch[...])
        put_pieces(keep_ref, send_ref, out_grad, me_ref[0] % 2, 0)


def weight_back_kernel(
    me_ref, normed_ref, dq_ref, dk_ref, dv_ref, keep_ref, send_ref, sums_ref, grad
):
    step = pl.program_id(0)

    @pl.when(step == 0)
    def _():
        sums_ref[0:1] = col_sum(dq_ref[...].astype(F32))
        sums_ref[1:2] = col_sum(dv_ref[...].astype(F32))

    for part, ref in enumerate((dq_ref, dk_ref, dv_ref)):

        @pl.when(step == part)
        def _():
            grad[...] = tn(normed_ref[...], ref[...])

    put_pieces(keep_ref, send_ref, grad, me_ref[0] % 2, 0)


def input_kernel(table_ref, x_ref, dq_ref, dk_ref, dv_ref, grad_ref, vec_ref, *refs):
    sources, (out_ref, sums_ref, weight, sem) = refs[:SOURCES], refs[SOURCES:]

    @pl.when(pl.program_id(0) == 0)
    def _():
        fill(weight, table_ref, sources, sem, QKV_BLOCKS)
        sums_ref[...] = jnp.zeros_like(sums_ref)

    back = nt(dq_ref[...], weight[:, :D])
    back += nt(dk_ref[...], weight[:, D : 2 * D])
    back += nt(dv_ref[...], weight[:, 2 * D :])
    unit, root = norm_parts(x_ref[...].astype(F32))
    out_ref[...] = grad_ref[...] + norm_back(unit, root, vec_ref[LN1_GAIN : LN1_GAIN + 1], back)
    sums_ref[0:1] += col_sum(back * unit)
    sums_ref[1:2] += col_sum(back)


def lay_kernel(source_ref, *refs):
    out_ref, pieces = refs[-2:]
    begin = 0
    for ref in refs[:-2]:
        pieces[begin : begin + ref.shape[0]] = ref[...]
        begin += ref.shape[0]
    shards, own = out_ref.shape[:2]
    for shard in range(shards):
        for slot in range(own):
            out_ref[shard, slot] = pieces[source_ref[shard * own + slot]]


def factor_kernel(
    shard_ref,
    grad_ref,
    right_ref,
    matrix_ref,
    left_stat_ref,
    right_stat_ref,
    left_root_ref,
    rows_ref,
    left_ref,
    right_new_ref,
    matrix_new_ref,
    whole_grad,
    grad_t,
):
    rows = matrix_ref.shape[1]
    pieces, _, height, _ = grad_ref.shape
    for piece in range(pieces):
        whole_grad[piece * height : (piece + 1) * height, :] = grad_ref[piece, 0]
    grad = whole_grad[...]
    grad_t[...] = grad.T
    own = pl.ds(pl.multiple_of(shard_ref[0] * rows, rows), rows)
    grad_rows = whole_grad[own, :]
    rows_ref[0] = grad_rows.astype(F32)
    left_ref[0] = DECAY * left_stat_ref[0] + (1.0 - DECAY) * nn(grad_rows, grad_t[...])
    right_new_ref[0] = DECAY * right_stat_ref[0] + (1.0 - DECAY) * nn(grad_t[own, :], grad)
    half = nn(left_root_ref[0].astype(BF), grad)
    update = nn(half.astype(BF), right_ref[0])
    matrix_new_ref[0] = matrix_ref[0] - MATRIX_RATE * update


def core_sum_kernel(*refs):
    out_ref = refs[-1]
    begin = 0
    for keep, sent in zip(refs[:-1:2], refs[1:-1:2]):
        blocks = keep.shape[1]
        out_ref[0, begin : begin + blocks] = (keep[0].astype(F32) + sent[0].astype(F32)).astype(BF)
        begin += blocks


def across_dp(values, bit):
    count = lax.axis_size("dp")
    return lax.ppermute(values, "dp", [(i, i ^ (1 << bit)) for i in range(count)])


def across_fsdp(values, offset):
    count = lax.axis_size("fsdp")
    return lax.ppermute(values, "fsdp", [(i, i ^ offset) for i in range(count)])


def gather_by_permutes(values, me, shard):
    fsdp_count, dp_count = lax.axis_size("fsdp"), lax.axis_size("dp")
    held = jnp.stack([values] + [across_fsdp(values, k) for k in range(1, fsdp_count)])
    for bit in range(dp_count.bit_length() - 1):
        held = jnp.stack([held, across_dp(held, bit)])
    held = held.reshape((dp_count, fsdp_count) + values.shape)
    held = jnp.take(held, jnp.arange(dp_count) ^ me, axis=0)
    held = jnp.take(held, jnp.arange(fsdp_count) ^ shard, axis=1)
    return held.transpose(2, 0, 1, 3, 4).reshape((-1,) + values.shape[1:])


def core_sum(grads, name, ties=()):
    ins = []
    for keep, send in grads:
        ins += [keep, across_dp(send, 0)]
    pairs = ins[0].shape[0]
    rest = ins[0].shape[2:]
    blocks = sum(keep.shape[1] for keep, _ in grads)

    def one(array):
        return (array, (1,) + array.shape[1:], lambda i: (i, 0, 0, 0))

    return call(
        core_sum_kernel,
        (pairs,),
        [one(array) for array in ins],
        [((pairs, blocks) + rest, BF, (1, blocks) + rest, lambda i: (i, 0, 0, 0))],
        ties=ties,
        name=name,
    )[0]


def plane_parts(values):
    pairs = lax.axis_size("dp") // 2
    groups = [[2 * pair + core for pair in range(pairs)] for core in range(2)]
    return lax.all_to_all(values, "dp", 0, 0, axis_index_groups=groups, tiled=True)


def dp_sum(values):
    for bit in range(lax.axis_size("dp").bit_length() - 1):
        values = values + across_dp(values, bit)
    return values


def fsdp_sum(values):
    offset = 1
    while offset < lax.axis_size("fsdp"):
        values = values + across_fsdp(values, offset)
        offset *= 2
    return values


def per_device(
    tokens,
    cotangent,
    doc_lengths,
    block_slot,
    matrices,
    vectors,
    vector_second,
    left_stat,
    right_stat,
    left_root,
    right_root,
):
    dp_count = lax.axis_size("dp")
    fsdp_count = lax.axis_size("fsdp")
    own_blocks, own_rows, width = matrices.shape
    blocks = own_blocks * dp_count
    height = width // dp_count
    me = lax.axis_index("dp").astype(jnp.int32).reshape(1)
    shard = lax.axis_index("fsdp").astype(jnp.int32).reshape(1)
    half = lax.axis_index("fsdp")
    half = sum((half >> bit) & 1 for bit in range(fsdp_count.bit_length())) % 2
    half = half.astype(jnp.int32).reshape(1)
    numbers = jnp.arange(blocks, dtype=jnp.int32)
    holder = block_slot // own_blocks
    before = (holder[None, :] == holder[:, None]) & (numbers[None, :] < numbers[:, None])
    rank = jnp.sum(before.astype(jnp.int32), axis=1)
    early = max(2, 2 * own_blocks // 3 // 2 * 2)
    here = jnp.arange(own_blocks, dtype=jnp.int32)
    mine = (holder == me[0]) & (rank[None, :] == here[:, None])
    local = jnp.sum(jnp.where(mine, block_slot[None, :] % own_blocks, 0), axis=1)
    low = jnp.take(matrices, local, axis=0).astype(BF)
    late = lax.all_gather(low[early:], ("dp", "fsdp"), axis=1, tiled=True)
    late = late.reshape(-1, own_rows, width)
    right_whole = lax.all_gather(right_root.astype(BF), "fsdp", axis=1, tiled=True)

    line = jnp.stack([low[:early]] + [across_fsdp(low[:early], k) for k in range(1, fsdp_count)])
    plane_bits = list(range(1, dp_count.bit_length() - 1))
    sources, plane_places = [], []
    rel = holder ^ me[0]
    for part, order in enumerate((plane_bits, plane_bits[::-1])):
        held = line[:, part * early // 2 : (part + 1) * early // 2]
        for bit in order:
            held = jnp.stack([held, across_dp(held, bit)])
        sources += [held, across_dp(held, 0)]
        plane_places.append(sum(((rel >> bit) & 1) << i for i, bit in enumerate(order)))
    sources = [source.reshape(-1, own_rows, width) for source in sources]
    units = jnp.arange(fsdp_count, dtype=jnp.int32)[None, :]
    second_half = (rank >= early // 2).astype(jnp.int32)
    plane_place = jnp.where(second_half == 1, plane_places[1], plane_places[0])[:, None]
    inside = (rank - second_half * (early // 2))[:, None]
    early_index = (plane_place * fsdp_count + (units ^ shard[0])) * (early // 2) + inside
    late_index = ((rank[:, None] - early) * dp_count + holder[:, None]) * fsdp_count + units
    is_late = rank[:, None] >= early
    source_at = jnp.where(is_late, 4, (second_half * 2 + (rel & 1))[:, None] + 0 * units)
    table = jnp.concatenate(
        [source_at.reshape(-1), jnp.where(is_late, late_index, early_index).reshape(-1)]
    ).astype(jnp.int32)
    qkv_early = jnp.max(rank[:12]) < early

    vec = vectors.reshape(-1, D)
    count = tokens.shape[0]
    rows_here, docs = doc_lengths.shape
    seq_len = count // rows_here
    steps = count // TILE

    def from_units(last):
        return [(source, None, None) for source in sources + [last]]

    def qkv(last):
        return tuple(
            call(
                qkv_kernel,
                (steps,),
                [tokens_in(tokens), whole(vec)] + from_units(last),
                [
                    ((count, D), BF, (TILE, D), lambda i, *_: (i, 0)),
                    ((count, 3 * D), BF, (TILE, 3 * D), lambda i, *_: (i, 0)),
                ],
                [pltpu.VMEM((D, 3 * D), BF), pltpu.SemaphoreType.DMA],
                scalars=[table],
                name="qkv",
            )
        )

    def qkv_with_late():
        return qkv(gather_by_permutes(low[early:], me[0], shard[0]))

    normed1, projected = lax.cond(qkv_early, lambda: qkv(sources[0]), qkv_with_late)
    weights_in = from_units(late)

    pairs = HEADS // 2
    bias_rows = spans(seq_len)[1]

    def pair_in(array, row, offset):
        return (array, (seq_len, PAIR), lambda p, *_: (row, offset + p))

    attended, lses = [], []
    for row in range(rows_here):
        one, lse = call(
            functools.partial(attend_kernel, row=row, docs=docs),
            (pairs,),
            [pair_in(projected, row, part * pairs) for part in range(3)],
            [
                ((seq_len, D), BF, (seq_len, PAIR), lambda p, *_: (0, p)),
                ((pairs, 2, seq_len), F32, (1, 2, seq_len), lambda p, *_: (p, 0, 0)),
            ],
            [pltpu.VMEM((bias_rows, TILE), F32), pltpu.VMEM((PAIR, seq_len), F32)],
            scalars=[doc_lengths],
            name="attend",
        )
        attended.append(one)
        lses.append(lse)
    attended = attended[0] if rows_here == 1 else jnp.concatenate(attended, axis=0)

    middle, normed2, sums_mid = call(
        out_kernel,
        (steps,),
        [tokens_in(attended), tokens_in(tokens), whole(vec)] + weights_in,
        [
            ((count, D), F32, (TILE, D), lambda i, *_: (i, 0)),
            ((count, D), BF, (TILE, D), lambda i, *_: (i, 0)),
            out_whole((8, D), F32),
        ],
        [pltpu.VMEM((D, D), BF), pltpu.SemaphoreType.DMA],
        scalars=[table],
        name="attn_out",
    )

    ff_cols = FF // width
    pair_count = dp_count // 2
    tiles = FF // D
    mlp, back2, grads, keep, send, fc_sums = call(
        mlp_kernel,
        (tiles,),
        [whole(normed2), whole(cotangent), whole(vec)] + weights_in,
        [
            out_whole((count, D), F32),
            out_whole((count, D), F32),
            (
                (dp_count, FIRST_TILES, 8, height, width),
                BF,
                (dp_count, 1, 8, height, width),
                lambda t, *_: (0, jnp.minimum(t, FIRST_TILES - 1), 0, 0, 0),
            ),
        ]
        + [
            (
                (pair_count, (tiles - FIRST_TILES) * 8, height, width),
                BF,
                (pair_count, 8, height, width),
                lambda t, *_: (0, jnp.maximum(t - FIRST_TILES, 0), 0, 0),
            )
        ]
        * 2
        + [((tiles, 1, D), F32, (1, 1, D), lambda t, *_: (t, 0, 0))],
        [pltpu.VMEM((tiles, D, D), BF)] * 2
        + [pltpu.VMEM((count, D), BF)] * 2
        + [pltpu.VMEM((D, D), F32), pltpu.SemaphoreType.DMA((2 * tiles,))],
        scalars=[table, me],
        name="mlp",
    )
    mlp_grads = (keep, send)
    first_grads = lax.psum_scatter(
        grads.reshape(-1, width), "dp", scatter_dimension=0, tiled=True
    )

    output, grad_middle, grad_attended, *out_grads, sums_back = call(
        middle_kernel,
        (steps,),
        [
            tokens_in(middle),
            tokens_in(mlp),
            tokens_in(back2),
            tokens_in(cotangent),
            whole(attended),
            whole(vec),
        ]
        + weights_in,
        [
            ((count, D), BF, (TILE, D), lambda i, *_: (i, 0)),
            ((count, D), F32, (TILE, D), lambda i, *_: (i, 0)),
            ((count, D), BF, (TILE, D), lambda i, *_: (i, 0)),
            out_whole((pair_count, 4, height, width), BF),
            out_whole((pair_count, 4, height, width), BF),
            out_whole((8, D), F32),
        ],
        [
            pltpu.VMEM((D, D), BF),
            pltpu.VMEM((count, D), BF),
            pltpu.VMEM((D, D), F32),
            pltpu.SemaphoreType.DMA,
        ],
        scalars=[table, me],
        ties=[right_whole],
        name="middle_back",
    )

    second_core = core_sum([mlp_grads, out_grads], "second_core")
    second_parts = plane_parts(second_core)
    def attend_back(row, begin, stop, onto, ties):
        return call(
            functools.partial(attend_back_kernel, row=row, docs=docs),
            (stop - begin,),
            [pair_in(projected, row, part * pairs + begin) for part in range(3)]
            + [
                pair_in(attended, row, begin),
                pair_in(grad_attended, row, begin),
                (lses[row], (1, 2, seq_len), lambda p, *_: (p + begin, 0, 0)),
            ],
            [((count, D), BF, (seq_len, PAIR), lambda p, *_: (row, p + begin))] * 3,
            [
                pltpu.VMEM((bias_rows, TILE), F32),
                pltpu.VMEM((seq_len, PAIR), F32),
                pltpu.VMEM((seq_len, PAIR), F32),
                pltpu.VMEM((PAIR, seq_len), F32),
            ],
            scalars=[doc_lengths],
            ties=ties,
            onto=onto,
            name="attend_back",
        )

    grads = ()
    for row in range(rows_here):
        grads = attend_back(row, 0, pairs // 2, grads, [second_core])
        grads = attend_back(row, pairs // 2, pairs, grads, [])
    dq, dk, dv = grads

    half_shape = (pair_count, 12, height, width)
    keep, send, sums_qkv = call(
        weight_back_kernel,
        (3,),
        [whole(array) for array in (normed1, dq, dk, dv)],
        [(half_shape, BF, (pair_count, 4, height, width), lambda p, *_: (0, p, 0, 0))] * 2
        + [out_whole((8, D), F32)],
        [pltpu.VMEM((D, D), F32)],
        scalars=[me],
        name="qkv_weight_back",
    )
    third_core = core_sum([(keep, send)], "third_core")
    second_halves = plane_sum(second_parts, half, [], "second_plane")
    third_parts = plane_parts(third_core)

    x_grad, sums_in = call(
        input_kernel,
        (steps,),
        [
            tokens_in(tokens),
            tokens_in(dq),
            tokens_in(dk),
            tokens_in(dv),
            tokens_in(grad_middle),
            whole(vec),
        ]
        + weights_in,
        [((count, D), F32, (TILE, D), lambda i, *_: (i, 0)), out_whole((8, D), F32)],
        [pltpu.VMEM((D, 3 * D), BF), pltpu.SemaphoreType.DMA],
        scalars=[table],
        ties=[second_halves[0], third_core],
        name="input_back",
    )

    second_half = line_half(second_halves, [x_grad], "second_half")
    first_halves = plane_sum(
        first_grads.reshape(1, -1, height, width), half, [second_half], "first_split"
    )
    first_half = line_half(first_halves, [], "first_half")
    first_total = line_rest(first_half, [], "first_rest")
    second_total = line_rest(second_half, [], "second_rest")
    vector_local = call(
        pack_kernel,
        (1,),
        [whole(array) for array in (sums_in, sums_qkv, sums_back, sums_mid, fc_sums)],
        [out_whole((16, D), F32)],
        name="pack",
    )[0]
    vector_plane = dp_sum(vector_local)
    vector_sums = fsdp_sum(vector_plane)
    third_halves = plane_sum(third_parts, half, [second_half, first_halves[0]], "third_plane")
    third_total = line_rest(line_half(third_halves, [], "third_half"), [], "third_rest")
    vector_grad = vector_sums[:12].reshape(-1)
    square_sums = vector_sums[12, :4]

    order = []
    for tile in range(FF // D):
        order += [16 + r * ff_cols + 2 * tile + c for r in range(2) for c in range(2)]
        order += [16 + 2 * ff_cols + 2 * (2 * tile + r) + c for r in range(2) for c in range(2)]
    order += list(range(12, 16))
    order += [r * 6 + 2 * part + c for part in range(3) for r in range(2) for c in range(2)]
    standing = jnp.array([order.index(u) for u in range(blocks)], jnp.int32)
    source = jnp.sum(
        jnp.where(block_slot[None, :] == numbers[:, None], standing[None, :], 0), axis=1
    )
    begin = 0
    spread = []
    for total in (first_total, second_total, third_total):
        size = total.shape[0]
        inside = source - begin
        moved = begin + (inside // size ^ half[0]) * size + inside % size
        source = jnp.where((inside >= 0) & (inside < size * 2), moved, source)
        begin += size * 2
        spread += line_spread(total)
    laid = call(
        lay_kernel,
        (1,),
        [whole(array) for array in spread],
        [out_whole((dp_count, own_blocks, height, width), BF)],
        [pltpu.VMEM((blocks, height, width), BF)],
        scalars=[source],
        ties=[vector_plane],
        name="lay",
    )[0]
    grad_whole = lax.all_to_all(laid, "dp", 0, 0, tiled=True)

    def block_in(array):
        return (array, (1,) + array.shape[1:], lambda b, *_: (b, 0, 0))

    matrix_grad, left_new, right_new, matrix_new = call(
        factor_kernel,
        (own_blocks,),
        [(grad_whole, (dp_count, 1, height, width), lambda b, *_: (0, b, 0, 0))]
        + [block_in(a) for a in (right_whole, matrices, left_stat, right_stat, left_root)],
        [(matrices.shape, F32, (1, own_rows, width), lambda b, *_: (b, 0, 0))] * 4,
        [pltpu.VMEM((width, width), BF)] * 2,
        scalars=[shard],
        name="factor",
    )

    residual_scale = jnp.sqrt(square_sums / (count * dp_count * fsdp_count * D))
    second_new = DECAY * vector_second + (1.0 - DECAY) * vector_grad * vector_grad
    vector_new = vectors - VECTOR_RATE * vector_grad / (jnp.sqrt(second_new) + ROOT_EPSILON)
    return (
        output,
        x_grad,
        matrix_grad,
        left_new,
        right_new,
        matrix_new,
        vector_grad,
        second_new,
        vector_new,
        residual_scale,
    )


def solution(mesh):
    tokens = P(("dp", "fsdp"), None)
    stored = P("dp", "fsdp", None)
    return jax.shard_map(
        per_device,
        mesh=mesh,
        in_specs=(tokens, tokens, tokens, P(), stored, P(), P()) + (stored,) * 4,
        out_specs=(tokens, tokens) + (stored,) * 4 + (P(),) * 4,
        check_vma=False,
    )
```

```python
import functools

import jax
import jax.numpy as jnp
from jax import lax
from jax.experimental import pallas as pl
from jax.experimental.pallas import tpu as pltpu
from jax.sharding import PartitionSpec as P

D = 768
HEADS = 12
HEAD_DIM = 64
FF = 3072
LONGEST = 512

NORM_EPSILON = 1e-05
ROOT_EPSILON = 1e-08
DECAY = 0.5
MATRIX_RATE = 1.5
VECTOR_RATE = 0.1
MASKED = -1e30

BF = jnp.bfloat16
F32 = jnp.float32
PAIR = 2 * HEAD_DIM
TILE = 256
VMEM = 60 * 1024 * 1024
FIRST_TILES = 2

LN1_GAIN, LN1_SHIFT, Q_BIAS, V_BIAS, OUT_BIAS, LN2_GAIN, LN2_SHIFT, PROJ_BIAS, FC_BIAS = range(9)


def nn(left, right):
    return jnp.dot(left, right, preferred_element_type=F32)


def nt(left, right):
    return lax.dot_general(left, right, (((1,), (1,)), ((), ())), preferred_element_type=F32)


def tn(left, right):
    return lax.dot_general(left, right, (((0,), (0,)), ((), ())), preferred_element_type=F32)


def col_sum(values):
    return jnp.sum(values, axis=0, keepdims=True)


def norm_parts(values):
    center = values - jnp.mean(values, axis=-1, keepdims=True)
    spread = jnp.mean(center * center, axis=-1, keepdims=True)
    root = lax.rsqrt(spread + NORM_EPSILON)
    return center * root, root


def norm_back(unit, root, gain, grad):
    scaled = grad * gain
    return root * (
        scaled
        - jnp.mean(scaled, axis=-1, keepdims=True)
        - unit * jnp.mean(scaled * unit, axis=-1, keepdims=True)
    )


def start_fill(weight, table_ref, sources, sem, blocks):
    _, height, width = sources[0].shape
    units = width // height
    half = table_ref.shape[0] // 2
    for number, row, col in blocks:
        at = number * units
        source = table_ref[at]
        for which, ref in enumerate(sources):

            @pl.when(source == which)
            def _():
                for unit in range(units):
                    top = row * width + unit * height
                    target = weight.at[pl.ds(top, height), pl.ds(col * width, width)]
                    pltpu.make_async_copy(ref.at[table_ref[half + at + unit]], target, sem).start()


def wait_fill(weight, sem):
    pltpu.make_async_copy(weight, weight, sem).wait()


def fill(weight, table_ref, sources, sem, blocks):
    start_fill(weight, table_ref, sources, sem, blocks)
    wait_fill(weight, sem)


QKV_BLOCKS = [(row * 6 + col, row, col) for row in range(2) for col in range(6)]
OUT_BLOCKS = [(12 + row * 2 + col, row, col) for row in range(2) for col in range(2)]
SOURCES = 9


def call(kernel, grid, ins, outs, scratch=(), scalars=(), ties=(), onto=(), name=None):
    first = len(scalars) + len(ins)
    ties = list(onto) + list(ties)

    def body(*refs):
        kernel(*refs[:first], *refs[first + len(ties) :])

    spec = pltpu.PrefetchScalarGridSpec(
        num_scalar_prefetch=len(scalars),
        grid=grid,
        in_specs=[
            pl.BlockSpec(memory_space=pltpu.HBM) if block is None else pl.BlockSpec(block, index)
            for _, block, index in ins
        ]
        + [pl.BlockSpec(memory_space=pl.ANY)] * len(ties),
        out_specs=[pl.BlockSpec(block, index) for _, _, block, index in outs],
        scratch_shapes=list(scratch),
    )
    return pl.pallas_call(
        body,
        grid_spec=spec,
        out_shape=[jax.ShapeDtypeStruct(shape, dtype) for shape, dtype, _, _ in outs],
        compiler_params=pltpu.CompilerParams(
            dimension_semantics=("arbitrary",) * len(grid), vmem_limit_bytes=VMEM
        ),
        cost_estimate=pl.CostEstimate(flops=1024, bytes_accessed=1024, transcendentals=0),
        input_output_aliases={first + place: place for place in range(len(onto))},
        name=name,
    )(*scalars, *[array for array, _, _ in ins], *ties)


def whole(array):
    return (array, array.shape, lambda *_: (0,) * array.ndim)


def tokens_in(array, cols=None):
    return (array, (TILE, cols or array.shape[1]), lambda i, *_: (i, 0))


def out_whole(shape, dtype):
    return (shape, dtype, shape, lambda *_: (0,) * len(shape))


def plane_sum_kernel(half_ref, *refs):
    half = len(refs) // 2
    for parts, out in zip(refs[:half], refs[half:]):
        total = parts[0].astype(F32)
        for part in range(1, parts.shape[0]):
            total = total + parts[part].astype(F32)
        out[...] = total.astype(BF)


def plane_sum(parts, half, ties, name):
    count, blocks, height, width = parts.shape
    size = blocks // 2

    def group(offset):
        return (parts, (count, size, height, width), lambda i, at: (0, at[0] ^ offset, 0, 0))

    return call(
        plane_sum_kernel,
        (1,),
        [group(0), group(1)],
        [out_whole((size, height, width), BF)] * 2,
        scalars=[half],
        ties=ties,
        name=name,
    )


def add_kernel(left_ref, right_ref, out_ref):
    out_ref[...] = (left_ref[...].astype(F32) + right_ref[...].astype(F32)).astype(BF)


def add_up(left, right, ties, name):
    return call(
        add_kernel,
        (1,),
        [whole(left), whole(right)],
        [out_whole(left.shape, BF)],
        ties=ties,
        name=name,
    )[0]


def line_half(halves, ties, name):
    return add_up(halves[0], across_fsdp(halves[1], 1), ties, name)


def line_rest(total, ties, name):
    offset = 3
    while offset <= lax.axis_size("fsdp"):
        total = add_up(total, across_fsdp(total, offset), ties, name)
        offset = 2 * offset - 1
    return total


def line_spread(total):
    return [total, across_fsdp(total, 1)]


def pack_kernel(in_ref, qkv_ref, back_ref, mid_ref, *refs):
    fc_refs, out_ref = refs[:-1], refs[-1]
    out_ref[0:2] = in_ref[0:2]
    out_ref[2:4] = qkv_ref[0:2]
    out_ref[4:5] = back_ref[4:5]
    out_ref[5:7] = back_ref[2:4]
    out_ref[7:8] = back_ref[5:6]
    row = 8
    for ref in fc_refs:
        for tile in range(ref.shape[0]):
            out_ref[row : row + 1] = ref[tile]
            row += 1
    lanes = lax.broadcasted_iota(jnp.int32, (1, D), 1)
    line = jnp.zeros((1, D), F32)
    for lane, value in enumerate((mid_ref[0:1], back_ref[0:1], mid_ref[1:2], back_ref[1:2])):
        line = jnp.where(lanes == lane, jnp.sum(value), line)
    out_ref[row : row + 1] = line
    out_ref[row + 1 :] = jnp.zeros_like(out_ref[row + 1 :])


def qkv_kernel(table_ref, x_ref, vec_ref, *refs):
    sources, (normed_ref, projected_ref, weight, sem) = refs[:SOURCES], refs[SOURCES:]

    @pl.when(pl.program_id(0) == 0)
    def _():
        fill(weight, table_ref, sources, sem, QKV_BLOCKS)

    unit, _ = norm_parts(x_ref[...].astype(F32))
    normed = (unit * vec_ref[LN1_GAIN : LN1_GAIN + 1] + vec_ref[LN1_SHIFT : LN1_SHIFT + 1]).astype(
        BF
    )
    normed_ref[...] = normed
    for part in range(3):
        cols = slice(part * D, (part + 1) * D)
        value = nn(normed, weight[:, cols])
        if part != 1:
            row = Q_BIAS if part == 0 else V_BIAS
            value = value + vec_ref[row : row + 1]
        projected_ref[:, cols] = value.astype(BF)


def spans(seq_len):
    out = []
    start = 0
    for first in range(0, seq_len, TILE):
        low = max(0, first - LONGEST)
        out.append((first, low, first + TILE, start))
        start += first + TILE - low
    return out, start


def fill_bias(bias, lengths_ref, row, seq_len, docs):
    for first, low, high, start in spans(seq_len)[0]:
        place_q = lax.broadcasted_iota(jnp.int32, (1, TILE), 1) + first
        begin = jnp.zeros((1, TILE), jnp.int32)
        end = jnp.int32(0)
        for doc in range(docs):
            end = end + lengths_ref[row, doc]
            begin = jnp.where(place_q >= end, end, begin)
        place_k = lax.broadcasted_iota(jnp.int32, (high - low, TILE), 0) + low
        allowed = (place_k >= begin) & (place_k <= place_q)
        bias[start : start + high - low, :] = jnp.where(allowed, 0.0, MASKED)


def head_rows(values, head):
    rows = lax.broadcasted_iota(jnp.int32, values.shape, 0) // HEAD_DIM
    return jnp.where(rows == head, values, jnp.zeros_like(values))


def head_cols(values, head):
    cols = lax.broadcasted_iota(jnp.int32, values.shape, 1) // HEAD_DIM
    return jnp.where(cols == head, values, jnp.zeros_like(values))


def staged(bodies, stages, lags):
    held = [None] * len(bodies)
    for step in range(len(bodies) + sum(lags)):
        at = step
        for index, stage in enumerate(stages):
            if 0 <= at < len(bodies):
                held[at] = stage(*bodies[at]) if index == 0 else stage(held[at], *bodies[at])
            if index < len(lags):
                at -= lags[index]


def attend_kernel(lengths_ref, q_ref, k_ref, v_ref, out_ref, lse_ref, bias, mixed, *, row, docs):
    seq_len = q_ref.shape[0]

    @pl.when(pl.program_id(0) == 0)
    def _():
        fill_bias(bias, lengths_ref, row, seq_len, docs)

    query_t = (q_ref[...] * BF(HEAD_DIM**-0.5)).T
    value_t = v_ref[...].T
    query_h = [head_rows(query_t, head) for head in range(2)]

    def scores_of(head, first, low, high, start):
        cols = slice(first, first + TILE)
        scores = nn(k_ref[low:high, :], query_h[head][:, cols]) + bias[start : start + high - low, :]
        return scores, jnp.max(scores, axis=0, keepdims=True)

    def weights_of(held, head, first, low, high, start):
        scores, peak = held
        weights = jnp.exp(scores - peak)
        total = jnp.sum(weights, axis=0, keepdims=True)
        lse_ref[0, head : head + 1, first : first + TILE] = peak + jnp.log(total)
        return weights.astype(BF), 1.0 / total

    def mix(held, head, first, low, high, start):
        weights, scale = held
        rows = slice(head * HEAD_DIM, (head + 1) * HEAD_DIM)
        mixed[rows, first : first + TILE] = nn(value_t[rows, low:high], weights) * scale

    bodies = [(head,) + span for head in range(2) for span in spans(seq_len)[0]]
    staged(bodies, (scores_of, weights_of, mix), (2, 1))
    out_ref[...] = mixed[...].astype(BF).T


def attend_back_kernel(
    lengths_ref,
    q_ref,
    k_ref,
    v_ref,
    out_ref,
    grad_ref,
    lse_ref,
    dq_ref,
    dk_ref,
    dv_ref,
    bias,
    key_sum,
    value_sum,
    query_sum,
    *,
    row,
    docs,
):
    seq_len = q_ref.shape[0]

    @pl.when(pl.program_id(0) == 0)
    def _():
        fill_bias(bias, lengths_ref, row, seq_len, docs)

    query = q_ref[...] * BF(HEAD_DIM**-0.5)
    query_t = query.T
    key_t = k_ref[...].T
    grad = grad_ref[...]
    grad_t = grad.T
    weighted = grad_t.astype(F32) * out_ref[...].T.astype(F32)
    key_sum[...] = jnp.zeros_like(key_sum)
    value_sum[...] = jnp.zeros_like(value_sum)
    query_th = [head_rows(query_t, head) for head in range(2)]
    grad_th = [head_rows(grad_t, head) for head in range(2)]
    query_h = [head_cols(query, head) for head in range(2)]
    grad_h = [head_cols(grad, head) for head in range(2)]
    inner = [
        col_sum(weighted[head * HEAD_DIM : (head + 1) * HEAD_DIM, :]) for head in range(2)
    ]
    bodies = []
    for first, low, high, start in spans(seq_len)[0]:
        for head in range(2):
            for key in range(low, high, TILE):
                bodies.append((head, first, key, start + key - low, key == low))

    def products(head, first, key, start, opening):
        cols, rows = slice(first, first + TILE), slice(key, key + TILE)
        scores = nn(k_ref[rows, :], query_th[head][:, cols]) + bias[start : start + TILE, :]
        return scores, nn(v_ref[rows, :], grad_th[head][:, cols])

    def score_grads(held, head, first, key, start, opening):
        scores, grad_probs = held
        cols = slice(first, first + TILE)
        probs = jnp.exp(scores - lse_ref[0, head : head + 1, cols])
        return probs.astype(BF), (probs * (grad_probs - inner[head][:, cols])).astype(BF)

    def add_grads(held, head, first, key, start, opening):
        probs, grad_scores = held
        cols, rows = slice(first, first + TILE), slice(key, key + TILE)
        value_sum[rows, :] += nn(probs, grad_h[head][cols, :])
        key_sum[rows, :] += nn(grad_scores, query_h[head][cols, :])
        lanes = slice(head * HEAD_DIM, (head + 1) * HEAD_DIM)
        part = nn(key_t[lanes, rows], grad_scores)
        if opening:
            query_sum[lanes, cols] = part
        else:
            query_sum[lanes, cols] += part

    staged(bodies, (products, score_grads, add_grads), (2, 1))
    dq_ref[...] = (query_sum[...] * (HEAD_DIM**-0.5)).astype(BF).T
    dk_ref[...] = key_sum[...].astype(BF)
    dv_ref[...] = value_sum[...].astype(BF)


def out_kernel(table_ref, att_ref, x_ref, vec_ref, *refs):
    sources, (middle_ref, normed_ref, sums_ref, weight, sem) = refs[:SOURCES], refs[SOURCES:]

    @pl.when(pl.program_id(0) == 0)
    def _():
        fill(weight, table_ref, sources, sem, OUT_BLOCKS)
        sums_ref[...] = jnp.zeros_like(sums_ref)

    branch = nn(att_ref[...], weight[...]) + vec_ref[OUT_BIAS : OUT_BIAS + 1]
    middle = x_ref[...].astype(F32) + branch
    middle_ref[...] = middle
    unit, _ = norm_parts(middle)
    normed_ref[...] = (
        unit * vec_ref[LN2_GAIN : LN2_GAIN + 1] + vec_ref[LN2_SHIFT : LN2_SHIFT + 1]
    ).astype(BF)
    sums_ref[0:1] += col_sum(middle * middle)
    sums_ref[1:2] += col_sum(branch * branch)


def put_pieces(keep_ref, send_ref, grad, core, base):
    height, width = keep_ref.shape[-2:]
    for held, ref in enumerate((keep_ref, send_ref)):
        for pair in range(ref.shape[0]):
            piece = 2 * pair + (core ^ held)
            for row in range(2):
                top = pl.multiple_of(row * width + piece * height, 8)
                for col in range(2):
                    ref[pair, base + 2 * row + col] = grad[
                        pl.ds(top, height), col * width : (col + 1) * width
                    ].astype(BF)


def mlp_kernel(table_ref, me_ref, normed_ref, cot_ref, vec_ref, *refs):
    sources, refs = refs[:SOURCES], refs[SOURCES:]
    mlp_ref, back_ref, grad_ref, keep_ref, send_ref, bias_ref = refs[:6]
    fc_tiles, proj_tiles, hidden, grad_pre, whole_grad, sems = refs[6:]
    step = pl.program_id(0)
    width = sources[0].shape[-1]
    ff_cols = FF // width
    tiles = fc_tiles.shape[0]

    @pl.when(step == 0)
    def _():
        for tile in range(tiles):
            at = 2 * tile
            fc_blocks = [(16 + r * ff_cols + at + c, r, c) for r in range(2) for c in range(2)]
            proj_first = 16 + 2 * ff_cols + 2 * at
            proj_blocks = [(proj_first + 2 * r + c, r, c) for r in range(2) for c in range(2)]
            start_fill(fc_tiles.at[tile], table_ref, sources, sems.at[tile], fc_blocks)
            start_fill(proj_tiles.at[tile], table_ref, sources, sems.at[tiles + tile], proj_blocks)

    w_fc, w_proj = fc_tiles.at[step], proj_tiles.at[step]
    wait_fill(w_fc, sems.at[step])
    wait_fill(w_proj, sems.at[tiles + step])
    bias_row = vec_ref[pl.ds(FC_BIAS + step, 1)]

    @pl.when(step == 0)
    def _():
        mlp_ref[...] = jnp.zeros_like(mlp_ref)
        back_ref[...] = jnp.zeros_like(back_ref)

    def entering(rows):
        return nn(normed_ref[rows], w_fc[...]) + bias_row, nt(cot_ref[rows], w_proj[...])

    def activated(held, rows):
        pre, grad = held
        root = 0.7978845608028654
        square = pre * pre
        tanh = jnp.tanh(pre * (root + root * 0.044715 * square))
        half = 0.5 + 0.5 * tanh
        low = (pre * half).astype(BF)
        slope = half + (0.5 * pre) * (1.0 - tanh * tanh) * (root + root * 3.0 * 0.044715 * square)
        back = (grad * slope).astype(BF)
        hidden[rows] = low
        grad_pre[rows] = back
        mlp_ref[rows] += nn(low, w_proj[...])
        back_ref[rows] += nt(back, w_fc[...])
        sums.append(col_sum(back.astype(F32)))

    sums = []
    count = normed_ref.shape[0]
    staged(
        [(slice(row, row + TILE),) for row in range(0, count, TILE)], (entering, activated), (1,)
    )
    bias_ref[0] = sum(sums)
    for base, left, right in ((0, normed_ref, grad_pre), (4, hidden, cot_ref)):
        grad = tn(left[...], right[...])

        @pl.when(step < FIRST_TILES)
        def _():
            pieces, _, _, height, _ = grad_ref.shape
            low = grad.astype(BF)
            for row in range(2):
                for col in range(2):
                    for piece in range(pieces):
                        top = row * width + piece * height
                        grad_ref[piece, 0, base + 2 * row + col] = low[
                            top : top + height, col * width : (col + 1) * width
                        ]

        @pl.when(step >= FIRST_TILES)
        def _():
            whole_grad[...] = grad
            put_pieces(keep_ref, send_ref, whole_grad, me_ref[0] % 2, base)


def middle_kernel(
    table_ref,
    me_ref,
    middle_ref,
    mlp_ref,
    back_ref,
    cot_ref,
    att_ref,
    vec_ref,
    *refs,
):
    sources, refs = refs[:SOURCES], refs[SOURCES:]
    output_ref, grad_ref, grad_att_ref, keep_ref, send_ref, sums_ref = refs[:6]
    weight, branch, out_grad, sem = refs[6:]
    step = pl.program_id(0)

    @pl.when(step == 0)
    def _():
        fill(weight, table_ref, sources, sem, OUT_BLOCKS)
        sums_ref[...] = jnp.zeros_like(sums_ref)

    middle = middle_ref[...]
    mlp = mlp_ref[...] + vec_ref[PROJ_BIAS : PROJ_BIAS + 1]
    result = middle + mlp
    output_ref[...] = result.astype(BF)
    cot = cot_ref[...].astype(F32)
    unit, root = norm_parts(middle)
    back = back_ref[...]
    grad = cot + norm_back(unit, root, vec_ref[LN2_GAIN : LN2_GAIN + 1], back)
    grad_ref[...] = grad
    low = grad.astype(BF)
    branch[pl.ds(pl.multiple_of(step * TILE, TILE), TILE)] = low
    grad_att_ref[...] = nt(low, weight[...]).astype(BF)
    sums_ref[0:1] += col_sum(result * result)
    sums_ref[1:2] += col_sum(mlp * mlp)
    sums_ref[2:3] += col_sum(back * unit)
    sums_ref[3:4] += col_sum(back)
    sums_ref[4:5] += col_sum(low.astype(F32))
    sums_ref[5:6] += col_sum(cot)

    @pl.when(step == pl.num_programs(0) - 1)
    def _():
        out_grad[...] = tn(att_ref[...], branch[...])
        put_pieces(keep_ref, send_ref, out_grad, me_ref[0] % 2, 0)


def weight_back_kernel(
    me_ref, normed_ref, dq_ref, dk_ref, dv_ref, keep_ref, send_ref, sums_ref, grad
):
    step = pl.program_id(0)

    @pl.when(step == 0)
    def _():
        sums_ref[0:1] = col_sum(dq_ref[...].astype(F32))
        sums_ref[1:2] = col_sum(dv_ref[...].astype(F32))

    for part, ref in enumerate((dq_ref, dk_ref, dv_ref)):

        @pl.when(step == part)
        def _():
            grad[...] = tn(normed_ref[...], ref[...])

    put_pieces(keep_ref, send_ref, grad, me_ref[0] % 2, 0)


def input_kernel(table_ref, x_ref, dq_ref, dk_ref, dv_ref, grad_ref, vec_ref, *refs):
    sources, (out_ref, sums_ref, weight, sem) = refs[:SOURCES], refs[SOURCES:]

    @pl.when(pl.program_id(0) == 0)
    def _():
        fill(weight, table_ref, sources, sem, QKV_BLOCKS)
        sums_ref[...] = jnp.zeros_like(sums_ref)

    back = nt(dq_ref[...], weight[:, :D])
    back += nt(dk_ref[...], weight[:, D : 2 * D])
    back += nt(dv_ref[...], weight[:, 2 * D :])
    unit, root = norm_parts(x_ref[...].astype(F32))
    out_ref[...] = grad_ref[...] + norm_back(unit, root, vec_ref[LN1_GAIN : LN1_GAIN + 1], back)
    sums_ref[0:1] += col_sum(back * unit)
    sums_ref[1:2] += col_sum(back)


def lay_kernel(source_ref, *refs):
    out_ref, pieces = refs[-2:]
    begin = 0
    for ref in refs[:-2]:
        pieces[begin : begin + ref.shape[0]] = ref[...]
        begin += ref.shape[0]
    shards, own = out_ref.shape[:2]
    for shard in range(shards):
        for slot in range(own):
            out_ref[shard, slot] = pieces[source_ref[shard * own + slot]]


def factor_kernel(
    shard_ref,
    grad_ref,
    right_ref,
    matrix_ref,
    left_stat_ref,
    right_stat_ref,
    left_root_ref,
    rows_ref,
    left_ref,
    right_new_ref,
    matrix_new_ref,
    whole_grad,
    grad_t,
):
    rows = matrix_ref.shape[1]
    pieces, _, height, _ = grad_ref.shape
    for piece in range(pieces):
        whole_grad[piece * height : (piece + 1) * height, :] = grad_ref[piece, 0]
    grad = whole_grad[...]
    grad_t[...] = grad.T
    own = pl.ds(pl.multiple_of(shard_ref[0] * rows, rows), rows)
    grad_rows = whole_grad[own, :]
    rows_ref[0] = grad_rows.astype(F32)
    left_ref[0] = DECAY * left_stat_ref[0] + (1.0 - DECAY) * nn(grad_rows, grad_t[...])
    right_new_ref[0] = DECAY * right_stat_ref[0] + (1.0 - DECAY) * nn(grad_t[own, :], grad)
    half = nn(left_root_ref[0].astype(BF), grad)
    update = nn(half.astype(BF), right_ref[0])
    matrix_new_ref[0] = matrix_ref[0] - MATRIX_RATE * update


def core_sum_kernel(*refs):
    out_ref = refs[-1]
    begin = 0
    for keep, sent in zip(refs[:-1:2], refs[1:-1:2]):
        blocks = keep.shape[1]
        out_ref[0, begin : begin + blocks] = (keep[0].astype(F32) + sent[0].astype(F32)).astype(BF)
        begin += blocks


def across_dp(values, bit):
    count = lax.axis_size("dp")
    return lax.ppermute(values, "dp", [(i, i ^ (1 << bit)) for i in range(count)])


def across_fsdp(values, offset):
    count = lax.axis_size("fsdp")
    return lax.ppermute(values, "fsdp", [(i, i ^ offset) for i in range(count)])


def gather_by_permutes(values, me, shard):
    fsdp_count, dp_count = lax.axis_size("fsdp"), lax.axis_size("dp")
    held = jnp.stack([values] + [across_fsdp(values, k) for k in range(1, fsdp_count)])
    for bit in range(dp_count.bit_length() - 1):
        held = jnp.stack([held, across_dp(held, bit)])
    held = held.reshape((dp_count, fsdp_count) + values.shape)
    held = jnp.take(held, jnp.arange(dp_count) ^ me, axis=0)
    held = jnp.take(held, jnp.arange(fsdp_count) ^ shard, axis=1)
    return held.transpose(2, 0, 1, 3, 4).reshape((-1,) + values.shape[1:])


def core_sum(grads, name, ties=()):
    ins = []
    for keep, send in grads:
        ins += [keep, across_dp(send, 0)]
    pairs = ins[0].shape[0]
    rest = ins[0].shape[2:]
    blocks = sum(keep.shape[1] for keep, _ in grads)

    def one(array):
        return (array, (1,) + array.shape[1:], lambda i: (i, 0, 0, 0))

    return call(
        core_sum_kernel,
        (pairs,),
        [one(array) for array in ins],
        [((pairs, blocks) + rest, BF, (1, blocks) + rest, lambda i: (i, 0, 0, 0))],
        ties=ties,
        name=name,
    )[0]


def plane_parts(values):
    pairs = lax.axis_size("dp") // 2
    groups = [[2 * pair + core for pair in range(pairs)] for core in range(2)]
    return lax.all_to_all(values, "dp", 0, 0, axis_index_groups=groups, tiled=True)


def dp_sum(values):
    for bit in range(lax.axis_size("dp").bit_length() - 1):
        values = values + across_dp(values, bit)
    return values


def fsdp_sum(values):
    offset = 1
    while offset < lax.axis_size("fsdp"):
        values = values + across_fsdp(values, offset)
        offset *= 2
    return values


def per_device(
    tokens,
    cotangent,
    doc_lengths,
    block_slot,
    matrices,
    vectors,
    vector_second,
    left_stat,
    right_stat,
    left_root,
    right_root,
):
    dp_count = lax.axis_size("dp")
    fsdp_count = lax.axis_size("fsdp")
    own_blocks, own_rows, width = matrices.shape
    blocks = own_blocks * dp_count
    height = width // dp_count
    me = lax.axis_index("dp").astype(jnp.int32).reshape(1)
    shard = lax.axis_index("fsdp").astype(jnp.int32).reshape(1)
    half = lax.axis_index("fsdp")
    half = sum((half >> bit) & 1 for bit in range(fsdp_count.bit_length())) % 2
    half = half.astype(jnp.int32).reshape(1)
    numbers = jnp.arange(blocks, dtype=jnp.int32)
    holder = block_slot // own_blocks
    before = (holder[None, :] == holder[:, None]) & (numbers[None, :] < numbers[:, None])
    rank = jnp.sum(before.astype(jnp.int32), axis=1)
    early = max(2, 2 * own_blocks // 3 // 2 * 2)
    here = jnp.arange(own_blocks, dtype=jnp.int32)
    mine = (holder == me[0]) & (rank[None, :] == here[:, None])
    local = jnp.sum(jnp.where(mine, block_slot[None, :] % own_blocks, 0), axis=1)
    low = jnp.take(matrices, local, axis=0).astype(BF)
    late = lax.all_gather(low[early:], ("dp", "fsdp"), axis=1, tiled=True)
    late = late.reshape(-1, own_rows, width)
    right_whole = lax.all_gather(right_root.astype(BF), "fsdp", axis=1, tiled=True)

    line = jnp.stack([low[:early]] + [across_fsdp(low[:early], k) for k in range(1, fsdp_count)])
    plane_bits = list(range(1, dp_count.bit_length() - 1))
    sources, plane_places = [], []
    rel = holder ^ me[0]
    last_bits = []
    for part, order in enumerate((plane_bits, plane_bits[::-1])):
        held = line[:, part * early // 2 : (part + 1) * early // 2]
        for bit in order[:-1]:
            held = jnp.stack([held, across_dp(held, bit)])
        other = across_dp(held, order[-1])
        sources += [held, other, across_dp(held, 0), across_dp(other, 0)]
        plane_places.append(sum(((rel >> bit) & 1) << i for i, bit in enumerate(order[:-1])))
        last_bits.append((rel >> order[-1]) & 1)
    sources = [source.reshape(-1, own_rows, width) for source in sources]
    units = jnp.arange(fsdp_count, dtype=jnp.int32)[None, :]
    second_half = (rank >= early // 2).astype(jnp.int32)
    plane_place = jnp.where(second_half == 1, plane_places[1], plane_places[0])[:, None]
    inside = (rank - second_half * (early // 2))[:, None]
    early_index = (plane_place * fsdp_count + (units ^ shard[0])) * (early // 2) + inside
    late_index = ((rank[:, None] - early) * dp_count + holder[:, None]) * fsdp_count + units
    is_late = rank[:, None] >= early
    last_bit = jnp.where(second_half == 1, last_bits[1], last_bits[0])
    early_source = second_half * 4 + (rel & 1) * 2 + last_bit
    source_at = jnp.where(is_late, SOURCES - 1, early_source[:, None] + 0 * units)
    table = jnp.concatenate(
        [source_at.reshape(-1), jnp.where(is_late, late_index, early_index).reshape(-1)]
    ).astype(jnp.int32)
    qkv_early = jnp.max(rank[:12]) < early

    vec = vectors.reshape(-1, D)
    count = tokens.shape[0]
    rows_here, docs = doc_lengths.shape
    seq_len = count // rows_here
    steps = count // TILE

    def from_units(last):
        return [(source, None, None) for source in sources + [last]]

    def qkv(last):
        return tuple(
            call(
                qkv_kernel,
                (steps,),
                [tokens_in(tokens), whole(vec)] + from_units(last),
                [
                    ((count, D), BF, (TILE, D), lambda i, *_: (i, 0)),
                    ((count, 3 * D), BF, (TILE, 3 * D), lambda i, *_: (i, 0)),
                ],
                [pltpu.VMEM((D, 3 * D), BF), pltpu.SemaphoreType.DMA],
                scalars=[table],
                name="qkv",
            )
        )

    def qkv_with_late():
        return qkv(gather_by_permutes(low[early:], me[0], shard[0]))

    normed1, projected = lax.cond(qkv_early, lambda: qkv(sources[0]), qkv_with_late)
    weights_in = from_units(late)

    pairs = HEADS // 2
    bias_rows = spans(seq_len)[1]

    def pair_in(array, row, offset):
        return (array, (seq_len, PAIR), lambda p, *_: (row, offset + p))

    attended, lses = [], []
    for row in range(rows_here):
        one, lse = call(
            functools.partial(attend_kernel, row=row, docs=docs),
            (pairs,),
            [pair_in(projected, row, part * pairs) for part in range(3)],
            [
                ((seq_len, D), BF, (seq_len, PAIR), lambda p, *_: (0, p)),
                ((pairs, 2, seq_len), F32, (1, 2, seq_len), lambda p, *_: (p, 0, 0)),
            ],
            [pltpu.VMEM((bias_rows, TILE), F32), pltpu.VMEM((PAIR, seq_len), F32)],
            scalars=[doc_lengths],
            name="attend",
        )
        attended.append(one)
        lses.append(lse)
    attended = attended[0] if rows_here == 1 else jnp.concatenate(attended, axis=0)

    middle, normed2, sums_mid = call(
        out_kernel,
        (steps,),
        [tokens_in(attended), tokens_in(tokens), whole(vec)] + weights_in,
        [
            ((count, D), F32, (TILE, D), lambda i, *_: (i, 0)),
            ((count, D), BF, (TILE, D), lambda i, *_: (i, 0)),
            out_whole((8, D), F32),
        ],
        [pltpu.VMEM((D, D), BF), pltpu.SemaphoreType.DMA],
        scalars=[table],
        name="attn_out",
    )

    ff_cols = FF // width
    pair_count = dp_count // 2
    tiles = FF // D
    mlp, back2, grads, keep, send, fc_sums = call(
        mlp_kernel,
        (tiles,),
        [whole(normed2), whole(cotangent), whole(vec)] + weights_in,
        [
            out_whole((count, D), F32),
            out_whole((count, D), F32),
            (
                (dp_count, FIRST_TILES, 8, height, width),
                BF,
                (dp_count, 1, 8, height, width),
                lambda t, *_: (0, jnp.minimum(t, FIRST_TILES - 1), 0, 0, 0),
            ),
        ]
        + [
            (
                (pair_count, (tiles - FIRST_TILES) * 8, height, width),
                BF,
                (pair_count, 8, height, width),
                lambda t, *_: (0, jnp.maximum(t - FIRST_TILES, 0), 0, 0),
            )
        ]
        * 2
        + [((tiles, 1, D), F32, (1, 1, D), lambda t, *_: (t, 0, 0))],
        [pltpu.VMEM((tiles, D, D), BF)] * 2
        + [pltpu.VMEM((count, D), BF)] * 2
        + [pltpu.VMEM((D, D), F32), pltpu.SemaphoreType.DMA((2 * tiles,))],
        scalars=[table, me],
        name="mlp",
    )
    mlp_grads = (keep, send)
    first_grads = lax.psum_scatter(
        grads.reshape(-1, width), "dp", scatter_dimension=0, tiled=True
    )

    output, grad_middle, grad_attended, *out_grads, sums_back = call(
        middle_kernel,
        (steps,),
        [
            tokens_in(middle),
            tokens_in(mlp),
            tokens_in(back2),
            tokens_in(cotangent),
            whole(attended),
            whole(vec),
        ]
        + weights_in,
        [
            ((count, D), BF, (TILE, D), lambda i, *_: (i, 0)),
            ((count, D), F32, (TILE, D), lambda i, *_: (i, 0)),
            ((count, D), BF, (TILE, D), lambda i, *_: (i, 0)),
            out_whole((pair_count, 4, height, width), BF),
            out_whole((pair_count, 4, height, width), BF),
            out_whole((8, D), F32),
        ],
        [
            pltpu.VMEM((D, D), BF),
            pltpu.VMEM((count, D), BF),
            pltpu.VMEM((D, D), F32),
            pltpu.SemaphoreType.DMA,
        ],
        scalars=[table, me],
        ties=[right_whole],
        name="middle_back",
    )

    second_core = core_sum([mlp_grads, out_grads], "second_core")
    second_parts = plane_parts(second_core)
    def attend_back(row, begin, stop, onto, ties):
        return call(
            functools.partial(attend_back_kernel, row=row, docs=docs),
            (stop - begin,),
            [pair_in(projected, row, part * pairs + begin) for part in range(3)]
            + [
                pair_in(attended, row, begin),
                pair_in(grad_attended, row, begin),
                (lses[row], (1, 2, seq_len), lambda p, *_: (p + begin, 0, 0)),
            ],
            [((count, D), BF, (seq_len, PAIR), lambda p, *_: (row, p + begin))] * 3,
            [
                pltpu.VMEM((bias_rows, TILE), F32),
                pltpu.VMEM((seq_len, PAIR), F32),
                pltpu.VMEM((seq_len, PAIR), F32),
                pltpu.VMEM((PAIR, seq_len), F32),
            ],
            scalars=[doc_lengths],
            ties=ties,
            onto=onto,
            name="attend_back",
        )

    grads = ()
    for row in range(rows_here):
        grads = attend_back(row, 0, pairs // 2, grads, [second_core])
        grads = attend_back(row, pairs // 2, pairs, grads, [])
    dq, dk, dv = grads

    half_shape = (pair_count, 12, height, width)
    keep, send, sums_qkv = call(
        weight_back_kernel,
        (3,),
        [whole(array) for array in (normed1, dq, dk, dv)],
        [(half_shape, BF, (pair_count, 4, height, width), lambda p, *_: (0, p, 0, 0))] * 2
        + [out_whole((8, D), F32)],
        [pltpu.VMEM((D, D), F32)],
        scalars=[me],
        name="qkv_weight_back",
    )
    third_core = core_sum([(keep, send)], "third_core")
    second_halves = plane_sum(second_parts, half, [], "second_plane")
    third_parts = plane_parts(third_core)

    x_grad, sums_in = call(
        input_kernel,
        (steps,),
        [
            tokens_in(tokens),
            tokens_in(dq),
            tokens_in(dk),
            tokens_in(dv),
            tokens_in(grad_middle),
            whole(vec),
        ]
        + weights_in,
        [((count, D), F32, (TILE, D), lambda i, *_: (i, 0)), out_whole((8, D), F32)],
        [pltpu.VMEM((D, 3 * D), BF), pltpu.SemaphoreType.DMA],
        scalars=[table],
        ties=[second_halves[0], third_core],
        name="input_back",
    )

    second_half = line_half(second_halves, [x_grad], "second_half")
    first_halves = plane_sum(
        first_grads.reshape(1, -1, height, width), half, [second_half], "first_split"
    )
    first_half = line_half(first_halves, [], "first_half")
    first_total = line_rest(first_half, [], "first_rest")
    second_total = line_rest(second_half, [], "second_rest")
    vector_local = call(
        pack_kernel,
        (1,),
        [whole(array) for array in (sums_in, sums_qkv, sums_back, sums_mid, fc_sums)],
        [out_whole((16, D), F32)],
        name="pack",
    )[0]
    vector_plane = dp_sum(vector_local)
    vector_sums = fsdp_sum(vector_plane)
    third_halves = plane_sum(third_parts, half, [second_half, first_halves[0]], "third_plane")
    third_total = line_rest(line_half(third_halves, [], "third_half"), [], "third_rest")
    vector_grad = vector_sums[:12].reshape(-1)
    square_sums = vector_sums[12, :4]

    order = []
    for tile in range(FF // D):
        order += [16 + r * ff_cols + 2 * tile + c for r in range(2) for c in range(2)]
        order += [16 + 2 * ff_cols + 2 * (2 * tile + r) + c for r in range(2) for c in range(2)]
    order += list(range(12, 16))
    order += [r * 6 + 2 * part + c for part in range(3) for r in range(2) for c in range(2)]
    standing = jnp.array([order.index(u) for u in range(blocks)], jnp.int32)
    source = jnp.sum(
        jnp.where(block_slot[None, :] == numbers[:, None], standing[None, :], 0), axis=1
    )
    begin = 0
    spread = []
    for total in (first_total, second_total, third_total):
        size = total.shape[0]
        inside = source - begin
        moved = begin + (inside // size ^ half[0]) * size + inside % size
        source = jnp.where((inside >= 0) & (inside < size * 2), moved, source)
        begin += size * 2
        spread += line_spread(total)
    laid = call(
        lay_kernel,
        (1,),
        [whole(array) for array in spread],
        [out_whole((dp_count, own_blocks, height, width), BF)],
        [pltpu.VMEM((blocks, height, width), BF)],
        scalars=[source],
        ties=[vector_plane],
        name="lay",
    )[0]
    grad_whole = lax.all_to_all(laid, "dp", 0, 0, tiled=True)

    def block_in(array):
        return (array, (1,) + array.shape[1:], lambda b, *_: (b, 0, 0))

    matrix_grad, left_new, right_new, matrix_new = call(
        factor_kernel,
        (own_blocks,),
        [(grad_whole, (dp_count, 1, height, width), lambda b, *_: (0, b, 0, 0))]
        + [block_in(a) for a in (right_whole, matrices, left_stat, right_stat, left_root)],
        [(matrices.shape, F32, (1, own_rows, width), lambda b, *_: (b, 0, 0))] * 4,
        [pltpu.VMEM((width, width), BF)] * 2,
        scalars=[shard],
        name="factor",
    )

    residual_scale = jnp.sqrt(square_sums / (count * dp_count * fsdp_count * D))
    second_new = DECAY * vector_second + (1.0 - DECAY) * vector_grad * vector_grad
    vector_new = vectors - VECTOR_RATE * vector_grad / (jnp.sqrt(second_new) + ROOT_EPSILON)
    return (
        output,
        x_grad,
        matrix_grad,
        left_new,
        right_new,
        matrix_new,
        vector_grad,
        second_new,
        vector_new,
        residual_scale,
    )


def solution(mesh):
    tokens = P(("dp", "fsdp"), None)
    stored = P("dp", "fsdp", None)
    return jax.shard_map(
        per_device,
        mesh=mesh,
        in_specs=(tokens, tokens, tokens, P(), stored, P(), P()) + (stored,) * 4,
        out_specs=(tokens, tokens) + (stored,) * 4 + (P(),) * 4,
        check_vma=False,
    )
```

```python
import functools

import jax
import jax.numpy as jnp
from jax import lax
from jax.experimental import pallas as pl
from jax.experimental.pallas import tpu as pltpu
from jax.sharding import PartitionSpec as P

D = 768
HEADS = 12
HEAD_DIM = 64
FF = 3072
LONGEST = 512

NORM_EPSILON = 1e-05
ROOT_EPSILON = 1e-08
DECAY = 0.5
MATRIX_RATE = 1.5
VECTOR_RATE = 0.1
MASKED = -1e30

BF = jnp.bfloat16
F32 = jnp.float32
PAIR = 2 * HEAD_DIM
TILE = 256
VMEM = 60 * 1024 * 1024
FIRST_TILES = 2

LN1_GAIN, LN1_SHIFT, Q_BIAS, V_BIAS, OUT_BIAS, LN2_GAIN, LN2_SHIFT, PROJ_BIAS, FC_BIAS = range(9)


def nn(left, right):
    return jnp.dot(left, right, preferred_element_type=F32)


def nt(left, right):
    return lax.dot_general(left, right, (((1,), (1,)), ((), ())), preferred_element_type=F32)


def tn(left, right):
    return lax.dot_general(left, right, (((0,), (0,)), ((), ())), preferred_element_type=F32)


def col_sum(values):
    return jnp.sum(values, axis=0, keepdims=True)


def norm_parts(values):
    center = values - jnp.mean(values, axis=-1, keepdims=True)
    spread = jnp.mean(center * center, axis=-1, keepdims=True)
    root = lax.rsqrt(spread + NORM_EPSILON)
    return center * root, root


def norm_back(unit, root, gain, grad):
    scaled = grad * gain
    return root * (
        scaled
        - jnp.mean(scaled, axis=-1, keepdims=True)
        - unit * jnp.mean(scaled * unit, axis=-1, keepdims=True)
    )


def start_fill(weight, table_ref, sources, sem, blocks):
    _, height, width = sources[0].shape
    units = width // height
    half = table_ref.shape[0] // 2
    for number, row, col in blocks:
        at = number * units
        source = table_ref[at]
        for which, ref in enumerate(sources):

            @pl.when(source == which)
            def _():
                for unit in range(units):
                    top = row * width + unit * height
                    target = weight.at[pl.ds(top, height), pl.ds(col * width, width)]
                    pltpu.make_async_copy(ref.at[table_ref[half + at + unit]], target, sem).start()


def wait_fill(weight, sem):
    pltpu.make_async_copy(weight, weight, sem).wait()


def fill(weight, table_ref, sources, sem, blocks):
    start_fill(weight, table_ref, sources, sem, blocks)
    wait_fill(weight, sem)


QKV_BLOCKS = [(row * 6 + col, row, col) for row in range(2) for col in range(6)]
OUT_BLOCKS = [(12 + row * 2 + col, row, col) for row in range(2) for col in range(2)]
SOURCES = 9


def call(kernel, grid, ins, outs, scratch=(), scalars=(), ties=(), onto=(), name=None):
    first = len(scalars) + len(ins)
    ties = list(onto) + list(ties)

    def body(*refs):
        kernel(*refs[:first], *refs[first + len(ties) :])

    spec = pltpu.PrefetchScalarGridSpec(
        num_scalar_prefetch=len(scalars),
        grid=grid,
        in_specs=[
            pl.BlockSpec(memory_space=pltpu.HBM) if block is None else pl.BlockSpec(block, index)
            for _, block, index in ins
        ]
        + [pl.BlockSpec(memory_space=pl.ANY)] * len(ties),
        out_specs=[pl.BlockSpec(block, index) for _, _, block, index in outs],
        scratch_shapes=list(scratch),
    )
    return pl.pallas_call(
        body,
        grid_spec=spec,
        out_shape=[jax.ShapeDtypeStruct(shape, dtype) for shape, dtype, _, _ in outs],
        compiler_params=pltpu.CompilerParams(
            dimension_semantics=("arbitrary",) * len(grid), vmem_limit_bytes=VMEM
        ),
        cost_estimate=pl.CostEstimate(flops=1024, bytes_accessed=1024, transcendentals=0),
        input_output_aliases={first + place: place for place in range(len(onto))},
        name=name,
    )(*scalars, *[array for array, _, _ in ins], *ties)


def whole(array):
    return (array, array.shape, lambda *_: (0,) * array.ndim)


def tokens_in(array, cols=None):
    return (array, (TILE, cols or array.shape[1]), lambda i, *_: (i, 0))


def out_whole(shape, dtype):
    return (shape, dtype, shape, lambda *_: (0,) * len(shape))


def plane_sum_kernel(half_ref, *refs):
    half = len(refs) // 2
    for parts, out in zip(refs[:half], refs[half:]):
        total = parts[0].astype(F32)
        for part in range(1, parts.shape[0]):
            total = total + parts[part].astype(F32)
        out[...] = total.astype(BF)


def plane_sum(parts, half, ties, name):
    count, blocks, height, width = parts.shape
    size = blocks // 2

    def group(offset):
        return (parts, (count, size, height, width), lambda i, at: (0, at[0] ^ offset, 0, 0))

    return call(
        plane_sum_kernel,
        (1,),
        [group(0), group(1)],
        [out_whole((size, height, width), BF)] * 2,
        scalars=[half],
        ties=ties,
        name=name,
    )


def add_kernel(left_ref, right_ref, out_ref):
    out_ref[...] = (left_ref[...].astype(F32) + right_ref[...].astype(F32)).astype(BF)


def add_up(left, right, ties, name):
    return call(
        add_kernel,
        (1,),
        [whole(left), whole(right)],
        [out_whole(left.shape, BF)],
        ties=ties,
        name=name,
    )[0]


def line_half(halves, ties, name):
    return add_up(halves[0], across_fsdp(halves[1], 1), ties, name)


def line_rest(total, ties, name):
    offset = 3
    while offset <= lax.axis_size("fsdp"):
        total = add_up(total, across_fsdp(total, offset), ties, name)
        offset = 2 * offset - 1
    return total


def line_spread(total):
    return [total, across_fsdp(total, 1)]


def pack_kernel(in_ref, qkv_ref, back_ref, mid_ref, *refs):
    fc_refs, out_ref = refs[:-1], refs[-1]
    out_ref[0:2] = in_ref[0:2]
    out_ref[2:4] = qkv_ref[0:2]
    out_ref[4:5] = back_ref[4:5]
    out_ref[5:7] = back_ref[2:4]
    out_ref[7:8] = back_ref[5:6]
    row = 8
    for ref in fc_refs:
        for tile in range(ref.shape[0]):
            out_ref[row : row + 1] = ref[tile]
            row += 1
    lanes = lax.broadcasted_iota(jnp.int32, (1, D), 1)
    line = jnp.zeros((1, D), F32)
    for lane, value in enumerate((mid_ref[0:1], back_ref[0:1], mid_ref[1:2], back_ref[1:2])):
        line = jnp.where(lanes == lane, jnp.sum(value), line)
    out_ref[row : row + 1] = line
    out_ref[row + 1 :] = jnp.zeros_like(out_ref[row + 1 :])


def qkv_kernel(table_ref, x_ref, vec_ref, *refs):
    sources, (normed_ref, projected_ref, weight, sem) = refs[:SOURCES], refs[SOURCES:]

    @pl.when(pl.program_id(0) == 0)
    def _():
        fill(weight, table_ref, sources, sem, QKV_BLOCKS)

    unit, _ = norm_parts(x_ref[...].astype(F32))
    normed = (unit * vec_ref[LN1_GAIN : LN1_GAIN + 1] + vec_ref[LN1_SHIFT : LN1_SHIFT + 1]).astype(
        BF
    )
    normed_ref[...] = normed
    for part in range(3):
        cols = slice(part * D, (part + 1) * D)
        value = nn(normed, weight[:, cols])
        if part != 1:
            row = Q_BIAS if part == 0 else V_BIAS
            value = value + vec_ref[row : row + 1]
        projected_ref[:, cols] = value.astype(BF)


def spans(seq_len):
    out = []
    start = 0
    for first in range(0, seq_len, TILE):
        low = max(0, first - LONGEST)
        out.append((first, low, first + TILE, start))
        start += first + TILE - low
    return out, start


def fill_bias(bias, lengths_ref, row, seq_len, docs):
    for first, low, high, start in spans(seq_len)[0]:
        place_q = lax.broadcasted_iota(jnp.int32, (1, TILE), 1) + first
        begin = jnp.zeros((1, TILE), jnp.int32)
        end = jnp.int32(0)
        for doc in range(docs):
            end = end + lengths_ref[row, doc]
            begin = jnp.where(place_q >= end, end, begin)
        place_k = lax.broadcasted_iota(jnp.int32, (high - low, TILE), 0) + low
        allowed = (place_k >= begin) & (place_k <= place_q)
        bias[start : start + high - low, :] = jnp.where(allowed, 0.0, MASKED)


def head_rows(values, head):
    rows = lax.broadcasted_iota(jnp.int32, values.shape, 0) // HEAD_DIM
    return jnp.where(rows == head, values, jnp.zeros_like(values))


def head_cols(values, head):
    cols = lax.broadcasted_iota(jnp.int32, values.shape, 1) // HEAD_DIM
    return jnp.where(cols == head, values, jnp.zeros_like(values))


def staged(bodies, stages, lags):
    held = [None] * len(bodies)
    for step in range(len(bodies) + sum(lags)):
        at = step
        for index, stage in enumerate(stages):
            if 0 <= at < len(bodies):
                held[at] = stage(*bodies[at]) if index == 0 else stage(held[at], *bodies[at])
            if index < len(lags):
                at -= lags[index]


def attend_kernel(lengths_ref, q_ref, k_ref, v_ref, out_ref, lse_ref, bias, mixed, *, row, docs):
    seq_len = q_ref.shape[0]

    @pl.when(pl.program_id(0) == 0)
    def _():
        fill_bias(bias, lengths_ref, row, seq_len, docs)

    query_t = (q_ref[...] * BF(HEAD_DIM**-0.5)).T
    value_t = v_ref[...].T
    query_h = [head_rows(query_t, head) for head in range(2)]

    def scores_of(head, first, low, high, start):
        cols = slice(first, first + TILE)
        scores = nn(k_ref[low:high, :], query_h[head][:, cols]) + bias[start : start + high - low, :]
        return scores, jnp.max(scores, axis=0, keepdims=True)

    def weights_of(held, head, first, low, high, start):
        scores, peak = held
        weights = jnp.exp(scores - peak)
        total = jnp.sum(weights, axis=0, keepdims=True)
        lse_ref[0, head : head + 1, first : first + TILE] = peak + jnp.log(total)
        return weights.astype(BF), 1.0 / total

    def mix(held, head, first, low, high, start):
        weights, scale = held
        rows = slice(head * HEAD_DIM, (head + 1) * HEAD_DIM)
        mixed[rows, first : first + TILE] = nn(value_t[rows, low:high], weights) * scale

    bodies = [(head,) + span for head in range(2) for span in spans(seq_len)[0]]
    staged(bodies, (scores_of, weights_of, mix), (2, 1))
    out_ref[...] = mixed[...].astype(BF).T


def attend_back_kernel(
    lengths_ref,
    q_ref,
    k_ref,
    v_ref,
    out_ref,
    grad_ref,
    lse_ref,
    dq_ref,
    dk_ref,
    dv_ref,
    bias,
    key_sum,
    value_sum,
    query_sum,
    *,
    row,
    docs,
):
    seq_len = q_ref.shape[0]

    @pl.when(pl.program_id(0) == 0)
    def _():
        fill_bias(bias, lengths_ref, row, seq_len, docs)

    query = q_ref[...] * BF(HEAD_DIM**-0.5)
    query_t = query.T
    key_t = k_ref[...].T
    grad = grad_ref[...]
    grad_t = grad.T
    weighted = grad_t.astype(F32) * out_ref[...].T.astype(F32)
    key_sum[...] = jnp.zeros_like(key_sum)
    value_sum[...] = jnp.zeros_like(value_sum)
    query_th = [head_rows(query_t, head) for head in range(2)]
    grad_th = [head_rows(grad_t, head) for head in range(2)]
    query_h = [head_cols(query, head) for head in range(2)]
    grad_h = [head_cols(grad, head) for head in range(2)]
    inner = [
        col_sum(weighted[head * HEAD_DIM : (head + 1) * HEAD_DIM, :]) for head in range(2)
    ]
    bodies = []
    for first, low, high, start in spans(seq_len)[0]:
        for head in range(2):
            for key in range(low, high, TILE):
                bodies.append((head, first, key, start + key - low, key == low))

    def products(head, first, key, start, opening):
        cols, rows = slice(first, first + TILE), slice(key, key + TILE)
        scores = nn(k_ref[rows, :], query_th[head][:, cols]) + bias[start : start + TILE, :]
        return scores, nn(v_ref[rows, :], grad_th[head][:, cols])

    def score_grads(held, head, first, key, start, opening):
        scores, grad_probs = held
        cols = slice(first, first + TILE)
        probs = jnp.exp(scores - lse_ref[0, head : head + 1, cols])
        return probs.astype(BF), (probs * (grad_probs - inner[head][:, cols])).astype(BF)

    def add_grads(held, head, first, key, start, opening):
        probs, grad_scores = held
        cols, rows = slice(first, first + TILE), slice(key, key + TILE)
        value_sum[rows, :] += nn(probs, grad_h[head][cols, :])
        key_sum[rows, :] += nn(grad_scores, query_h[head][cols, :])
        lanes = slice(head * HEAD_DIM, (head + 1) * HEAD_DIM)
        part = nn(key_t[lanes, rows], grad_scores)
        if opening:
            query_sum[lanes, cols] = part
        else:
            query_sum[lanes, cols] += part

    staged(bodies, (products, score_grads, add_grads), (2, 1))
    dq_ref[...] = (query_sum[...] * (HEAD_DIM**-0.5)).astype(BF).T
    dk_ref[...] = key_sum[...].astype(BF)
    dv_ref[...] = value_sum[...].astype(BF)


def out_kernel(table_ref, att_ref, x_ref, vec_ref, *refs):
    sources, (middle_ref, normed_ref, sums_ref, weight, sem) = refs[:SOURCES], refs[SOURCES:]

    @pl.when(pl.program_id(0) == 0)
    def _():
        fill(weight, table_ref, sources, sem, OUT_BLOCKS)
        sums_ref[...] = jnp.zeros_like(sums_ref)

    branch = nn(att_ref[...], weight[...]) + vec_ref[OUT_BIAS : OUT_BIAS + 1]
    middle = x_ref[...].astype(F32) + branch
    middle_ref[...] = middle
    unit, _ = norm_parts(middle)
    normed_ref[...] = (
        unit * vec_ref[LN2_GAIN : LN2_GAIN + 1] + vec_ref[LN2_SHIFT : LN2_SHIFT + 1]
    ).astype(BF)
    sums_ref[0:1] += col_sum(middle * middle)
    sums_ref[1:2] += col_sum(branch * branch)


def put_pieces(keep_ref, send_ref, grad, core, base):
    height, width = keep_ref.shape[-2:]
    for held, ref in enumerate((keep_ref, send_ref)):
        for pair in range(ref.shape[0]):
            piece = 2 * pair + (core ^ held)
            for row in range(2):
                top = pl.multiple_of(row * width + piece * height, 8)
                for col in range(2):
                    ref[pair, base + 2 * row + col] = grad[
                        pl.ds(top, height), col * width : (col + 1) * width
                    ].astype(BF)


def mlp_kernel(table_ref, me_ref, normed_ref, cot_ref, vec_ref, *refs):
    sources, refs = refs[:SOURCES], refs[SOURCES:]
    mlp_ref, back_ref, grad_ref, keep_ref, send_ref, bias_ref = refs[:6]
    fc_tiles, proj_tiles, hidden, grad_pre, whole_grad, sems = refs[6:]
    step = pl.program_id(0)
    width = sources[0].shape[-1]
    ff_cols = FF // width
    tiles = fc_tiles.shape[0]

    @pl.when(step == 0)
    def _():
        for tile in range(tiles):
            at = 2 * tile
            fc_blocks = [(16 + r * ff_cols + at + c, r, c) for r in range(2) for c in range(2)]
            proj_first = 16 + 2 * ff_cols + 2 * at
            proj_blocks = [(proj_first + 2 * r + c, r, c) for r in range(2) for c in range(2)]
            start_fill(fc_tiles.at[tile], table_ref, sources, sems.at[tile], fc_blocks)
            start_fill(proj_tiles.at[tile], table_ref, sources, sems.at[tiles + tile], proj_blocks)

    w_fc, w_proj = fc_tiles.at[step], proj_tiles.at[step]
    wait_fill(w_fc, sems.at[step])
    wait_fill(w_proj, sems.at[tiles + step])
    bias_row = vec_ref[pl.ds(FC_BIAS + step, 1)]

    @pl.when(step == 0)
    def _():
        mlp_ref[...] = jnp.zeros_like(mlp_ref)
        back_ref[...] = jnp.zeros_like(back_ref)

    def entering(rows):
        return nn(normed_ref[rows], w_fc[...]) + bias_row, nt(cot_ref[rows], w_proj[...])

    def activated(held, rows):
        pre, grad = held
        root = 0.7978845608028654
        square = pre * pre
        tanh = jnp.tanh(pre * (root + root * 0.044715 * square))
        half = 0.5 + 0.5 * tanh
        low = (pre * half).astype(BF)
        slope = half + (0.5 * pre) * (1.0 - tanh * tanh) * (root + root * 3.0 * 0.044715 * square)
        back = (grad * slope).astype(BF)
        hidden[rows] = low
        grad_pre[rows] = back
        mlp_ref[rows] += nn(low, w_proj[...])
        back_ref[rows] += nt(back, w_fc[...])
        sums.append(col_sum(back.astype(F32)))

    sums = []
    count = normed_ref.shape[0]
    staged(
        [(slice(row, row + TILE),) for row in range(0, count, TILE)], (entering, activated), (1,)
    )
    bias_ref[0] = sum(sums)
    whole_grad[0] = tn(normed_ref[...], grad_pre[...])
    whole_grad[1] = tn(hidden[...], cot_ref[...])

    @pl.when(step < FIRST_TILES)
    def _():
        pieces, _, _, height, _ = grad_ref.shape
        for base in range(2):
            for row in range(2):
                for col in range(2):
                    for piece in range(pieces):
                        top = row * width + piece * height
                        grad_ref[piece, 0, 4 * base + 2 * row + col] = whole_grad[
                            base, top : top + height, col * width : (col + 1) * width
                        ].astype(BF)

    @pl.when(step >= FIRST_TILES)
    def _():
        for base in range(2):
            put_pieces(keep_ref, send_ref, whole_grad.at[base], me_ref[0] % 2, 4 * base)


def middle_kernel(
    table_ref,
    me_ref,
    middle_ref,
    mlp_ref,
    back_ref,
    cot_ref,
    att_ref,
    vec_ref,
    *refs,
):
    sources, refs = refs[:SOURCES], refs[SOURCES:]
    output_ref, grad_ref, grad_att_ref, keep_ref, send_ref, sums_ref = refs[:6]
    weight, branch, out_grad, sem = refs[6:]
    step = pl.program_id(0)

    @pl.when(step == 0)
    def _():
        fill(weight, table_ref, sources, sem, OUT_BLOCKS)
        sums_ref[...] = jnp.zeros_like(sums_ref)

    middle = middle_ref[...]
    mlp = mlp_ref[...] + vec_ref[PROJ_BIAS : PROJ_BIAS + 1]
    result = middle + mlp
    output_ref[...] = result.astype(BF)
    cot = cot_ref[...].astype(F32)
    unit, root = norm_parts(middle)
    back = back_ref[...]
    grad = cot + norm_back(unit, root, vec_ref[LN2_GAIN : LN2_GAIN + 1], back)
    grad_ref[...] = grad
    low = grad.astype(BF)
    branch[pl.ds(pl.multiple_of(step * TILE, TILE), TILE)] = low
    grad_att_ref[...] = nt(low, weight[...]).astype(BF)
    sums_ref[0:1] += col_sum(result * result)
    sums_ref[1:2] += col_sum(mlp * mlp)
    sums_ref[2:3] += col_sum(back * unit)
    sums_ref[3:4] += col_sum(back)
    sums_ref[4:5] += col_sum(low.astype(F32))
    sums_ref[5:6] += col_sum(cot)

    @pl.when(step == pl.num_programs(0) - 1)
    def _():
        out_grad[...] = tn(att_ref[...], branch[...])
        put_pieces(keep_ref, send_ref, out_grad, me_ref[0] % 2, 0)


def weight_back_kernel(
    me_ref, normed_ref, dq_ref, dk_ref, dv_ref, keep_ref, send_ref, sums_ref, grad
):
    step = pl.program_id(0)

    @pl.when(step == 0)
    def _():
        sums_ref[0:1] = col_sum(dq_ref[...].astype(F32))
        sums_ref[1:2] = col_sum(dv_ref[...].astype(F32))

    for part, ref in enumerate((dq_ref, dk_ref, dv_ref)):

        @pl.when(step == part)
        def _():
            grad[...] = tn(normed_ref[...], ref[...])

    put_pieces(keep_ref, send_ref, grad, me_ref[0] % 2, 0)


def input_kernel(table_ref, x_ref, dq_ref, dk_ref, dv_ref, grad_ref, vec_ref, *refs):
    sources, (out_ref, sums_ref, weight, sem) = refs[:SOURCES], refs[SOURCES:]

    @pl.when(pl.program_id(0) == 0)
    def _():
        fill(weight, table_ref, sources, sem, QKV_BLOCKS)
        sums_ref[...] = jnp.zeros_like(sums_ref)

    back = nt(dq_ref[...], weight[:, :D])
    back += nt(dk_ref[...], weight[:, D : 2 * D])
    back += nt(dv_ref[...], weight[:, 2 * D :])
    unit, root = norm_parts(x_ref[...].astype(F32))
    out_ref[...] = grad_ref[...] + norm_back(unit, root, vec_ref[LN1_GAIN : LN1_GAIN + 1], back)
    sums_ref[0:1] += col_sum(back * unit)
    sums_ref[1:2] += col_sum(back)


def lay_kernel(source_ref, *refs):
    out_ref, pieces = refs[-2:]
    begin = 0
    for ref in refs[:-2]:
        pieces[begin : begin + ref.shape[0]] = ref[...]
        begin += ref.shape[0]
    shards, own = out_ref.shape[:2]
    for shard in range(shards):
        for slot in range(own):
            out_ref[shard, slot] = pieces[source_ref[shard * own + slot]]


def factor_kernel(
    shard_ref,
    grad_ref,
    right_ref,
    matrix_ref,
    left_stat_ref,
    right_stat_ref,
    left_root_ref,
    rows_ref,
    left_ref,
    right_new_ref,
    matrix_new_ref,
    whole_grad,
    grad_t,
):
    rows = matrix_ref.shape[1]
    pieces, _, height, _ = grad_ref.shape
    for piece in range(pieces):
        whole_grad[piece * height : (piece + 1) * height, :] = grad_ref[piece, 0]
    grad = whole_grad[...]
    grad_t[...] = grad.T
    own = pl.ds(pl.multiple_of(shard_ref[0] * rows, rows), rows)
    grad_rows = whole_grad[own, :]
    rows_ref[0] = grad_rows.astype(F32)
    left_ref[0] = DECAY * left_stat_ref[0] + (1.0 - DECAY) * nn(grad_rows, grad_t[...])
    right_new_ref[0] = DECAY * right_stat_ref[0] + (1.0 - DECAY) * nn(grad_t[own, :], grad)
    half = nn(left_root_ref[0].astype(BF), grad)
    update = nn(half.astype(BF), right_ref[0])
    matrix_new_ref[0] = matrix_ref[0] - MATRIX_RATE * update


def core_sum_kernel(*refs):
    out_ref = refs[-1]
    begin = 0
    for keep, sent in zip(refs[:-1:2], refs[1:-1:2]):
        blocks = keep.shape[1]
        out_ref[0, begin : begin + blocks] = (keep[0].astype(F32) + sent[0].astype(F32)).astype(BF)
        begin += blocks


def across_dp(values, bit):
    count = lax.axis_size("dp")
    return lax.ppermute(values, "dp", [(i, i ^ (1 << bit)) for i in range(count)])


def across_fsdp(values, offset):
    count = lax.axis_size("fsdp")
    return lax.ppermute(values, "fsdp", [(i, i ^ offset) for i in range(count)])


def gather_by_permutes(values, me, shard):
    fsdp_count, dp_count = lax.axis_size("fsdp"), lax.axis_size("dp")
    held = jnp.stack([values] + [across_fsdp(values, k) for k in range(1, fsdp_count)])
    for bit in range(dp_count.bit_length() - 1):
        held = jnp.stack([held, across_dp(held, bit)])
    held = held.reshape((dp_count, fsdp_count) + values.shape)
    held = jnp.take(held, jnp.arange(dp_count) ^ me, axis=0)
    held = jnp.take(held, jnp.arange(fsdp_count) ^ shard, axis=1)
    return held.transpose(2, 0, 1, 3, 4).reshape((-1,) + values.shape[1:])


def core_sum(grads, name, ties=()):
    ins = []
    for keep, send in grads:
        ins += [keep, across_dp(send, 0)]
    pairs = ins[0].shape[0]
    rest = ins[0].shape[2:]
    blocks = sum(keep.shape[1] for keep, _ in grads)

    def one(array):
        return (array, (1,) + array.shape[1:], lambda i: (i, 0, 0, 0))

    return call(
        core_sum_kernel,
        (pairs,),
        [one(array) for array in ins],
        [((pairs, blocks) + rest, BF, (1, blocks) + rest, lambda i: (i, 0, 0, 0))],
        ties=ties,
        name=name,
    )[0]


def plane_parts(values):
    pairs = lax.axis_size("dp") // 2
    groups = [[2 * pair + core for pair in range(pairs)] for core in range(2)]
    return lax.all_to_all(values, "dp", 0, 0, axis_index_groups=groups, tiled=True)


def dp_sum(values):
    for bit in range(lax.axis_size("dp").bit_length() - 1):
        values = values + across_dp(values, bit)
    return values


def fsdp_sum(values):
    offset = 1
    while offset < lax.axis_size("fsdp"):
        values = values + across_fsdp(values, offset)
        offset *= 2
    return values


def per_device(
    tokens,
    cotangent,
    doc_lengths,
    block_slot,
    matrices,
    vectors,
    vector_second,
    left_stat,
    right_stat,
    left_root,
    right_root,
):
    dp_count = lax.axis_size("dp")
    fsdp_count = lax.axis_size("fsdp")
    own_blocks, own_rows, width = matrices.shape
    blocks = own_blocks * dp_count
    height = width // dp_count
    me = lax.axis_index("dp").astype(jnp.int32).reshape(1)
    shard = lax.axis_index("fsdp").astype(jnp.int32).reshape(1)
    half = lax.axis_index("fsdp")
    half = sum((half >> bit) & 1 for bit in range(fsdp_count.bit_length())) % 2
    half = half.astype(jnp.int32).reshape(1)
    numbers = jnp.arange(blocks, dtype=jnp.int32)
    holder = block_slot // own_blocks
    before = (holder[None, :] == holder[:, None]) & (numbers[None, :] < numbers[:, None])
    rank = jnp.sum(before.astype(jnp.int32), axis=1)
    early = max(2, 2 * own_blocks // 3 // 2 * 2)
    here = jnp.arange(own_blocks, dtype=jnp.int32)
    mine = (holder == me[0]) & (rank[None, :] == here[:, None])
    local = jnp.sum(jnp.where(mine, block_slot[None, :] % own_blocks, 0), axis=1)
    low = jnp.take(matrices, local, axis=0).astype(BF)
    late = lax.all_gather(low[early:], ("dp", "fsdp"), axis=1, tiled=True)
    late = late.reshape(-1, own_rows, width)
    right_whole = lax.all_gather(right_root.astype(BF), "fsdp", axis=1, tiled=True)

    line = jnp.stack([low[:early]] + [across_fsdp(low[:early], k) for k in range(1, fsdp_count)])
    plane_bits = list(range(1, dp_count.bit_length() - 1))
    sources, plane_places = [], []
    rel = holder ^ me[0]
    last_bits = []
    for part, order in enumerate((plane_bits, plane_bits[::-1])):
        held = line[:, part * early // 2 : (part + 1) * early // 2]
        for bit in order[:-1]:
            held = jnp.stack([held, across_dp(held, bit)])
        other = across_dp(held, order[-1])
        sources += [held, other, across_dp(held, 0), across_dp(other, 0)]
        plane_places.append(sum(((rel >> bit) & 1) << i for i, bit in enumerate(order[:-1])))
        last_bits.append((rel >> order[-1]) & 1)
    sources = [source.reshape(-1, own_rows, width) for source in sources]
    units = jnp.arange(fsdp_count, dtype=jnp.int32)[None, :]
    second_half = (rank >= early // 2).astype(jnp.int32)
    plane_place = jnp.where(second_half == 1, plane_places[1], plane_places[0])[:, None]
    inside = (rank - second_half * (early // 2))[:, None]
    early_index = (plane_place * fsdp_count + (units ^ shard[0])) * (early // 2) + inside
    late_index = ((rank[:, None] - early) * dp_count + holder[:, None]) * fsdp_count + units
    is_late = rank[:, None] >= early
    last_bit = jnp.where(second_half == 1, last_bits[1], last_bits[0])
    early_source = second_half * 4 + (rel & 1) * 2 + last_bit
    source_at = jnp.where(is_late, SOURCES - 1, early_source[:, None] + 0 * units)
    table = jnp.concatenate(
        [source_at.reshape(-1), jnp.where(is_late, late_index, early_index).reshape(-1)]
    ).astype(jnp.int32)
    qkv_early = jnp.max(rank[:12]) < early

    vec = vectors.reshape(-1, D)
    count = tokens.shape[0]
    rows_here, docs = doc_lengths.shape
    seq_len = count // rows_here
    steps = count // TILE

    def from_units(last):
        return [(source, None, None) for source in sources + [last]]

    def qkv(last):
        return tuple(
            call(
                qkv_kernel,
                (steps,),
                [tokens_in(tokens), whole(vec)] + from_units(last),
                [
                    ((count, D), BF, (TILE, D), lambda i, *_: (i, 0)),
                    ((count, 3 * D), BF, (TILE, 3 * D), lambda i, *_: (i, 0)),
                ],
                [pltpu.VMEM((D, 3 * D), BF), pltpu.SemaphoreType.DMA],
                scalars=[table],
                name="qkv",
            )
        )

    def qkv_with_late():
        return qkv(gather_by_permutes(low[early:], me[0], shard[0]))

    normed1, projected = lax.cond(qkv_early, lambda: qkv(sources[0]), qkv_with_late)
    weights_in = from_units(late)

    pairs = HEADS // 2
    bias_rows = spans(seq_len)[1]

    def pair_in(array, row, offset):
        return (array, (seq_len, PAIR), lambda p, *_: (row, offset + p))

    attended, lses = [], []
    for row in range(rows_here):
        one, lse = call(
            functools.partial(attend_kernel, row=row, docs=docs),
            (pairs,),
            [pair_in(projected, row, part * pairs) for part in range(3)],
            [
                ((seq_len, D), BF, (seq_len, PAIR), lambda p, *_: (0, p)),
                ((pairs, 2, seq_len), F32, (1, 2, seq_len), lambda p, *_: (p, 0, 0)),
            ],
            [pltpu.VMEM((bias_rows, TILE), F32), pltpu.VMEM((PAIR, seq_len), F32)],
            scalars=[doc_lengths],
            name="attend",
        )
        attended.append(one)
        lses.append(lse)
    attended = attended[0] if rows_here == 1 else jnp.concatenate(attended, axis=0)

    middle, normed2, sums_mid = call(
        out_kernel,
        (steps,),
        [tokens_in(attended), tokens_in(tokens), whole(vec)] + weights_in,
        [
            ((count, D), F32, (TILE, D), lambda i, *_: (i, 0)),
            ((count, D), BF, (TILE, D), lambda i, *_: (i, 0)),
            out_whole((8, D), F32),
        ],
        [pltpu.VMEM((D, D), BF), pltpu.SemaphoreType.DMA],
        scalars=[table],
        name="attn_out",
    )

    ff_cols = FF // width
    pair_count = dp_count // 2
    tiles = FF // D
    mlp, back2, grads, keep, send, fc_sums = call(
        mlp_kernel,
        (tiles,),
        [whole(normed2), whole(cotangent), whole(vec)] + weights_in,
        [
            out_whole((count, D), F32),
            out_whole((count, D), F32),
            (
                (dp_count, FIRST_TILES, 8, height, width),
                BF,
                (dp_count, 1, 8, height, width),
                lambda t, *_: (0, jnp.minimum(t, FIRST_TILES - 1), 0, 0, 0),
            ),
        ]
        + [
            (
                (pair_count, (tiles - FIRST_TILES) * 8, height, width),
                BF,
                (pair_count, 8, height, width),
                lambda t, *_: (0, jnp.maximum(t - FIRST_TILES, 0), 0, 0),
            )
        ]
        * 2
        + [((tiles, 1, D), F32, (1, 1, D), lambda t, *_: (t, 0, 0))],
        [pltpu.VMEM((tiles, D, D), BF)] * 2
        + [pltpu.VMEM((count, D), BF)] * 2
        + [pltpu.VMEM((2, D, D), F32), pltpu.SemaphoreType.DMA((2 * tiles,))],
        scalars=[table, me],
        name="mlp",
    )
    mlp_grads = (keep, send)
    first_grads = lax.psum_scatter(
        grads.reshape(-1, width), "dp", scatter_dimension=0, tiled=True
    )

    output, grad_middle, grad_attended, *out_grads, sums_back = call(
        middle_kernel,
        (steps,),
        [
            tokens_in(middle),
            tokens_in(mlp),
            tokens_in(back2),
            tokens_in(cotangent),
            whole(attended),
            whole(vec),
        ]
        + weights_in,
        [
            ((count, D), BF, (TILE, D), lambda i, *_: (i, 0)),
            ((count, D), F32, (TILE, D), lambda i, *_: (i, 0)),
            ((count, D), BF, (TILE, D), lambda i, *_: (i, 0)),
            out_whole((pair_count, 4, height, width), BF),
            out_whole((pair_count, 4, height, width), BF),
            out_whole((8, D), F32),
        ],
        [
            pltpu.VMEM((D, D), BF),
            pltpu.VMEM((count, D), BF),
            pltpu.VMEM((D, D), F32),
            pltpu.SemaphoreType.DMA,
        ],
        scalars=[table, me],
        ties=[right_whole],
        name="middle_back",
    )

    second_core = core_sum([mlp_grads, out_grads], "second_core")
    second_parts = plane_parts(second_core)
    def attend_back(row, begin, stop, onto, ties):
        return call(
            functools.partial(attend_back_kernel, row=row, docs=docs),
            (stop - begin,),
            [pair_in(projected, row, part * pairs + begin) for part in range(3)]
            + [
                pair_in(attended, row, begin),
                pair_in(grad_attended, row, begin),
                (lses[row], (1, 2, seq_len), lambda p, *_: (p + begin, 0, 0)),
            ],
            [((count, D), BF, (seq_len, PAIR), lambda p, *_: (row, p + begin))] * 3,
            [
                pltpu.VMEM((bias_rows, TILE), F32),
                pltpu.VMEM((seq_len, PAIR), F32),
                pltpu.VMEM((seq_len, PAIR), F32),
                pltpu.VMEM((PAIR, seq_len), F32),
            ],
            scalars=[doc_lengths],
            ties=ties,
            onto=onto,
            name="attend_back",
        )

    grads = ()
    for row in range(rows_here):
        grads = attend_back(row, 0, pairs // 2, grads, [second_core])
        grads = attend_back(row, pairs // 2, pairs, grads, [])
    dq, dk, dv = grads

    half_shape = (pair_count, 12, height, width)
    keep, send, sums_qkv = call(
        weight_back_kernel,
        (3,),
        [whole(array) for array in (normed1, dq, dk, dv)],
        [(half_shape, BF, (pair_count, 4, height, width), lambda p, *_: (0, p, 0, 0))] * 2
        + [out_whole((8, D), F32)],
        [pltpu.VMEM((D, D), F32)],
        scalars=[me],
        name="qkv_weight_back",
    )
    third_core = core_sum([(keep, send)], "third_core")
    second_halves = plane_sum(second_parts, half, [], "second_plane")
    third_parts = plane_parts(third_core)

    x_grad, sums_in = call(
        input_kernel,
        (steps,),
        [
            tokens_in(tokens),
            tokens_in(dq),
            tokens_in(dk),
            tokens_in(dv),
            tokens_in(grad_middle),
            whole(vec),
        ]
        + weights_in,
        [((count, D), F32, (TILE, D), lambda i, *_: (i, 0)), out_whole((8, D), F32)],
        [pltpu.VMEM((D, 3 * D), BF), pltpu.SemaphoreType.DMA],
        scalars=[table],
        ties=[second_halves[0], third_core],
        name="input_back",
    )

    second_half = line_half(second_halves, [x_grad], "second_half")
    first_halves = plane_sum(
        first_grads.reshape(1, -1, height, width), half, [second_half], "first_split"
    )
    first_half = line_half(first_halves, [], "first_half")
    first_total = line_rest(first_half, [], "first_rest")
    second_total = line_rest(second_half, [], "second_rest")
    vector_local = call(
        pack_kernel,
        (1,),
        [whole(array) for array in (sums_in, sums_qkv, sums_back, sums_mid, fc_sums)],
        [out_whole((16, D), F32)],
        name="pack",
    )[0]
    vector_plane = dp_sum(vector_local)
    vector_sums = fsdp_sum(vector_plane)
    third_halves = plane_sum(third_parts, half, [second_half, first_halves[0]], "third_plane")
    third_total = line_rest(line_half(third_halves, [], "third_half"), [], "third_rest")
    vector_grad = vector_sums[:12].reshape(-1)
    square_sums = vector_sums[12, :4]

    order = []
    for tile in range(FF // D):
        order += [16 + r * ff_cols + 2 * tile + c for r in range(2) for c in range(2)]
        order += [16 + 2 * ff_cols + 2 * (2 * tile + r) + c for r in range(2) for c in range(2)]
    order += list(range(12, 16))
    order += [r * 6 + 2 * part + c for part in range(3) for r in range(2) for c in range(2)]
    standing = jnp.array([order.index(u) for u in range(blocks)], jnp.int32)
    source = jnp.sum(
        jnp.where(block_slot[None, :] == numbers[:, None], standing[None, :], 0), axis=1
    )
    begin = 0
    spread = []
    for total in (first_total, second_total, third_total):
        size = total.shape[0]
        inside = source - begin
        moved = begin + (inside // size ^ half[0]) * size + inside % size
        source = jnp.where((inside >= 0) & (inside < size * 2), moved, source)
        begin += size * 2
        spread += line_spread(total)
    laid = call(
        lay_kernel,
        (1,),
        [whole(array) for array in spread],
        [out_whole((dp_count, own_blocks, height, width), BF)],
        [pltpu.VMEM((blocks, height, width), BF)],
        scalars=[source],
        ties=[vector_plane],
        name="lay",
    )[0]
    grad_whole = lax.all_to_all(laid, "dp", 0, 0, tiled=True)

    def block_in(array):
        return (array, (1,) + array.shape[1:], lambda b, *_: (b, 0, 0))

    matrix_grad, left_new, right_new, matrix_new = call(
        factor_kernel,
        (own_blocks,),
        [(grad_whole, (dp_count, 1, height, width), lambda b, *_: (0, b, 0, 0))]
        + [block_in(a) for a in (right_whole, matrices, left_stat, right_stat, left_root)],
        [(matrices.shape, F32, (1, own_rows, width), lambda b, *_: (b, 0, 0))] * 4,
        [pltpu.VMEM((width, width), BF)] * 2,
        scalars=[shard],
        name="factor",
    )

    residual_scale = jnp.sqrt(square_sums / (count * dp_count * fsdp_count * D))
    second_new = DECAY * vector_second + (1.0 - DECAY) * vector_grad * vector_grad
    vector_new = vectors - VECTOR_RATE * vector_grad / (jnp.sqrt(second_new) + ROOT_EPSILON)
    return (
        output,
        x_grad,
        matrix_grad,
        left_new,
        right_new,
        matrix_new,
        vector_grad,
        second_new,
        vector_new,
        residual_scale,
    )


def solution(mesh):
    tokens = P(("dp", "fsdp"), None)
    stored = P("dp", "fsdp", None)
    return jax.shard_map(
        per_device,
        mesh=mesh,
        in_specs=(tokens, tokens, tokens, P(), stored, P(), P()) + (stored,) * 4,
        out_specs=(tokens, tokens) + (stored,) * 4 + (P(),) * 4,
        check_vma=False,
    )
```
